512 devices in a mesh: seq: 128 (over z, y, core), mp: 4 (over x).
Axes of the slice: x: 4, y: 8, z: 8, core: 2. Of those that a mesh axis runs over, the one named last changes fastest.
Arguments:
- tokens: bfloat16 [65536, 768], P('seq'), may hold values from -6 to 6
- slide_tiles: int32 [4], replicated, may hold values from 1 to 49152, 65536 in all
- attn_gain: bfloat16 [768], replicated, may hold values from 0.099609375 to 1.8984375
- w_query: bfloat16 [768, 768], P(None, 'mp'), may hold values from -16 to 16
- w_key: bfloat16 [768, 768], P(None, 'mp'), may hold values from -0.21875 to 0.21875
- w_value: bfloat16 [768, 768], P(None, 'mp'), may hold values from -0.21875 to 0.21875
- w_out: bfloat16 [768, 768], P('mp'), may hold values from -0.21875 to 0.21875
- ffn_gain: bfloat16 [768], replicated, may hold values from 0.099609375 to 1.8984375
- w_up: bfloat16 [768, 3072], P(None, 'mp'), may hold values from -0.21875 to 0.21875
- w_down: bfloat16 [3072, 768], P('mp'), may hold values from -0.109375 to 0.109375
Outputs:
- attended: bfloat16 [65536, 768], P(('seq', 'mp'))
- far_attended: bfloat16 [2048, 768], P('seq', 'mp')
- ffn_out: bfloat16 [65536, 768], P(('seq', 'mp'))
The draws below stay inside these ranges and needn't reach their ends.
Inputs may be any that keep to these rules, and one draw needn't show every extreme that they name: `slide_tiles`: the tile counts of the slides sum to 65536; the longest slide has 49152 tiles.
All inputs are finite; a program needn't handle non-finite values.
Results may differ from the reference program's by a relative error of at most 0.023.
The reference program's roundings to bfloat16 on the way (of `normed`, `mixed`, `normed_ffn` and `hidden`) count: a program that leaves them out, or rounds other values in their place, can miss the bound.
Values may be sent and summed in bfloat16 or wider, within the bound.
No kernel may reach another device: no remote copies, remote signals or barrier semaphores. Data moves between devices by JAX's collectives and lax.ppermute only.
A program may use at most 64 MiB of HBM per device.

```python
import math
import jax
import jax.numpy as jnp
import numpy as np
from jax import lax

D = 768
HEADS = 12
FF = 3072
HEAD_DIM = 64
TOK_DEV = 512
SLIDES = 4
NEAR_DEVS = 4
MID_DEVS = 8
RATE_MID = 4
RATE_FAR = 32
TOKENS = 65536
N_MP = 4


def draw_w_query(key, part):
    key = jax.random.fold_in(key, 7)
    base_draw = jax.random.truncated_normal(key, -3.0, 3.0, (D, D), jnp.float32)
    factor = 3.0
    return (base_draw * (factor / math.sqrt(D))).astype(jnp.bfloat16)


def level_of(rng, shape, shards, low, high):
    gain, own = 1.0, jax.random.fold_in(rng, 6)
    for dim, parts in shards:
        heights = jnp.exp(jax.random.uniform(jax.random.fold_in(own, dim), (parts,), jnp.float32, low / len(shards), high / len(shards)))
        gain = gain * jnp.repeat(heights, shape[dim] // parts).reshape([-1 if axis == dim else 1 for axis in range(len(shape))])
    return gain


def length_profile(amount, total, most, lean):
    portions = [(1 << 20) // math.isqrt(rank ** lean) + 1 for rank in range(2, amount + 1)]
    surplus, given = total - most - (amount - 1), [1] * (amount - 1)
    while surplus > 0:
        free = [i for i in range(amount - 1) if given[i] < most]
        pool, left = sum([portions[i] for i in free]), surplus
        for i in free:
            more = min(most - given[i], max(1, left * portions[i] // pool), surplus)
            given[i] = given[i] + more
            surplus = surplus - more
    return np.array([most] + given)


def uneven(stream_key, amount, total, limit, skew):
    if amount == 2:
        one = jax.random.randint(stream_key, (), max(1, total - limit), min(limit, total - 1) + 1)
        return jnp.stack([one, total - one])
    sizes = jnp.asarray(length_profile(amount, total, limit, skew), jnp.int32)
    pairs = (amount - 1) // 2
    donor, taker = sizes[1:1 + 2 * pairs:2], sizes[2:2 + 2 * pairs:2]
    room = jnp.minimum(donor - 1, limit - taker)
    moved = jax.random.randint(jax.random.fold_in(stream_key, 1), (pairs,), 0, 1 << 20) % (room + 1)
    sizes = sizes.at[1:1 + 2 * pairs:2].set(donor - moved).at[2:2 + 2 * pairs:2].set(taker + moved)
    return sizes[jax.random.permutation(jax.random.fold_in(stream_key, 2), amount)]


def centred(own_key, shape, scale, limit, cuts=(), kind=jnp.bfloat16):
    entries = jax.random.normal(own_key, shape, jnp.float32) * scale
    if len(cuts) > 0:
        entries = level_of(own_key, shape, cuts, -0.22, 0.18) * entries
    return jnp.clip(entries, min=-limit, max=limit).astype(kind)


def setup_inputs(seed: int = 0) -> dict:
    key_list = jax.random.split(jax.random.key(seed), 11)
    tokens = centred(key_list[0], (TOKENS, D), 1.0, 6.0, ((0, 128),))
    slide_tiles = uneven(key_list[1], SLIDES, TOKENS, TOKENS * 3 // 4, 2).astype(jnp.int32)
    attn_gain = jnp.clip(1.0 + 0.18 * jax.random.normal(key_list[2], (D,), jnp.float32), 0.099609375, 1.8984375).astype(jnp.bfloat16)
    w_query = draw_w_query(jax.random.fold_in(key_list[10], 71), 0)
    w_key = centred(key_list[4], (D, D), D ** -0.5, 0.21875, ((1, 4),))
    w_value = centred(key_list[5], (D, D), D ** -0.5, 0.21875, ((1, 4),))
    w_out = centred(key_list[6], (D, D), D ** -0.5, 0.21875, ((0, 4),))
    ffn_gain = jnp.clip(1.0 + 0.18 * jax.random.normal(key_list[7], (D,), jnp.float32), 0.099609375, 1.8984375).astype(jnp.bfloat16)
    w_up = centred(key_list[8], (D, FF), D ** -0.5, 0.21875, ((1, 4),))
    w_down = centred(key_list[9], (FF, D), FF ** -0.5, 0.109375, ((0, 4),))
    return {"tokens": tokens, "slide_tiles": slide_tiles, "attn_gain": attn_gain, "w_query": w_query, "w_key": w_key, "w_value": w_value, "w_out": w_out, "ffn_gain": ffn_gain, "w_up": w_up, "w_down": w_down}


EPS = 1e-05

def layer_norm(values, norm_gain):
    as_float = values.astype(jnp.float32)
    mean_val = lax.optimization_barrier(jnp.mean(as_float, -1, keepdims=True))
    centered = as_float - mean_val
    variance = lax.optimization_barrier(jnp.mean(centered * centered, -1, keepdims=True))
    return (centered * lax.rsqrt(variance + EPS) * norm_gain.astype(jnp.float32)).astype(jnp.bfloat16)

def slide_of(positions, slide_tiles):
    slide_ends = jnp.cumsum(slide_tiles).astype(jnp.int32)
    return lax.optimization_barrier(jnp.sum((positions[..., None] >= slide_ends).astype(jnp.int32), -1)).astype(jnp.int32)

def attend(query, keyval, query_slide, key_slide):
    head_width = query.shape[-1]
    key_part = keyval[..., :head_width]
    value_part = keyval[..., head_width:]
    scores = jnp.einsum('qhd,khd->hqk', query.astype(jnp.float32), key_part.astype(jnp.float32), precision=lax.Precision.HIGHEST)
    scores = scores * (1.0 / math.sqrt(head_width))
    same_slide = query_slide.T[:, :, None] == key_slide.T[:, None, :]
    scores = jnp.where(same_slide, scores, -1e+30)
    peak_score = lax.optimization_barrier(jnp.max(scores, -1))
    weights = jnp.where(same_slide, jnp.exp(scores - peak_score[..., None]), 0.0)
    totals = lax.optimization_barrier(jnp.sum(weights, -1))
    rounded = lax.optimization_barrier(weights.astype(jnp.bfloat16)).astype(jnp.float32)
    partial_out = jnp.einsum('hqk,khd->qhd', rounded, value_part.astype(jnp.float32), precision=lax.Precision.HIGHEST)
    return (peak_score.T, totals.T, partial_out)

def pick(values, stride, offsets):
    shaped = values.reshape((values.shape[0] // stride, stride) + values.shape[1:])
    pick_index = offsets.astype(jnp.int32).reshape((1, 1, -1) + (1,) * (values.ndim - 2))
    pick_index = jnp.broadcast_to(pick_index, (shaped.shape[0], 1) + values.shape[1:])
    return jnp.take_along_axis(shaped, pick_index, axis=1)[:, 0]

def spread(values, stride, offsets, filler):
    head_count = offsets.shape[0]
    present = jnp.arange(stride, dtype=jnp.int32)[:, None] == offsets[None, :]
    present = present.reshape((1, stride, head_count) + (1,) * (values.ndim - 2))
    widened = jnp.where(present, values[:, None], filler)
    return widened.reshape((values.shape[0] * stride,) + values.shape[1:])

def branch_raw(query, keyval, slides, stride, segment_rows, offsets):
    picked_query = pick(query, stride, offsets)
    picked_kv = pick(keyval, stride, offsets)
    picked_slide = pick(slides, stride, offsets)
    segment_count = picked_query.shape[0] // segment_rows

    def one_segment(pieces):
        return attend(pieces[0], pieces[1], pieces[2], pieces[2])
    peak_score, totals, partial_out = lax.map(one_segment, (picked_query.reshape((segment_count, segment_rows) + picked_query.shape[1:]), picked_kv.reshape((segment_count, segment_rows) + picked_kv.shape[1:]), picked_slide.reshape((segment_count, segment_rows) + picked_slide.shape[1:])))
    count_rows = picked_query.shape[0]
    peak_score = peak_score.reshape((count_rows,) + peak_score.shape[2:])
    totals = totals.reshape((count_rows,) + totals.shape[2:])
    partial_out = partial_out.reshape((count_rows,) + partial_out.shape[2:])
    return (peak_score, totals, partial_out)

def spread_all(results, stride, offsets):
    return (spread(results[0], stride, offsets, -1e+30), spread(results[1], stride, offsets, 0.0), spread(results[2], stride, offsets, 0.0))

def combine(results):
    largest = results[0][0]
    for item in results[1:]:
        largest = jnp.maximum(largest, item[0])
    numerator = jnp.zeros_like(results[0][2])
    denominator = jnp.zeros_like(results[0][1])
    for item in results:
        factor = jnp.exp(item[0] - largest)
        numerator = numerator + factor[..., None] * item[2]
        denominator = denominator + factor * item[1]
    return (numerator / denominator[..., None]).astype(jnp.bfloat16)

def group_sum(left, right, group_count):
    width = left.shape[1] // group_count
    summed = jnp.zeros((left.shape[0], right.shape[1]), jnp.float32)
    for group in range(group_count):
        term = jnp.dot(left[:, group * width:(group + 1) * width], right[group * width:(group + 1) * width], preferred_element_type=jnp.float32)
        summed = summed + lax.optimization_barrier(term.astype(jnp.bfloat16)).astype(jnp.float32)
    return summed.astype(jnp.bfloat16)

def reference(tokens, slide_tiles, attn_gain, w_query, w_key, w_value, w_out, ffn_gain, w_up, w_down):
    normed = layer_norm(tokens, attn_gain)

    def project(weight):
        return jnp.dot(normed, weight, preferred_element_type=jnp.float32).astype(jnp.bfloat16).reshape(TOKENS, HEADS, HEAD_DIM)
    query = project(w_query)
    keyval = jnp.concatenate([project(w_key), project(w_value)], -1)
    positions = jnp.arange(TOKENS, dtype=jnp.int32)
    slides = jnp.broadcast_to(slide_of(positions, slide_tiles)[:, None], (TOKENS, HEADS))
    head_ids = jnp.arange(HEADS, dtype=jnp.int32)
    near = spread_all(branch_raw(query, keyval, slides, 1, NEAR_DEVS * TOK_DEV, head_ids % 1), 1, head_ids % 1)
    middle = spread_all(branch_raw(query, keyval, slides, RATE_MID, MID_DEVS * TOK_DEV // RATE_MID, head_ids % RATE_MID), RATE_MID, head_ids % RATE_MID)
    far_raw = branch_raw(query, keyval, slides, RATE_FAR, TOKENS // RATE_FAR, head_ids % RATE_FAR)
    far_attended = (far_raw[2] / far_raw[1][..., None]).astype(jnp.bfloat16).reshape(TOKENS // RATE_FAR, D)
    distant = spread_all(far_raw, RATE_FAR, head_ids % RATE_FAR)
    mixed = combine([near, middle, distant]).reshape(TOKENS, D)
    attended = group_sum(mixed, w_out, N_MP)
    normed_ffn = layer_norm(tokens.astype(jnp.float32) + attended.astype(jnp.float32), ffn_gain)
    hidden = jax.nn.gelu(jnp.dot(normed_ffn, w_up, preferred_element_type=jnp.float32), approximate=False).astype(jnp.bfloat16)
    ffn_out = group_sum(hidden, w_down, N_MP)
    return (attended, far_attended, ffn_out)
```

```python
import functools

import jax
import jax.numpy as jnp
from jax import lax
from jax.experimental import pallas as pl
from jax.experimental.pallas import tpu as pltpu
from jax.sharding import PartitionSpec as P

HEAD_DIM = 64
LOCAL_HEADS = 3
RATE_MID = 4
RATE_FAR = 32
ROWS = 512
CLASS_ROWS = ROWS // RATE_MID
FAR_ROWS = ROWS // RATE_FAR
LANES = 128
SLIDES = 4
EPS = 1e-05
HIDDEN_SCORE = -1e30
VMEM = 56 * 1024 * 1024

KEY_TILE = (0, 0, 2)
VALUE_TILE = (1, 1, 2)
QUERY_TILE = (0, 0, 1)


def iota(shape, dim):
    return lax.broadcasted_iota(jnp.int32, shape, dim)


def place_of(row):
    return (row & 3) * CLASS_ROWS + ((row >> 2) & 7) * FAR_ROWS + (row >> 5)


def row_at(place):
    return (place & 15) * RATE_FAR + ((place >> 4) & 7) * RATE_MID + (place >> 7)


def layer_norm(as_float, gain):
    mean_val = jnp.mean(as_float, -1, keepdims=True)
    centered = as_float - mean_val
    variance = jnp.mean(centered * centered, -1, keepdims=True)
    return (centered * lax.rsqrt(variance + EPS) * gain.astype(jnp.float32)).astype(jnp.bfloat16)


def matmul(left, right):
    return jnp.dot(left, right, preferred_element_type=jnp.float32)


def slide_of(positions, ends):
    index = (positions >= ends[0]).astype(jnp.int32)
    for end in ends[1:]:
        index = index + (positions >= end).astype(jnp.int32)
    return index


def slide_ends(tiles_ref):
    ends = [tiles_ref[0]]
    for slide in range(1, SLIDES - 1):
        ends.append(ends[-1] + tiles_ref[slide])
    return ends


def query_marks(positions, ends):
    rows = positions.shape[0]
    lane = iota((rows, LANES), 1)
    return (lane == slide_of(positions, ends)).astype(jnp.bfloat16)


def key_marks(positions, ends):
    rows = positions.shape[0]
    lane = iota((rows, LANES), 1)
    hide = (lane < SLIDES) & (lane != slide_of(positions, ends))
    marks = jnp.where(hide, HIDDEN_SCORE, jnp.where(lane == SLIDES, 1.0, 0.0))
    return marks.astype(jnp.bfloat16)


def head_lanes(value, head):
    lane = iota(value.shape, 1)
    keep = lane < HEAD_DIM if head != 1 else lane >= HEAD_DIM
    return jnp.where(keep, value, jnp.zeros_like(value))


def tile(index):
    return slice(index * LANES, (index + 1) * LANES)


def project_kernel(tokens, gain, w_query, w_key, w_value, place, query, keyval, mid, far):
    normed = layer_norm(tokens[...].astype(jnp.float32), gain[...])
    order = iota((ROWS, ROWS), 0) == place_of(iota((ROWS, ROWS), 1))
    normed = matmul(order.astype(jnp.bfloat16), normed).astype(jnp.bfloat16)
    scaled = (matmul(normed, w_query[...]) * (1.0 / 8.0)).astype(jnp.bfloat16)
    query[:, :192] = scaled
    query[:, 192:] = jnp.zeros((ROWS, 64), jnp.bfloat16)
    key = matmul(normed, w_key[...]).astype(jnp.bfloat16)
    value = matmul(normed, w_value[...]).astype(jnp.bfloat16)
    keyval[:, tile(0)] = key[:, :128]
    keyval[:, tile(1)] = value[:, :128]
    keyval[:, tile(2)] = jnp.concatenate([key[:, 128:], value[:, 128:]], 1)
    for source, rows, target in (("mid", CLASS_ROWS, mid), ("far", FAR_ROWS, far)):
        picked = []
        for head in range(LOCAL_HEADS):
            number = place[1] * LOCAL_HEADS + head
            start = (number & 3) * CLASS_ROWS
            if source == "far":
                start = start + (number >> 2) * FAR_ROWS
            picked.append(pl.ds(pl.multiple_of(start, rows), rows))
        for index in range(2):
            low, high = keyval[picked[0], tile(index)], keyval[picked[1], tile(index)]
            lane = iota(low.shape, 1)
            target[:, tile(index)] = jnp.where(lane < HEAD_DIM, low, high)
        target[:, tile(2)] = keyval[picked[2], tile(2)]


def scores_of(query, keys):
    return lax.dot_general(
        query, keys, (((1,), (1,)), ((), ())), preferred_element_type=jnp.float32
    )


def attend(query, keys, values):
    scores = scores_of(query, keys)
    peak = jnp.max(scores, -1, keepdims=True)
    weights = jnp.exp(scores - peak).astype(jnp.bfloat16)
    return peak, matmul(weights, values)


def near_kernel(tiles, place, query, own, other, peaks, sums):
    ends = slide_ends(tiles)
    base = place[0] * ROWS
    rows = row_at(iota((ROWS, LANES), 0))
    marks = query_marks(rows + base, ends)
    keys_marks = jnp.concatenate(
        [key_marks(rows + base, ends), key_marks(rows + (place[0] ^ 1) * ROWS, ends)], 0
    )
    for head in range(LOCAL_HEADS):
        asked = head_lanes(query[:, tile(QUERY_TILE[head])], head)
        asked = jnp.concatenate([asked, marks], 1)
        keys = jnp.concatenate(
            [own[:, tile(KEY_TILE[head])], other[:, tile(KEY_TILE[head])]], 0
        )
        values = jnp.concatenate(
            [own[:, tile(VALUE_TILE[head])], other[:, tile(VALUE_TILE[head])]], 0
        )
        peak, total = attend(
            asked,
            jnp.concatenate([keys, keys_marks], 1),
            jnp.concatenate([values, keys_marks], 1),
        )
        peaks[head] = jnp.broadcast_to(peak, (ROWS, LANES))
        sums[head] = total


def join(peaks, sums, head, rows, peak, total):
    held = peaks[head, rows, :][:, :1]
    largest = jnp.maximum(held, peak)
    sums[head, rows, :] = sums[head, rows, :] * jnp.exp(held - largest) + total * jnp.exp(
        peak - largest
    )
    peaks[head, rows, :] = jnp.broadcast_to(largest, (largest.shape[0], LANES))


def rest_kernel(
    tiles, place, query, own, core, side, corner, mid, far, peaks_in, sums_in,
    mixed, far_out, peaks, sums,
):
    ends = slide_ends(tiles)
    seq, mp = place[0], place[1]
    rows = row_at(iota((ROWS, LANES), 0))
    marks = query_marks(rows + seq * ROWS, ends)
    far_parts = []
    near = (own, core, side, corner)
    near_marks = [key_marks(rows + (seq ^ step) * ROWS, ends) for step in range(4)]
    side_marks = jnp.concatenate(near_marks[2:], 0)
    peaks[...] = peaks_in[...]
    sums[...] = sums_in[...]
    for head in range(LOCAL_HEADS):
        key_tile, value_tile = tile(KEY_TILE[head]), tile(VALUE_TILE[head])
        asked = head_lanes(query[:, tile(QUERY_TILE[head])], head)
        keys = jnp.concatenate([side[:, key_tile], corner[:, key_tile]], 0)
        values = jnp.concatenate([side[:, value_tile], corner[:, value_tile]], 0)
        peak, total = attend(
            jnp.concatenate([asked, marks], 1),
            jnp.concatenate([keys, side_marks], 1),
            jnp.concatenate([values, side_marks], 1),
        )
        join(peaks, sums, head, slice(None), peak, total)

        number = mp * LOCAL_HEADS + head
        offset = number & 3
        picked = pl.ds(pl.multiple_of(offset * CLASS_ROWS, CLASS_ROWS), CLASS_ROWS)
        class_rows = offset + RATE_MID * (
            (iota((CLASS_ROWS, LANES), 0) >> 4) + ((iota((CLASS_ROWS, LANES), 0) & 15) << 3)
        )
        class_marks = jnp.concatenate(
            [key_marks(class_rows + (seq ^ step) * ROWS, ends) for step in range(8)], 0
        )
        asked = head_lanes(query[picked, tile(QUERY_TILE[head])], head)
        asked = jnp.concatenate([asked, query_marks(class_rows + seq * ROWS, ends)], 1)
        keys = jnp.concatenate([ref[picked, key_tile] for ref in near] + [mid[:, key_tile]], 0)
        values = jnp.concatenate(
            [ref[picked, value_tile] for ref in near] + [mid[:, value_tile]], 0
        )
        peak, total = attend(
            asked,
            jnp.concatenate([keys, class_marks], 1),
            jnp.concatenate([values, class_marks], 1),
        )
        join(peaks, sums, head, picked, peak, total)

        start = pl.multiple_of(
            offset * CLASS_ROWS + (number >> 2) * FAR_ROWS, FAR_ROWS
        )
        picked = pl.ds(start, FAR_ROWS)
        asked = head_lanes(query[picked, tile(QUERY_TILE[head])], head)
        scores = scores_of(asked, far[:, key_tile])
        own_slide = slide_of(
            seq * ROWS + number + RATE_FAR * iota(scores.shape, 0), ends
        )
        same = slide_of(number + RATE_FAR * iota(scores.shape, 1), ends) == own_slide
        scores = jnp.where(same, scores, HIDDEN_SCORE)
        peak = jnp.max(scores, -1, keepdims=True)
        weights = jnp.exp(scores - peak)
        total = jnp.sum(weights, -1, keepdims=True)
        part = matmul(weights.astype(jnp.bfloat16), far[:, value_tile])
        far_parts.append(part / total)
        lane = iota((FAR_ROWS, LANES), 1)
        stats = jnp.where(lane == SLIDES, total, 0.0)
        join(peaks, sums, head, picked, peak, jnp.concatenate([part, stats], 1))

    def packed(parts, out):
        lane = iota(parts[0].shape, 1)
        out[:, :128] = jnp.where(lane < HEAD_DIM, parts[0], parts[1]).astype(jnp.bfloat16)
        out[:, 128:] = parts[2][:, HEAD_DIM:].astype(jnp.bfloat16)

    packed(far_parts, far_out)
    back = (place_of(iota((ROWS, ROWS), 0)) == iota((ROWS, ROWS), 1)).astype(jnp.bfloat16)
    parts = []
    for head in range(LOCAL_HEADS):
        part = sums[head, :, :LANES] / sums[head, :, LANES + SLIDES : LANES + SLIDES + 1]
        parts.append(matmul(back, part.astype(jnp.bfloat16)))
    packed(parts, mixed)


def ffn_kernel(tokens, mixed, w_out, gain, w_up, w_down, place, attended, partial):
    summed = matmul(mixed[0], w_out[:192, :])
    for group in range(1, 4):
        summed = summed + matmul(mixed[group], w_out[192 * group : 192 * (group + 1), :])
    summed = summed.astype(jnp.bfloat16)
    partial[...] = summed
    attended[...] = partial[pl.ds(pl.multiple_of(place[1] * 128, 128), 128), :]
    normed = layer_norm(tokens[...].astype(jnp.float32) + summed.astype(jnp.float32), gain[...])
    raised = matmul(normed, w_up[...])
    hidden = (0.5 * raised * (1.0 + lax.erf(raised * 0.7071067811865476))).astype(jnp.bfloat16)
    partial[...] = matmul(hidden, w_down[...]).astype(jnp.bfloat16)


def call(kernel, outs, ins, scratch=()):
    places = {"smem": pltpu.SMEM, "vmem": pltpu.VMEM}
    return pl.pallas_call(
        kernel,
        out_shape=[jax.ShapeDtypeStruct(*out) for out in outs],
        in_specs=[pl.BlockSpec(memory_space=places[where]) for _, where in ins],
        out_specs=[pl.BlockSpec(memory_space=pltpu.VMEM) for _ in outs],
        scratch_shapes=list(scratch),
        compiler_params=pltpu.CompilerParams(vmem_limit_bytes=VMEM),
    )(*[array for array, _ in ins])


def swap(value, step):
    return lax.ppermute(value, "seq", [(i, i ^ step) for i in range(lax.axis_size("seq"))])


def local(tokens, slide_tiles, attn_gain, w_query, w_key, w_value, w_out, ffn_gain, w_up, w_down):
    bf16 = jnp.bfloat16
    place = jnp.stack([lax.axis_index("seq"), lax.axis_index("mp")]).astype(jnp.int32)
    attn_gain, ffn_gain = attn_gain.reshape(1, -1), ffn_gain.reshape(1, -1)
    v, s = "vmem", "smem"
    query, own, mid, far = call(
        project_kernel,
        [((ROWS, 256), bf16), ((ROWS, 384), bf16), ((CLASS_ROWS, 384), bf16), ((FAR_ROWS, 384), bf16)],
        [(tokens, v), (attn_gain, v), (w_query, v), (w_key, v), (w_value, v), (place, s)],
    )
    side = swap(own, 2)
    core = swap(own, 1)
    corner = swap(side, 1)
    mids = [swap(mid, step) for step in (4, 5, 6, 7)]
    far_all = lax.all_gather(far, "seq", axis=0, tiled=True)
    w_out_all = lax.all_gather(w_out, "mp", axis=0, tiled=True)
    state = [((LOCAL_HEADS, ROWS, LANES), jnp.float32), ((LOCAL_HEADS, ROWS, 256), jnp.float32)]
    peaks, sums = call(
        near_kernel,
        state,
        [(slide_tiles, s), (place, s), (query, v), (own, v), (core, v)],
    )
    mixed, far_attended = call(
        rest_kernel,
        [((ROWS, 192), bf16), ((FAR_ROWS, 192), bf16)],
        [
            (slide_tiles, s), (place, s), (query, v), (own, v), (core, v), (side, v), (corner, v),
            (jnp.concatenate(mids, 0), v), (far_all, v), (peaks, v), (sums, v),
        ],
        [pltpu.VMEM(*shape) for shape in state],
    )
    mixed_all = lax.all_gather(mixed, "mp", axis=0)
    attended, partial = call(
        ffn_kernel,
        [((ROWS // 4, 768), bf16), ((ROWS, 768), bf16)],
        [(tokens, v), (mixed_all, v), (w_out_all, v), (ffn_gain, v), (w_up, v), (w_down, v), (place, s)],
    )
    ffn_out = lax.psum_scatter(partial, "mp", scatter_dimension=0, tiled=True)
    return (attended, far_attended, ffn_out)


def solution(mesh):
    return jax.shard_map(
        local,
        mesh=mesh,
        in_specs=(
            P("seq", None),
            P(),
            P(),
            P(None, "mp"),
            P(None, "mp"),
            P(None, "mp"),
            P("mp", None),
            P(),
            P(None, "mp"),
            P("mp", None),
        ),
        out_specs=(P(("seq", "mp"), None), P("seq", "mp"), P(("seq", "mp"), None)),
        check_vma=False,
    )
```

```python
import functools

import jax
import jax.numpy as jnp
from jax import lax
from jax.experimental import pallas as pl
from jax.experimental.pallas import tpu as pltpu
from jax.sharding import PartitionSpec as P

HEAD_DIM = 64
LOCAL_HEADS = 3
RATE_MID = 4
RATE_FAR = 32
ROWS = 512
CLASS_ROWS = ROWS // RATE_MID
FAR_ROWS = ROWS // RATE_FAR
LANES = 128
SLIDES = 4
EPS = 1e-05
HIDDEN_SCORE = -1e30
VMEM = 56 * 1024 * 1024

KEY_TILE = (0, 0, 2)
VALUE_TILE = (1, 1, 2)
QUERY_TILE = (0, 0, 1)
SPARE = (64, 0, 0)
FAR_GROUP = 8


def iota(shape, dim):
    return lax.broadcasted_iota(jnp.int32, shape, dim)


def place_of(row):
    return (row & 3) * CLASS_ROWS + ((row >> 2) & 7) * FAR_ROWS + (row >> 5)


def row_at(place):
    return (place & 15) * RATE_FAR + ((place >> 4) & 7) * RATE_MID + (place >> 7)


def layer_norm(as_float, gain):
    mean_val = jnp.mean(as_float, -1, keepdims=True)
    centered = as_float - mean_val
    variance = jnp.mean(centered * centered, -1, keepdims=True)
    return (centered * lax.rsqrt(variance + EPS) * gain.astype(jnp.float32)).astype(jnp.bfloat16)


def matmul(left, right):
    return jnp.dot(left, right, preferred_element_type=jnp.float32)


def matmul_t(left, right):
    return lax.dot_general(
        left, right, (((1,), (1,)), ((), ())), preferred_element_type=jnp.float32
    )


def slide_of(positions, ends):
    index = (positions >= ends[0]).astype(jnp.int32)
    for end in ends[1:]:
        index = index + (positions >= end).astype(jnp.int32)
    return index


def slide_ends(tiles_ref):
    ends = [tiles_ref[0]]
    for slide in range(1, SLIDES - 1):
        ends.append(ends[-1] + tiles_ref[slide])
    return ends


def query_marks(positions, ends):
    rows = positions.shape[0]
    lane = iota((rows, LANES), 1)
    return (lane == slide_of(positions, ends)).astype(jnp.bfloat16)


def key_marks(positions, ends):
    rows = positions.shape[0]
    lane = iota((rows, LANES), 1)
    hide = (lane < SLIDES) & (lane != slide_of(positions, ends))
    marks = jnp.where(hide, HIDDEN_SCORE, jnp.where(lane == SLIDES, 1.0, 0.0))
    return marks.astype(jnp.bfloat16)


def head_lanes(value, head):
    lane = iota(value.shape, 1)
    keep = lane < HEAD_DIM if head != 1 else lane >= HEAD_DIM
    return jnp.where(keep, value, jnp.zeros_like(value))


def tile(index):
    return slice(index * LANES, (index + 1) * LANES)


def project_kernel(tokens, gain, w_query, w_key, w_value, query, keyval, mid, far):
    mp = lax.axis_index("mp")
    normed = layer_norm(tokens[...].astype(jnp.float32), gain[...])
    order = iota((ROWS, ROWS), 0) == place_of(iota((ROWS, ROWS), 1))
    normed = matmul(order.astype(jnp.bfloat16), normed).astype(jnp.bfloat16)
    scaled = (matmul_t(normed, w_query[...]) * (1.0 / 8.0)).astype(jnp.bfloat16)
    query[:, :192] = scaled
    query[:, 192:] = jnp.zeros((ROWS, 64), jnp.bfloat16)
    key = matmul_t(normed, w_key[...]).astype(jnp.bfloat16)
    value = matmul_t(normed, w_value[...]).astype(jnp.bfloat16)
    keyval[:, tile(0)] = key[:, :128]
    keyval[:, tile(1)] = value[:, :128]
    keyval[:, tile(2)] = jnp.concatenate([key[:, 128:], value[:, 128:]], 1)

    def pick(source, index, rows):
        starts = []
        for head in range(LOCAL_HEADS):
            number = mp * LOCAL_HEADS + head
            start = (number & 3) * CLASS_ROWS
            if rows == FAR_ROWS:
                start = start + (number >> 2) * FAR_ROWS
            starts.append(pl.ds(pl.multiple_of(start, rows), rows))
        if index == KEY_TILE[2] and source is keyval or index == QUERY_TILE[2] and source is query:
            return source[starts[2], tile(index)]
        low, high = source[starts[0], tile(index)], source[starts[1], tile(index)]
        return jnp.where(iota(low.shape, 1) < HEAD_DIM, low, high)

    for index in range(3):
        mid[:, tile(index)] = pick(keyval, index, CLASS_ROWS)
    picked = [pick(query, index, FAR_ROWS) for index in range(2)]
    picked += [pick(keyval, index, FAR_ROWS) for index in range(3)]
    for index in range(5):
        for copy in range(FAR_GROUP):
            far[copy, :, tile(index)] = picked[index]


def attend(query, keys, values):
    scores = matmul_t(query, keys)
    peak = jnp.max(scores, -1, keepdims=True)
    weights = jnp.exp(scores - peak).astype(jnp.bfloat16)
    return peak, matmul(weights, values)


def marks_near(seq, ends, steps):
    rows = row_at(iota((ROWS, LANES), 0))
    return jnp.concatenate([key_marks(rows + (seq ^ step) * ROWS, ends) for step in steps], 0)


def near_kernel(tiles, query, own, side, peaks, sums):
    ends = slide_ends(tiles)
    seq = lax.axis_index("seq")
    marks = query_marks(row_at(iota((ROWS, LANES), 0)) + seq * ROWS, ends)
    keys_marks = marks_near(seq, ends, (0, 2))
    for head in range(LOCAL_HEADS):
        key_tile, value_tile = tile(KEY_TILE[head]), tile(VALUE_TILE[head])
        asked = head_lanes(query[:, tile(QUERY_TILE[head])], head)
        keys = jnp.concatenate([own[:, key_tile], side[:, key_tile]], 0)
        values = jnp.concatenate([own[:, value_tile], side[:, value_tile]], 0)
        peak, total = attend(
            jnp.concatenate([asked, marks], 1),
            jnp.concatenate([keys, keys_marks], 1),
            jnp.concatenate([values, keys_marks], 1),
        )
        peaks[head] = jnp.broadcast_to(peak, (ROWS, LANES))
        sums[head] = total


def join(peaks, sums, head, rows, peak, total):
    held = peaks[head, rows, :][:, :1]
    largest = jnp.maximum(held, peak)
    sums[head, rows, :] = sums[head, rows, :] * jnp.exp(held - largest) + total * jnp.exp(
        peak - largest
    )
    peaks[head, rows, :] = jnp.broadcast_to(largest, (largest.shape[0], LANES))


def rest_kernel(tiles, query, own, side, mid_a, mid_b, swapped, peaks_in, sums_in, peaks, sums):
    ends = slide_ends(tiles)
    seq, mp = lax.axis_index("seq"), lax.axis_index("mp")
    marks = query_marks(row_at(iota((ROWS, LANES), 0)) + seq * ROWS, ends)
    near_marks = marks_near(seq, ends, (1, 3))
    peaks[...] = peaks_in[...]
    sums[...] = sums_in[...]
    for head in range(LOCAL_HEADS):
        key_tile, value_tile = tile(KEY_TILE[head]), tile(VALUE_TILE[head])
        asked = head_lanes(query[:, tile(QUERY_TILE[head])], head)
        peak, total = attend(
            jnp.concatenate([asked, marks], 1),
            jnp.concatenate([swapped[: 2 * ROWS, key_tile], near_marks], 1),
            jnp.concatenate([swapped[: 2 * ROWS, value_tile], near_marks], 1),
        )
        join(peaks, sums, head, slice(None), peak, total)

        offset = (mp * LOCAL_HEADS + head) & 3
        start = pl.multiple_of(offset * CLASS_ROWS, CLASS_ROWS)
        picked = pl.ds(start, CLASS_ROWS)
        place = iota((CLASS_ROWS, LANES), 0)
        class_rows = offset + RATE_MID * ((place >> 4) + ((place & 15) << 3))
        class_marks = jnp.concatenate(
            [key_marks(class_rows + (seq ^ step) * ROWS, ends) for step in (0, 2, 1, 3, 4, 6, 5, 7)],
            0,
        )
        asked = head_lanes(query[picked, tile(QUERY_TILE[head])], head)
        asked = jnp.concatenate([asked, query_marks(class_rows + seq * ROWS, ends)], 1)

        def gathered(lanes):
            return jnp.concatenate(
                [
                    own[picked, lanes],
                    side[picked, lanes],
                    swapped[picked, lanes],
                    swapped[pl.ds(start + ROWS, CLASS_ROWS), lanes],
                    mid_a[:, lanes],
                    mid_b[:, lanes],
                    swapped[2 * ROWS :, lanes],
                ],
                0,
            )

        peak, total = attend(
            asked,
            jnp.concatenate([gathered(key_tile), class_marks], 1),
            jnp.concatenate([gathered(value_tile), class_marks], 1),
        )
        join(peaks, sums, head, picked, peak, total)


def far_kernel(tiles, rows, here, other, parts):
    ends = slide_ends(tiles)
    seq, mp = lax.axis_index("seq"), lax.axis_index("mp")
    column = seq & 15
    beside = column ^ ((seq >> 4) << 1)
    count = FAR_GROUP * FAR_ROWS
    shape = (count, 2 * count)

    def position(place, holder):
        return ((place >> 4) * 16 + holder) * ROWS + (place & 15) * RATE_FAR

    at = iota(shape, 1)
    holder = jnp.where(at < count, beside, beside ^ 1)
    key_at = position(at & (count - 1), holder)
    query_at = position(iota(shape, 0), column)
    lane = iota((count, LANES), 1)
    for head in range(LOCAL_HEADS):
        number = mp * LOCAL_HEADS + head
        key_tile, value_tile = tile(KEY_TILE[head]), tile(VALUE_TILE[head])
        asked = rows[:, :, tile(QUERY_TILE[head])].reshape(count, LANES)
        asked = head_lanes(asked, head)
        scores = matmul_t(asked, jnp.concatenate([here[:, key_tile], other[:, key_tile]], 0))
        same = slide_of(query_at + number, ends) == slide_of(key_at + number, ends)
        scores = jnp.where(same, scores, HIDDEN_SCORE)
        peak = jnp.max(scores, -1, keepdims=True)
        weights = jnp.exp(scores - peak)
        total = jnp.sum(weights, -1, keepdims=True)
        values = jnp.concatenate([here[:, value_tile], other[:, value_tile]], 0)
        part = matmul(weights.astype(jnp.bfloat16), values)
        spare = SPARE[head]
        part = jnp.where(lane == spare, peak, jnp.where(lane == spare + 1, total, part))
        parts[:, :, tile(head)] = part.reshape(FAR_GROUP, FAR_ROWS, LANES)


def finish_kernel(parts, peaks_in, sums_in, mixed, far_out, peaks, sums):
    mp = lax.axis_index("mp")
    peaks[...] = peaks_in[...]
    sums[...] = sums_in[...]
    lane = iota((FAR_ROWS, LANES), 1)
    far_parts = []
    for head in range(LOCAL_HEADS):
        spare = SPARE[head]
        pieces = [parts[index, :, tile(head)] for index in range(FAR_GROUP)]
        tops = [piece[:, spare : spare + 1] for piece in pieces]
        peak = functools.reduce(jnp.maximum, tops)
        total = jnp.zeros((FAR_ROWS, LANES), jnp.float32)
        for piece, top in zip(pieces, tops):
            total = total + piece * jnp.exp(top - peak)
        weight = total[:, spare + 1 : spare + 2]
        far_parts.append(total / weight)
        number = mp * LOCAL_HEADS + head
        start = (number & 3) * CLASS_ROWS + (number >> 2) * FAR_ROWS
        picked = pl.ds(pl.multiple_of(start, FAR_ROWS), FAR_ROWS)
        stats = jnp.where(lane == SLIDES, weight, 0.0)
        join(peaks, sums, head, picked, peak, jnp.concatenate([total, stats], 1))

    def packed(values):
        first = jnp.where(iota(values[0].shape, 1) < HEAD_DIM, values[0], values[1])
        return first.astype(jnp.bfloat16), values[2].astype(jnp.bfloat16)

    first, last = packed(far_parts)
    far_out[:, :128] = first
    far_out[:, 128:] = last[:, HEAD_DIM:]
    back = (place_of(iota((ROWS, ROWS), 0)) == iota((ROWS, ROWS), 1)).astype(jnp.bfloat16)
    first, last = packed(
        [
            sums[head, :, :LANES] / sums[head, :, LANES + SLIDES : LANES + SLIDES + 1]
            for head in range(LOCAL_HEADS)
        ]
    )
    first = matmul(back, first).astype(jnp.bfloat16)
    last = matmul(back, last).astype(jnp.bfloat16)
    half = ROWS // 2
    last = jnp.concatenate([last[:half, HEAD_DIM:], last[half:, HEAD_DIM:]], 1)
    for copy in range(4):
        mixed[copy, :ROWS, :] = first
        mixed[copy, ROWS:, :] = last


def ffn_kernel(tokens, mixed, w_out, gain, w_up, w_down, attended, partial, held):
    half = ROWS // 2
    low = iota((half, LANES), 1) < HEAD_DIM
    none = jnp.zeros((half, LANES), jnp.bfloat16)
    summed = jnp.zeros((ROWS, 768), jnp.float32)
    for group in range(4):
        start = 192 * group
        summed = summed + matmul(mixed[group, :ROWS, :], w_out[start : start + 128, :])
        last = mixed[group, ROWS:, :]
        spread = jnp.concatenate([jnp.where(low, last, none), jnp.where(low, none, last)], 0)
        weight = w_out[start + 128 : start + 192, :]
        summed = summed + matmul(spread, jnp.concatenate([weight, weight], 0))
    summed = summed.astype(jnp.bfloat16)
    held[...] = summed
    attended[...] = held[pl.ds(pl.multiple_of(lax.axis_index("mp") * 128, 128), 128), :]
    normed = layer_norm(tokens[...].astype(jnp.float32) + summed.astype(jnp.float32), gain[...])
    raised = matmul(normed, w_up[...])
    hidden = (0.5 * raised * (1.0 + lax.erf(raised * 0.7071067811865476))).astype(jnp.bfloat16)
    partial[...] = matmul(hidden, w_down[...]).astype(jnp.bfloat16).reshape(4, 128, 768)


def call(kernel, micros, outs, ins, scratch=()):
    places = {"smem": pltpu.SMEM, "vmem": pltpu.VMEM}
    return pl.pallas_call(
        kernel,
        out_shape=[jax.ShapeDtypeStruct(*out) for out in outs],
        in_specs=[pl.BlockSpec(memory_space=places[where]) for _, where in ins],
        out_specs=[pl.BlockSpec(memory_space=pltpu.VMEM) for _ in outs],
        scratch_shapes=list(scratch),
        cost_estimate=pl.CostEstimate(
            flops=int(micros * 1.1e9), bytes_accessed=int(micros * 1e6), transcendentals=0
        ),
        compiler_params=pltpu.CompilerParams(vmem_limit_bytes=VMEM),
    )(*[array for array, _ in ins])


def swap(value, step):
    return lax.ppermute(value, "seq", [(i, i ^ step) for i in range(lax.axis_size("seq"))])


def local(tokens, slide_tiles, attn_gain, w_query, w_key, w_value, w_out, ffn_gain, w_up, w_down):
    bf16, f32 = jnp.bfloat16, jnp.float32
    v, s = "vmem", "smem"
    columns = [[16 * z + place for z in range(FAR_GROUP)] for place in range(16)]
    across = [
        (16 * z + (place ^ (2 * z)), 16 * z + place) for z in range(FAR_GROUP) for place in range(16)
    ]
    query, own, mid, far = call(
        project_kernel,
        4,
        [
            ((ROWS, 256), bf16), ((ROWS, 384), bf16), ((CLASS_ROWS, 384), bf16),
            ((FAR_GROUP, FAR_ROWS, 640), bf16),
        ],
        [(tokens, v), (attn_gain, v), (w_query.T, v), (w_key.T, v), (w_value.T, v)],
    )
    side = swap(own, 2)
    mid_a, mid_b = swap(mid, 4), swap(mid, 6)
    w_out_all = lax.all_gather(w_out, "mp", axis=0, tiled=True)
    far_rows = lax.all_to_all(
        far, "seq", split_axis=0, concat_axis=0, tiled=True, axis_index_groups=columns
    )
    far_here = lax.ppermute(far_rows[:, :, 256:].reshape(128, 384), "seq", across)
    swapped = swap(jnp.concatenate([own, side, mid_a, mid_b], 0), 1)
    far_other = swap(far_here, 1)
    state = [((LOCAL_HEADS, ROWS, LANES), f32), ((LOCAL_HEADS, ROWS, 256), f32)]
    held = [pltpu.VMEM(*shape) for shape in state]
    peaks, sums = call(
        near_kernel, 5, state, [(slide_tiles, s), (query, v), (own, v), (side, v)]
    )
    (parts,) = call(
        far_kernel,
        2,
        [((FAR_GROUP, FAR_ROWS, 384), f32)],
        [(slide_tiles, s), (far_rows, v), (far_here, v), (far_other, v)],
    )
    peaks, sums = call(
        rest_kernel,
        7,
        state,
        [
            (slide_tiles, s), (query, v), (own, v), (side, v), (mid_a, v), (mid_b, v), (swapped, v),
            (peaks, v), (sums, v),
        ],
    )
    parts = lax.all_to_all(
        parts, "seq", split_axis=0, concat_axis=0, tiled=True, axis_index_groups=columns
    )
    mixed, far_attended = call(
        finish_kernel,
        2,
        [((4, 768, LANES), bf16), ((FAR_ROWS, 192), bf16)],
        [(parts, v), (peaks, v), (sums, v)],
        held,
    )
    mixed = lax.all_to_all(mixed, "mp", split_axis=0, concat_axis=0, tiled=True)
    attended, partial = call(
        ffn_kernel,
        6,
        [((ROWS // 4, 768), bf16), ((4, 128, 768), bf16)],
        [(tokens, v), (mixed, v), (w_out_all, v), (ffn_gain, v), (w_up, v), (w_down, v)],
        [pltpu.VMEM((ROWS, 768), bf16)],
    )
    terms = lax.all_to_all(partial, "mp", split_axis=0, concat_axis=0, tiled=True)
    ffn_out = jnp.sum(terms.astype(f32), 0).astype(bf16)
    return (attended, far_attended, ffn_out)


def solution(mesh):
    return jax.shard_map(
        local,
        mesh=mesh,
        in_specs=(
            P("seq", None),
            P(),
            P(),
            P(None, "mp"),
            P(None, "mp"),
            P(None, "mp"),
            P("mp", None),
            P(),
            P(None, "mp"),
            P("mp", None),
        ),
        out_specs=(P(("seq", "mp"), None), P("seq", "mp"), P(("seq", "mp"), None)),
        check_vma=False,
    )
```

```python
import functools

import jax
import jax.numpy as jnp
from jax import lax
from jax.experimental import pallas as pl
from jax.experimental.pallas import tpu as pltpu
from jax.sharding import PartitionSpec as P

HEAD_DIM = 64
LOCAL_HEADS = 3
RATE_MID = 4
RATE_FAR = 32
ROWS = 512
CLASS_ROWS = ROWS // RATE_MID
FAR_ROWS = ROWS // RATE_FAR
LANES = 128
SLIDES = 4
WIDTH = 768
HALF = WIDTH // 2
BLOCK = 128
EPS = 1e-05
HIDDEN_SCORE = -1e30
VMEM = 24 * 1024 * 1024

KEY_TILE = (0, 0, 2)
VALUE_TILE = (1, 1, 2)
QUERY_TILE = (0, 0, 1)
SPARE = (64, 0, 0)
FAR_GROUP = 8


def iota(shape, dim):
    return lax.broadcasted_iota(jnp.int32, shape, dim)


def place_of(row):
    return (row & 3) * CLASS_ROWS + ((row >> 2) & 7) * FAR_ROWS + (row >> 5)


def row_at(place):
    return (place & 15) * RATE_FAR + ((place >> 4) & 7) * RATE_MID + (place >> 7)


def layer_norm(as_float, gain):
    mean_val = jnp.mean(as_float, -1, keepdims=True)
    centered = as_float - mean_val
    variance = jnp.mean(centered * centered, -1, keepdims=True)
    return (centered * lax.rsqrt(variance + EPS) * gain.astype(jnp.float32)).astype(jnp.bfloat16)


def matmul(left, right):
    return jnp.dot(left, right, preferred_element_type=jnp.float32)


def matmul_t(left, right):
    return lax.dot_general(
        left, right, (((1,), (1,)), ((), ())), preferred_element_type=jnp.float32
    )


def slide_of(positions, ends):
    index = (positions >= ends[0]).astype(jnp.int32)
    for end in ends[1:]:
        index = index + (positions >= end).astype(jnp.int32)
    return index


def slide_ends(tiles_ref):
    ends = [tiles_ref[0]]
    for slide in range(1, SLIDES - 1):
        ends.append(ends[-1] + tiles_ref[slide])
    return ends


def query_marks(positions, ends):
    rows = positions.shape[0]
    lane = iota((rows, LANES), 1)
    return (lane == slide_of(positions, ends)).astype(jnp.bfloat16)


def key_marks(positions, ends):
    rows = positions.shape[0]
    lane = iota((rows, LANES), 1)
    hide = (lane < SLIDES) & (lane != slide_of(positions, ends))
    marks = jnp.where(hide, HIDDEN_SCORE, jnp.where(lane == SLIDES, 1.0, 0.0))
    return marks.astype(jnp.bfloat16)


def head_lanes(value, head):
    lane = iota(value.shape, 1)
    keep = lane < HEAD_DIM if head != 1 else lane >= HEAD_DIM
    return jnp.where(keep, value, jnp.zeros_like(value))


def tile(index):
    return slice(index * LANES, (index + 1) * LANES)


def project_kernel(tokens, gain, w_query, w_key, w_value, query, keyval, mid, far):
    mp = lax.axis_index("mp")
    normed = layer_norm(tokens[...].astype(jnp.float32), gain[...])
    order = iota((ROWS, ROWS), 0) == place_of(iota((ROWS, ROWS), 1))
    normed = matmul(order.astype(jnp.bfloat16), normed).astype(jnp.bfloat16)
    scaled = (matmul_t(normed, w_query[...]) * (1.0 / 8.0)).astype(jnp.bfloat16)
    query[:, :192] = scaled
    query[:, 192:] = jnp.zeros((ROWS, 64), jnp.bfloat16)
    key = matmul_t(normed, w_key[...]).astype(jnp.bfloat16)
    value = matmul_t(normed, w_value[...]).astype(jnp.bfloat16)
    keyval[:, tile(0)] = key[:, :128]
    keyval[:, tile(1)] = value[:, :128]
    keyval[:, tile(2)] = jnp.concatenate([key[:, 128:], value[:, 128:]], 1)

    def pick(source, index, rows):
        starts = []
        for head in range(LOCAL_HEADS):
            number = mp * LOCAL_HEADS + head
            start = (number & 3) * CLASS_ROWS
            if rows == FAR_ROWS:
                start = start + (number >> 2) * FAR_ROWS
            starts.append(pl.ds(pl.multiple_of(start, rows), rows))
        if index == KEY_TILE[2] and source is keyval or index == QUERY_TILE[2] and source is query:
            return source[starts[2], tile(index)]
        low, high = source[starts[0], tile(index)], source[starts[1], tile(index)]
        return jnp.where(iota(low.shape, 1) < HEAD_DIM, low, high)

    for index in range(3):
        mid[:, tile(index)] = pick(keyval, index, CLASS_ROWS)
    picked = [pick(query, index, FAR_ROWS) for index in range(2)]
    picked += [pick(keyval, index, FAR_ROWS) for index in range(3)]
    for index in range(5):
        for copy in range(FAR_GROUP):
            far[copy, :, tile(index)] = picked[index]


def attend(query, keys, values, head):
    scores = matmul_t(query, keys)
    peak = jnp.max(scores, -1, keepdims=True)
    weights = jnp.exp(scores - peak).astype(jnp.bfloat16)
    sums = matmul(weights, values)
    lane = iota((sums.shape[0], LANES), 1)
    total = sums[:, LANES + SLIDES : LANES + SLIDES + 1]
    return peak, pack(sums[:, :LANES], peak, total, head, lane)


def pack(sums, peak, total, head, lane):
    return jnp.where(
        lane == SPARE[head], peak, jnp.where(lane == SPARE[head] + 1, total, sums)
    )


def join(held, more, peak, head):
    spare = SPARE[head]
    before = held[:, spare : spare + 1]
    largest = jnp.maximum(before, peak)
    both = held * jnp.exp(before - largest) + more * jnp.exp(peak - largest)
    return jnp.where(iota(both.shape, 1) == spare, largest, both)


def marks_near(seq, ends, steps):
    rows = row_at(iota((ROWS, LANES), 0))
    return jnp.concatenate([key_marks(rows + (seq ^ step) * ROWS, ends) for step in steps], 0)


def near_kernel(tiles, query, own, side, state):
    ends = slide_ends(tiles)
    seq = lax.axis_index("seq")
    marks = query_marks(row_at(iota((ROWS, LANES), 0)) + seq * ROWS, ends)
    keys_marks = marks_near(seq, ends, (0, 2))
    for head in range(LOCAL_HEADS):
        key_tile, value_tile = tile(KEY_TILE[head]), tile(VALUE_TILE[head])
        asked = head_lanes(query[:, tile(QUERY_TILE[head])], head)
        keys = jnp.concatenate([own[:, key_tile], side[:, key_tile]], 0)
        values = jnp.concatenate([own[:, value_tile], side[:, value_tile]], 0)
        _, state[head] = attend(
            jnp.concatenate([asked, marks], 1),
            jnp.concatenate([keys, keys_marks], 1),
            jnp.concatenate([values, keys_marks], 1),
            head,
        )


def rest_kernel(tiles, query, own, side, mid_a, mid_b, swapped, held, state):
    ends = slide_ends(tiles)
    seq, mp = lax.axis_index("seq"), lax.axis_index("mp")
    marks = query_marks(row_at(iota((ROWS, LANES), 0)) + seq * ROWS, ends)
    near_marks = marks_near(seq, ends, (1, 3))
    for head in range(LOCAL_HEADS):
        key_tile, value_tile = tile(KEY_TILE[head]), tile(VALUE_TILE[head])
        asked = head_lanes(query[:, tile(QUERY_TILE[head])], head)
        peak, more = attend(
            jnp.concatenate([asked, marks], 1),
            jnp.concatenate([swapped[: 2 * ROWS, key_tile], near_marks], 1),
            jnp.concatenate([swapped[: 2 * ROWS, value_tile], near_marks], 1),
            head,
        )
        state[head] = join(held[head], more, peak, head)

        offset = (mp * LOCAL_HEADS + head) & 3
        start = pl.multiple_of(offset * CLASS_ROWS, CLASS_ROWS)
        picked = pl.ds(start, CLASS_ROWS)
        place = iota((CLASS_ROWS, LANES), 0)
        class_rows = offset + RATE_MID * ((place >> 4) + ((place & 15) << 3))
        class_marks = jnp.concatenate(
            [key_marks(class_rows + (seq ^ step) * ROWS, ends) for step in (0, 2, 1, 3, 4, 6, 5, 7)],
            0,
        )
        asked = head_lanes(query[picked, tile(QUERY_TILE[head])], head)
        asked = jnp.concatenate([asked, query_marks(class_rows + seq * ROWS, ends)], 1)

        def gathered(lanes):
            return jnp.concatenate(
                [
                    own[picked, lanes],
                    side[picked, lanes],
                    swapped[picked, lanes],
                    swapped[pl.ds(start + ROWS, CLASS_ROWS), lanes],
                    mid_a[:, lanes],
                    mid_b[:, lanes],
                    swapped[2 * ROWS :, lanes],
                ],
                0,
            )

        peak, more = attend(
            asked,
            jnp.concatenate([gathered(key_tile), class_marks], 1),
            jnp.concatenate([gathered(value_tile), class_marks], 1),
            head,
        )
        state[head, picked, :] = join(state[head, picked, :], more, peak, head)


def far_kernel(tiles, rows, here, other, parts):
    ends = slide_ends(tiles)
    seq, mp = lax.axis_index("seq"), lax.axis_index("mp")
    column = seq & 15
    beside = column ^ ((seq >> 4) << 1)
    count = FAR_GROUP * FAR_ROWS
    shape = (count, 2 * count)

    def position(place, holder):
        return ((place >> 4) * 16 + holder) * ROWS + (place & 15) * RATE_FAR

    at = iota(shape, 1)
    holder = jnp.where(at < count, beside, beside ^ 1)
    key_at = position(at & (count - 1), holder)
    query_at = position(iota(shape, 0), column)
    lane = iota((count, LANES), 1)
    for head in range(LOCAL_HEADS):
        number = mp * LOCAL_HEADS + head
        key_tile, value_tile = tile(KEY_TILE[head]), tile(VALUE_TILE[head])
        asked = rows[:, :, tile(QUERY_TILE[head])].reshape(count, LANES)
        asked = head_lanes(asked, head)
        scores = matmul_t(asked, jnp.concatenate([here[:, key_tile], other[:, key_tile]], 0))
        same = slide_of(query_at + number, ends) == slide_of(key_at + number, ends)
        scores = jnp.where(same, scores, HIDDEN_SCORE)
        peak = jnp.max(scores, -1, keepdims=True)
        weights = jnp.exp(scores - peak)
        total = jnp.sum(weights, -1, keepdims=True)
        values = jnp.concatenate([here[:, value_tile], other[:, value_tile]], 0)
        part = matmul(weights.astype(jnp.bfloat16), values)
        part = pack(part, peak, total, head, lane)
        parts[:, :, tile(head)] = part.reshape(FAR_GROUP, FAR_ROWS, LANES)


def finish_kernel(parts, held, w_out, terms, far_out, state):
    mp = lax.axis_index("mp")
    state[...] = held[...]
    far_parts = []
    for head in range(LOCAL_HEADS):
        spare = SPARE[head]
        pieces = [parts[index, :, tile(head)] for index in range(FAR_GROUP)]
        tops = [piece[:, spare : spare + 1] for piece in pieces]
        peak = functools.reduce(jnp.maximum, tops)
        total = jnp.zeros((FAR_ROWS, LANES), jnp.float32)
        for piece, top in zip(pieces, tops):
            total = total + piece * jnp.exp(top - peak)
        far_parts.append(total / total[:, spare + 1 : spare + 2])
        number = mp * LOCAL_HEADS + head
        start = (number & 3) * CLASS_ROWS + (number >> 2) * FAR_ROWS
        picked = pl.ds(pl.multiple_of(start, FAR_ROWS), FAR_ROWS)
        state[head, picked, :] = join(state[head, picked, :], total, peak, head)

    def packed(values):
        first = jnp.where(iota(values[0].shape, 1) < HEAD_DIM, values[0], values[1])
        return first.astype(jnp.bfloat16), values[2].astype(jnp.bfloat16)

    first, last = packed(far_parts)
    far_out[:, :128] = first
    far_out[:, 128:] = last[:, HEAD_DIM:]
    back = (place_of(iota((ROWS, ROWS), 0)) == iota((ROWS, ROWS), 1)).astype(jnp.bfloat16)
    first, last = packed(
        [
            state[head] / state[head, :, SPARE[head] + 1 : SPARE[head] + 2]
            for head in range(LOCAL_HEADS)
        ]
    )
    mixed = jnp.concatenate([first, last[:, HEAD_DIM:]], 1)
    mixed = matmul(back, mixed).astype(jnp.bfloat16)
    terms[...] = matmul(mixed, w_out[...]).astype(jnp.bfloat16).reshape(4, BLOCK, WIDTH)


def weights_kernel(w_up, w_down, out, sems):
    start = pl.multiple_of((lax.axis_index("seq") & 1) * HALF, HALF)
    copies = [
        pltpu.make_async_copy(
            w_up.at[pl.ds(block * HALF, HALF), pl.ds(start, HALF)],
            out.at[pl.ds(0, HALF), pl.ds(block * HALF, HALF)],
            sems.at[block],
        )
        for block in range(2)
    ]
    copies.append(
        pltpu.make_async_copy(
            w_down.at[pl.ds(start, HALF), :], out.at[pl.ds(HALF, HALF), :], sems.at[2]
        )
    )
    for copy in copies:
        copy.start()
    for copy in copies:
        copy.wait()


def hidden_part(normed, weights):
    raised = matmul(normed[:, :HALF], weights[0, :HALF, :HALF])
    raised = raised + matmul(normed[:, HALF:], weights[0, :HALF, HALF:])
    hidden = (0.5 * raised * (1.0 + lax.erf(raised * 0.7071067811865476))).astype(jnp.bfloat16)
    return matmul(hidden, weights[0, HALF:, :])


def first_kernel(tokens, terms, gain, weights, attended, normed, total):
    @pl.when(pl.program_id(0) == 0)
    def _():
        summed = terms[0].astype(jnp.float32)
        for group in range(1, 4):
            summed = summed + terms[group].astype(jnp.float32)
        summed = summed.astype(jnp.bfloat16)
        attended[...] = summed
        start = pl.multiple_of(lax.axis_index("mp") * BLOCK, BLOCK)
        own = tokens[pl.ds(start, BLOCK), :].astype(jnp.float32)
        normed[...] = layer_norm(own + summed.astype(jnp.float32), gain[...])
        total[...] = jnp.zeros_like(total)

    total[...] += hidden_part(normed[...], weights)


def second_kernel(normed, before, weights, out, total):
    step = pl.program_id(0)

    @pl.when(step == 0)
    def _():
        total[...] = before[...]

    total[...] += hidden_part(normed[...], weights)

    @pl.when(step == pl.num_programs(0) - 1)
    def _():
        out[...] = total[...].astype(jnp.bfloat16)


def whole(shape):
    return pl.BlockSpec(shape, lambda step: (0,) * len(shape))


def ffn(kernel, arrays, weights, outs, scratch=()):
    return pl.pallas_call(
        kernel,
        grid=(4,),
        out_shape=[jax.ShapeDtypeStruct(*out) for out in outs],
        in_specs=[whole(array.shape) for array in arrays]
        + [pl.BlockSpec((1, 2 * HALF, WIDTH), lambda step: (step, 0, 0))],
        out_specs=[whole(out[0]) for out in outs],
        scratch_shapes=list(scratch),
        cost_estimate=pl.CostEstimate(
            flops=int(3e9), bytes_accessed=int(5e6), transcendentals=0
        ),
        compiler_params=pltpu.CompilerParams(vmem_limit_bytes=24 * 1024 * 1024),
    )(*arrays, weights)


def call(kernel, micros, outs, ins, scratch=()):
    places = {"smem": pltpu.SMEM, "vmem": pltpu.VMEM}
    return pl.pallas_call(
        kernel,
        out_shape=[jax.ShapeDtypeStruct(*out) for out in outs],
        in_specs=[pl.BlockSpec(memory_space=places[where]) for _, where in ins],
        out_specs=[pl.BlockSpec(memory_space=pltpu.VMEM) for _ in outs],
        scratch_shapes=list(scratch),
        cost_estimate=pl.CostEstimate(
            flops=int(micros * 1.1e9), bytes_accessed=int(micros * 1e6), transcendentals=0
        ),
        compiler_params=pltpu.CompilerParams(vmem_limit_bytes=VMEM),
    )(*[array for array, _ in ins])


def swap(value, step):
    return lax.ppermute(value, "seq", [(i, i ^ step) for i in range(lax.axis_size("seq"))])


def local(tokens, slide_tiles, attn_gain, w_query, w_key, w_value, w_out, ffn_gain, w_up, w_down):
    bf16, f32 = jnp.bfloat16, jnp.float32
    v, s = "vmem", "smem"
    columns = [[16 * z + place for z in range(FAR_GROUP)] for place in range(16)]
    across = [
        (16 * z + (place ^ (2 * z)), 16 * z + place) for z in range(FAR_GROUP) for place in range(16)
    ]
    packed = pl.pallas_call(
        weights_kernel,
        out_shape=jax.ShapeDtypeStruct((2 * HALF, WIDTH), bf16),
        in_specs=[pl.BlockSpec(memory_space=pl.ANY)] * 2,
        out_specs=pl.BlockSpec(memory_space=pl.ANY),
        scratch_shapes=[pltpu.SemaphoreType.DMA((3,))],
    )(w_up, w_down)
    mine = lax.all_gather(packed, "mp", axis=0)
    theirs = swap(mine, 1)
    query, own, mid, far = call(
        project_kernel,
        4,
        [
            ((ROWS, 256), bf16), ((ROWS, 384), bf16), ((CLASS_ROWS, 384), bf16),
            ((FAR_GROUP, FAR_ROWS, 640), bf16),
        ],
        [(tokens, v), (attn_gain, v), (w_query.T, v), (w_key.T, v), (w_value.T, v)],
    )
    side = swap(own, 2)
    mid_a, mid_b = swap(mid, 4), swap(mid, 6)
    far_rows = lax.all_to_all(
        far, "seq", split_axis=0, concat_axis=0, tiled=True, axis_index_groups=columns
    )
    far_here = lax.ppermute(far_rows[:, :, 256:].reshape(128, 384), "seq", across)
    swapped = swap(jnp.concatenate([own, side, mid_a, mid_b], 0), 1)
    far_other = swap(far_here, 1)
    state = ((LOCAL_HEADS, ROWS, LANES), f32)
    (near,) = call(
        near_kernel, 5, [state], [(slide_tiles, s), (query, v), (own, v), (side, v)]
    )
    (parts,) = call(
        far_kernel,
        2,
        [((FAR_GROUP, FAR_ROWS, 384), f32)],
        [(slide_tiles, s), (far_rows, v), (far_here, v), (far_other, v)],
    )
    (both,) = call(
        rest_kernel,
        7,
        [state],
        [
            (slide_tiles, s), (query, v), (own, v), (side, v), (mid_a, v), (mid_b, v), (swapped, v),
            (near, v),
        ],
    )
    parts = lax.all_to_all(
        parts, "seq", split_axis=0, concat_axis=0, tiled=True, axis_index_groups=columns
    )
    terms, far_attended = call(
        finish_kernel,
        3,
        [((4, BLOCK, WIDTH), bf16), ((FAR_ROWS, 192), bf16)],
        [(parts, v), (both, v), (w_out, v)],
        [pltpu.VMEM(*state)],
    )
    terms = lax.all_to_all(terms, "mp", split_axis=0, concat_axis=0, tiled=True)
    attended, normed, total = ffn(
        first_kernel,
        [tokens, terms, ffn_gain],
        mine,
        [((BLOCK, WIDTH), bf16), ((BLOCK, WIDTH), bf16), ((BLOCK, WIDTH), f32)],
    )
    (ffn_out,) = ffn(
        second_kernel,
        [normed, total],
        theirs,
        [((BLOCK, WIDTH), bf16)],
        [pltpu.VMEM((BLOCK, WIDTH), f32)],
    )
    return (attended, far_attended, ffn_out)


def solution(mesh):
    return jax.shard_map(
        local,
        mesh=mesh,
        in_specs=(
            P("seq", None),
            P(),
            P(),
            P(None, "mp"),
            P(None, "mp"),
            P(None, "mp"),
            P("mp", None),
            P(),
            P(None, "mp"),
            P("mp", None),
        ),
        out_specs=(P(("seq", "mp"), None), P("seq", "mp"), P(("seq", "mp"), None)),
        check_vma=False,
    )
```

```python
import functools

import jax
import jax.numpy as jnp
from jax import lax
from jax.experimental import pallas as pl
from jax.experimental.pallas import tpu as pltpu
from jax.sharding import PartitionSpec as P

HEAD_DIM = 64
LOCAL_HEADS = 3
RATE_MID = 4
RATE_FAR = 32
ROWS = 512
CLASS_ROWS = ROWS // RATE_MID
FAR_ROWS = ROWS // RATE_FAR
LANES = 128
SLIDES = 4
WIDTH = 768
HALF = WIDTH // 2
BLOCK = 128
EPS = 1e-05
HIDDEN_SCORE = -1e30
VMEM = 16 * 1024 * 1024

KEY_TILE = (0, 0, 2)
VALUE_TILE = (1, 1, 2)
QUERY_TILE = (0, 0, 1)
SPARE = (64, 0, 0)
FAR_GROUP = 8


def iota(shape, dim):
    return lax.broadcasted_iota(jnp.int32, shape, dim)


def place_of(row):
    return (row & 3) * CLASS_ROWS + ((row >> 2) & 7) * FAR_ROWS + (row >> 5)


def row_at(place):
    return (place & 15) * RATE_FAR + ((place >> 4) & 7) * RATE_MID + (place >> 7)


def layer_norm(as_float, gain):
    mean_val = jnp.mean(as_float, -1, keepdims=True)
    centered = as_float - mean_val
    variance = jnp.mean(centered * centered, -1, keepdims=True)
    return (centered * lax.rsqrt(variance + EPS) * gain.astype(jnp.float32)).astype(jnp.bfloat16)


def matmul(left, right):
    return jnp.dot(left, right, preferred_element_type=jnp.float32)


def matmul_t(left, right):
    return lax.dot_general(
        left, right, (((1,), (1,)), ((), ())), preferred_element_type=jnp.float32
    )


def slide_of(positions, ends):
    index = (positions >= ends[0]).astype(jnp.int32)
    for end in ends[1:]:
        index = index + (positions >= end).astype(jnp.int32)
    return index


def slide_ends(tiles_ref):
    ends = [tiles_ref[0]]
    for slide in range(1, SLIDES - 1):
        ends.append(ends[-1] + tiles_ref[slide])
    return ends


def query_marks(positions, ends):
    rows = positions.shape[0]
    lane = iota((rows, LANES), 1)
    return (lane == slide_of(positions, ends)).astype(jnp.bfloat16)


def key_marks(positions, ends):
    rows = positions.shape[0]
    lane = iota((rows, LANES), 1)
    hide = (lane < SLIDES) & (lane != slide_of(positions, ends))
    marks = jnp.where(hide, HIDDEN_SCORE, jnp.where(lane == SLIDES, 1.0, 0.0))
    return marks.astype(jnp.bfloat16)


def head_lanes(value, head):
    lane = iota(value.shape, 1)
    keep = lane < HEAD_DIM if head != 1 else lane >= HEAD_DIM
    return jnp.where(keep, value, jnp.zeros_like(value))


def tile(index):
    return slice(index * LANES, (index + 1) * LANES)


def project(normed, w_query, w_key, w_value):
    asked = (matmul_t(normed, w_query[...]) * (1.0 / 8.0)).astype(jnp.bfloat16)
    key = matmul_t(normed, w_key[...]).astype(jnp.bfloat16)
    value = matmul_t(normed, w_value[...]).astype(jnp.bfloat16)
    none = jnp.zeros_like(asked[:, 128:])
    queries = [asked[:, :128], jnp.concatenate([asked[:, 128:], none], 1)]
    keyvals = [key[:, :128], value[:, :128]]
    return queries, keyvals + [jnp.concatenate([key[:, 128:], value[:, 128:]], 1)]


def far_rows_kernel(tokens, gain, w_query, w_key, w_value, far):
    first = lax.axis_index("mp") * LOCAL_HEADS
    shape = (LOCAL_HEADS * FAR_ROWS, ROWS)
    place = iota(shape, 0)
    wanted = (place & 15) * RATE_FAR + (place >> 4) + first
    rows = matmul((iota(shape, 1) == wanted).astype(jnp.bfloat16), tokens[...])
    queries, keyvals = project(layer_norm(rows, gain[...]), w_query, w_key, w_value)
    low = iota((FAR_ROWS, LANES), 1) < HEAD_DIM
    for index, value in enumerate(queries + keyvals):
        parts = [value[FAR_ROWS * head : FAR_ROWS * (head + 1)] for head in range(LOCAL_HEADS)]
        chosen = parts[2] if index in (1, 4) else jnp.where(low, parts[0], parts[1])
        for copy in range(FAR_GROUP):
            far[copy, :, tile(index)] = chosen


def project_kernel(tokens, gain, w_query, w_key, w_value, query, keyval, mid):
    mp = lax.axis_index("mp")
    normed = layer_norm(tokens[...].astype(jnp.float32), gain[...])
    order = iota((ROWS, ROWS), 0) == place_of(iota((ROWS, ROWS), 1))
    normed = matmul(order.astype(jnp.bfloat16), normed).astype(jnp.bfloat16)
    queries, keyvals = project(normed, w_query, w_key, w_value)
    for index, value in enumerate(queries):
        query[:, tile(index)] = value
    for index, value in enumerate(keyvals):
        keyval[:, tile(index)] = value
    starts = []
    for head in range(LOCAL_HEADS):
        start = ((mp * LOCAL_HEADS + head) & 3) * CLASS_ROWS
        starts.append(pl.ds(pl.multiple_of(start, CLASS_ROWS), CLASS_ROWS))
    low = iota((CLASS_ROWS, LANES), 1) < HEAD_DIM
    for index in range(2):
        mid[:, tile(index)] = jnp.where(
            low, keyval[starts[0], tile(index)], keyval[starts[1], tile(index)]
        )
    mid[:, tile(2)] = keyval[starts[2], tile(2)]


def attend(query, keys, values, head):
    scores = matmul_t(query, keys)
    peak = jnp.max(scores, -1, keepdims=True)
    weights = jnp.exp(scores - peak).astype(jnp.bfloat16)
    sums = matmul(weights, values)
    lane = iota((sums.shape[0], LANES), 1)
    total = sums[:, LANES + SLIDES : LANES + SLIDES + 1]
    return peak, pack(sums[:, :LANES], peak, total, head, lane)


def pack(sums, peak, total, head, lane):
    return jnp.where(
        lane == SPARE[head], peak, jnp.where(lane == SPARE[head] + 1, total, sums)
    )


def join(held, more, peak, head):
    spare = SPARE[head]
    before = held[:, spare : spare + 1]
    largest = jnp.maximum(before, peak)
    both = held * jnp.exp(before - largest) + more * jnp.exp(peak - largest)
    return jnp.where(iota(both.shape, 1) == spare, largest, both)


def marks_near(seq, ends, steps):
    rows = row_at(iota((ROWS, LANES), 0))
    return jnp.concatenate([key_marks(rows + (seq ^ step) * ROWS, ends) for step in steps], 0)


def near_kernel(tiles, query, own, side, state):
    ends = slide_ends(tiles)
    seq = lax.axis_index("seq")
    marks = query_marks(row_at(iota((ROWS, LANES), 0)) + seq * ROWS, ends)
    keys_marks = marks_near(seq, ends, (0, 2))
    for head in range(LOCAL_HEADS):
        key_tile, value_tile = tile(KEY_TILE[head]), tile(VALUE_TILE[head])
        asked = head_lanes(query[:, tile(QUERY_TILE[head])], head)
        keys = jnp.concatenate([own[:, key_tile], side[:, key_tile]], 0)
        values = jnp.concatenate([own[:, value_tile], side[:, value_tile]], 0)
        _, state[head] = attend(
            jnp.concatenate([asked, marks], 1),
            jnp.concatenate([keys, keys_marks], 1),
            jnp.concatenate([values, keys_marks], 1),
            head,
        )


def rest_kernel(tiles, query, own, side, mid_a, mid_b, swapped, held, state):
    ends = slide_ends(tiles)
    seq, mp = lax.axis_index("seq"), lax.axis_index("mp")
    marks = query_marks(row_at(iota((ROWS, LANES), 0)) + seq * ROWS, ends)
    near_marks = marks_near(seq, ends, (1, 3))
    for head in range(LOCAL_HEADS):
        key_tile, value_tile = tile(KEY_TILE[head]), tile(VALUE_TILE[head])
        asked = head_lanes(query[:, tile(QUERY_TILE[head])], head)
        peak, more = attend(
            jnp.concatenate([asked, marks], 1),
            jnp.concatenate([swapped[: 2 * ROWS, key_tile], near_marks], 1),
            jnp.concatenate([swapped[: 2 * ROWS, value_tile], near_marks], 1),
            head,
        )
        state[head] = join(held[head], more, peak, head)

        offset = (mp * LOCAL_HEADS + head) & 3
        start = pl.multiple_of(offset * CLASS_ROWS, CLASS_ROWS)
        picked = pl.ds(start, CLASS_ROWS)
        place = iota((CLASS_ROWS, LANES), 0)
        class_rows = offset + RATE_MID * ((place >> 4) + ((place & 15) << 3))
        class_marks = jnp.concatenate(
            [key_marks(class_rows + (seq ^ step) * ROWS, ends) for step in (0, 2, 1, 3, 4, 6, 5, 7)],
            0,
        )
        asked = head_lanes(query[picked, tile(QUERY_TILE[head])], head)
        asked = jnp.concatenate([asked, query_marks(class_rows + seq * ROWS, ends)], 1)

        def gathered(lanes):
            return jnp.concatenate(
                [
                    own[picked, lanes],
                    side[picked, lanes],
                    swapped[picked, lanes],
                    swapped[pl.ds(start + ROWS, CLASS_ROWS), lanes],
                    mid_a[:, lanes],
                    mid_b[:, lanes],
                    swapped[2 * ROWS :, lanes],
                ],
                0,
            )

        peak, more = attend(
            asked,
            jnp.concatenate([gathered(key_tile), class_marks], 1),
            jnp.concatenate([gathered(value_tile), class_marks], 1),
            head,
        )
        state[head, picked, :] = join(state[head, picked, :], more, peak, head)


def far_kernel(tiles, rows, here, other, parts):
    ends = slide_ends(tiles)
    seq, mp = lax.axis_index("seq"), lax.axis_index("mp")
    column = seq & 15
    beside = column ^ ((seq >> 4) << 1)
    count = FAR_GROUP * FAR_ROWS
    shape = (count, 2 * count)

    def position(place, holder):
        return ((place >> 4) * 16 + holder) * ROWS + (place & 15) * RATE_FAR

    at = iota(shape, 1)
    holder = jnp.where(at < count, beside, beside ^ 1)
    key_at = position(at & (count - 1), holder)
    query_at = position(iota(shape, 0), column)
    lane = iota((count, LANES), 1)
    for head in range(LOCAL_HEADS):
        number = mp * LOCAL_HEADS + head
        key_tile, value_tile = tile(KEY_TILE[head]), tile(VALUE_TILE[head])
        asked = rows[:, :, tile(QUERY_TILE[head])].reshape(count, LANES)
        asked = head_lanes(asked, head)
        scores = matmul_t(asked, jnp.concatenate([here[:, key_tile], other[:, key_tile]], 0))
        same = slide_of(query_at + number, ends) == slide_of(key_at + number, ends)
        scores = jnp.where(same, scores, HIDDEN_SCORE)
        peak = jnp.max(scores, -1, keepdims=True)
        weights = jnp.exp(scores - peak)
        total = jnp.sum(weights, -1, keepdims=True)
        values = jnp.concatenate([here[:, value_tile], other[:, value_tile]], 0)
        part = matmul(weights.astype(jnp.bfloat16), values)
        part = pack(part, peak, total, head, lane)
        parts[:, :, tile(head)] = part.reshape(FAR_GROUP, FAR_ROWS, LANES)


def finish_kernel(parts, held, w_out, terms, far_out, state):
    mp = lax.axis_index("mp")
    state[...] = held[...]
    far_parts = []
    for head in range(LOCAL_HEADS):
        spare = SPARE[head]
        pieces = [parts[index, :, tile(head)] for index in range(FAR_GROUP)]
        tops = [piece[:, spare : spare + 1] for piece in pieces]
        peak = functools.reduce(jnp.maximum, tops)
        total = jnp.zeros((FAR_ROWS, LANES), jnp.float32)
        for piece, top in zip(pieces, tops):
            total = total + piece * jnp.exp(top - peak)
        far_parts.append(total / total[:, spare + 1 : spare + 2])
        number = mp * LOCAL_HEADS + head
        start = (number & 3) * CLASS_ROWS + (number >> 2) * FAR_ROWS
        picked = pl.ds(pl.multiple_of(start, FAR_ROWS), FAR_ROWS)
        state[head, picked, :] = join(state[head, picked, :], total, peak, head)

    def packed(values):
        first = jnp.where(iota(values[0].shape, 1) < HEAD_DIM, values[0], values[1])
        return first.astype(jnp.bfloat16), values[2].astype(jnp.bfloat16)

    first, last = packed(far_parts)
    far_out[:, :128] = first
    far_out[:, 128:] = last[:, HEAD_DIM:]
    back = (place_of(iota((ROWS, ROWS), 0)) == iota((ROWS, ROWS), 1)).astype(jnp.bfloat16)
    first, last = packed(
        [
            state[head] / state[head, :, SPARE[head] + 1 : SPARE[head] + 2]
            for head in range(LOCAL_HEADS)
        ]
    )
    mixed = jnp.concatenate([first, last[:, HEAD_DIM:]], 1)
    mixed = matmul(back, mixed).astype(jnp.bfloat16)
    terms[...] = matmul(mixed, w_out[...]).astype(jnp.bfloat16).reshape(4, BLOCK, WIDTH)


def weights_kernel(w_up, w_down, out):
    start = pl.multiple_of((lax.axis_index("seq") & 1) * HALF, HALF)
    out[:HALF, :HALF] = w_up[:HALF, pl.ds(start, HALF)]
    out[:HALF, HALF:] = w_up[HALF:, pl.ds(start, HALF)]
    out[HALF:, :] = w_down[pl.ds(start, HALF), :]


def hidden_part(normed, weights):
    raised = matmul(normed[:, :HALF], weights[0, :HALF, :HALF])
    raised = raised + matmul(normed[:, HALF:], weights[0, :HALF, HALF:])
    hidden = (0.5 * raised * (1.0 + lax.erf(raised * 0.7071067811865476))).astype(jnp.bfloat16)
    return matmul(hidden, weights[0, HALF:, :])


def first_kernel(tokens, terms, gain, weights, attended, normed, total):
    @pl.when(pl.program_id(0) == 0)
    def _():
        summed = terms[0].astype(jnp.float32)
        for group in range(1, 4):
            summed = summed + terms[group].astype(jnp.float32)
        summed = summed.astype(jnp.bfloat16)
        attended[...] = summed
        start = pl.multiple_of(lax.axis_index("mp") * BLOCK, BLOCK)
        own = tokens[pl.ds(start, BLOCK), :].astype(jnp.float32)
        normed[...] = layer_norm(own + summed.astype(jnp.float32), gain[...])
        total[...] = jnp.zeros_like(total)

    total[...] += hidden_part(normed[...], weights)


def second_kernel(normed, before, weights, out, total):
    step = pl.program_id(0)

    @pl.when(step == 0)
    def _():
        total[...] = before[...]

    total[...] += hidden_part(normed[...], weights)

    @pl.when(step == pl.num_programs(0) - 1)
    def _():
        out[...] = total[...].astype(jnp.bfloat16)


def whole(shape):
    return pl.BlockSpec(shape, lambda step: (0,) * len(shape))


def ffn(kernel, arrays, weights, outs, scratch=()):
    return pl.pallas_call(
        kernel,
        grid=(4,),
        out_shape=[jax.ShapeDtypeStruct(*out) for out in outs],
        in_specs=[whole(array.shape) for array in arrays]
        + [pl.BlockSpec((1, 2 * HALF, WIDTH), lambda step: (step, 0, 0))],
        out_specs=[whole(out[0]) for out in outs],
        scratch_shapes=list(scratch),
        cost_estimate=pl.CostEstimate(
            flops=int(3e9), bytes_accessed=int(5e6), transcendentals=0
        ),
        compiler_params=pltpu.CompilerParams(vmem_limit_bytes=24 * 1024 * 1024),
    )(*arrays, weights)


def call(kernel, micros, outs, ins, scratch=()):
    places = {"smem": pltpu.SMEM, "vmem": pltpu.VMEM}
    return pl.pallas_call(
        kernel,
        out_shape=[jax.ShapeDtypeStruct(*out) for out in outs],
        in_specs=[pl.BlockSpec(memory_space=places[where]) for _, where in ins],
        out_specs=[pl.BlockSpec(memory_space=pltpu.VMEM) for _ in outs],
        scratch_shapes=list(scratch),
        cost_estimate=pl.CostEstimate(
            flops=int(micros * 1.1e9), bytes_accessed=int(micros * 1e6), transcendentals=0
        ),
        compiler_params=pltpu.CompilerParams(vmem_limit_bytes=VMEM),
    )(*[array for array, _ in ins])


def swap(value, step):
    return lax.ppermute(value, "seq", [(i, i ^ step) for i in range(lax.axis_size("seq"))])


def local(tokens, slide_tiles, attn_gain, w_query, w_key, w_value, w_out, ffn_gain, w_up, w_down):
    bf16, f32 = jnp.bfloat16, jnp.float32
    v, s = "vmem", "smem"
    columns = [[16 * z + place for z in range(FAR_GROUP)] for place in range(16)]
    across = [
        (16 * z + (place ^ (2 * z)), 16 * z + place) for z in range(FAR_GROUP) for place in range(16)
    ]
    (packed,) = call(weights_kernel, 2, [((2 * HALF, WIDTH), bf16)], [(w_up, v), (w_down, v)])
    mine = lax.all_gather(packed, "mp", axis=0)
    w_query, w_key, w_value = w_query.T, w_key.T, w_value.T
    (far,) = call(
        far_rows_kernel,
        2,
        [((FAR_GROUP, FAR_ROWS, 640), bf16)],
        [(tokens, v), (attn_gain, v), (w_query, v), (w_key, v), (w_value, v)],
    )
    query, own, mid = call(
        project_kernel,
        3,
        [((ROWS, 256), bf16), ((ROWS, 384), bf16), ((CLASS_ROWS, 384), bf16)],
        [(tokens, v), (attn_gain, v), (w_query, v), (w_key, v), (w_value, v)],
    )
    side = swap(own, 2)
    mid_a, mid_b = swap(mid, 4), swap(mid, 6)
    far_rows = lax.all_to_all(
        far, "seq", split_axis=0, concat_axis=0, tiled=True, axis_index_groups=columns
    )
    far_here = lax.ppermute(far_rows[:, :, 256:].reshape(128, 384), "seq", across)
    swapped = swap(jnp.concatenate([own, side, mid_a, mid_b], 0), 1)
    far_other = swap(far_here, 1)
    state = ((LOCAL_HEADS, ROWS, LANES), f32)
    (near,) = call(
        near_kernel, 5, [state], [(slide_tiles, s), (query, v), (own, v), (side, v)]
    )
    (parts,) = call(
        far_kernel,
        2,
        [((FAR_GROUP, FAR_ROWS, 384), f32)],
        [(slide_tiles, s), (far_rows, v), (far_here, v), (far_other, v)],
    )
    (both,) = call(
        rest_kernel,
        7,
        [state],
        [
            (slide_tiles, s), (query, v), (own, v), (side, v), (mid_a, v), (mid_b, v), (swapped, v),
            (near, v),
        ],
    )
    late, _ = lax.optimization_barrier((mine, both))
    theirs = swap(late, 1)
    parts = lax.all_to_all(
        parts, "seq", split_axis=0, concat_axis=0, tiled=True, axis_index_groups=columns
    )
    terms, far_attended = call(
        finish_kernel,
        3,
        [((4, BLOCK, WIDTH), bf16), ((FAR_ROWS, 192), bf16)],
        [(parts, v), (both, v), (w_out, v)],
        [pltpu.VMEM(*state)],
    )
    terms = lax.all_to_all(terms, "mp", split_axis=0, concat_axis=0, tiled=True)
    attended, normed, total = ffn(
        first_kernel,
        [tokens, terms, ffn_gain],
        mine,
        [((BLOCK, WIDTH), bf16), ((BLOCK, WIDTH), bf16), ((BLOCK, WIDTH), f32)],
    )
    (ffn_out,) = ffn(
        second_kernel,
        [normed, total],
        theirs,
        [((BLOCK, WIDTH), bf16)],
        [pltpu.VMEM((BLOCK, WIDTH), f32)],
    )
    return (attended, far_attended, ffn_out)


def solution(mesh):
    return jax.shard_map(
        local,
        mesh=mesh,
        in_specs=(
            P("seq", None),
            P(),
            P(),
            P(None, "mp"),
            P(None, "mp"),
            P(None, "mp"),
            P("mp", None),
            P(),
            P(None, "mp"),
            P("mp", None),
        ),
        out_specs=(P(("seq", "mp"), None), P("seq", "mp"), P(("seq", "mp"), None)),
        check_vma=False,
    )
```

```python
import functools

import jax
import jax.numpy as jnp
from jax import lax
from jax.experimental import pallas as pl
from jax.experimental.pallas import tpu as pltpu
from jax.sharding import PartitionSpec as P

HEAD_DIM = 64
LOCAL_HEADS = 3
RATE_MID = 4
RATE_FAR = 32
ROWS = 512
CLASS_ROWS = ROWS // RATE_MID
FAR_ROWS = ROWS // RATE_FAR
LANES = 128
SLIDES = 4
WIDTH = 768
HALF = WIDTH // 2
BLOCK = 128
EPS = 1e-05
HIDDEN_SCORE = -1e30
VMEM = 16 * 1024 * 1024

KEY_TILE = (0, 0, 2)
VALUE_TILE = (1, 1, 2)
QUERY_TILE = (0, 0, 1)
SPARE = (64, 0, 0)
FAR_GROUP = 8


def iota(shape, dim):
    return lax.broadcasted_iota(jnp.int32, shape, dim)


def place_of(row):
    return (row & 3) * CLASS_ROWS + ((row >> 2) & 7) * FAR_ROWS + (row >> 5)


def row_at(place):
    return (place & 15) * RATE_FAR + ((place >> 4) & 7) * RATE_MID + (place >> 7)


def layer_norm(as_float, gain):
    mean_val = jnp.mean(as_float, -1, keepdims=True)
    centered = as_float - mean_val
    variance = jnp.mean(centered * centered, -1, keepdims=True)
    return (centered * lax.rsqrt(variance + EPS) * gain.astype(jnp.float32)).astype(jnp.bfloat16)


def matmul(left, right):
    return jnp.dot(left, right, preferred_element_type=jnp.float32)


def matmul_t(left, right):
    return lax.dot_general(
        left, right, (((1,), (1,)), ((), ())), preferred_element_type=jnp.float32
    )


def slide_of(positions, ends):
    index = (positions >= ends[0]).astype(jnp.int32)
    for end in ends[1:]:
        index = index + (positions >= end).astype(jnp.int32)
    return index


def slide_ends(tiles_ref):
    ends = [tiles_ref[0]]
    for slide in range(1, SLIDES - 1):
        ends.append(ends[-1] + tiles_ref[slide])
    return ends


def query_marks(positions, ends):
    rows = positions.shape[0]
    lane = iota((rows, LANES), 1)
    return (lane == slide_of(positions, ends)).astype(jnp.bfloat16)


def key_marks(positions, ends):
    rows = positions.shape[0]
    lane = iota((rows, LANES), 1)
    hide = (lane < SLIDES) & (lane != slide_of(positions, ends))
    marks = jnp.where(hide, HIDDEN_SCORE, jnp.where(lane == SLIDES, 1.0, 0.0))
    return marks.astype(jnp.bfloat16)


def head_lanes(value, head):
    lane = iota(value.shape, 1)
    keep = lane < HEAD_DIM if head != 1 else lane >= HEAD_DIM
    return jnp.where(keep, value, jnp.zeros_like(value))


def tile(index):
    return slice(index * LANES, (index + 1) * LANES)


def project(normed, w_query, w_key, w_value):
    asked = (matmul_t(normed, w_query[...]) * (1.0 / 8.0)).astype(jnp.bfloat16)
    key = matmul_t(normed, w_key[...]).astype(jnp.bfloat16)
    value = matmul_t(normed, w_value[...]).astype(jnp.bfloat16)
    none = jnp.zeros_like(asked[:, 128:])
    queries = [asked[:, :128], jnp.concatenate([asked[:, 128:], none], 1)]
    keyvals = [key[:, :128], value[:, :128]]
    return queries, keyvals + [jnp.concatenate([key[:, 128:], value[:, 128:]], 1)]


def far_rows_kernel(tokens, gain, w_query, w_key, w_value, far):
    first = lax.axis_index("mp") * LOCAL_HEADS
    shape = (LOCAL_HEADS * FAR_ROWS, ROWS)
    place = iota(shape, 0)
    wanted = (place & 15) * RATE_FAR + (place >> 4) + first
    rows = matmul((iota(shape, 1) == wanted).astype(jnp.bfloat16), tokens[...])
    queries, keyvals = project(layer_norm(rows, gain[...]), w_query, w_key, w_value)
    low = iota((FAR_ROWS, LANES), 1) < HEAD_DIM
    for index, value in enumerate(queries + keyvals):
        parts = [value[FAR_ROWS * head : FAR_ROWS * (head + 1)] for head in range(LOCAL_HEADS)]
        chosen = parts[2] if index in (1, 4) else jnp.where(low, parts[0], parts[1])
        for copy in range(FAR_GROUP):
            far[copy, :, tile(index)] = chosen


def project_kernel(tokens, gain, w_query, w_key, w_value, query, keyval, mid):
    mp = lax.axis_index("mp")
    normed = layer_norm(tokens[...].astype(jnp.float32), gain[...])
    order = iota((ROWS, ROWS), 0) == place_of(iota((ROWS, ROWS), 1))
    normed = matmul(order.astype(jnp.bfloat16), normed).astype(jnp.bfloat16)
    queries, keyvals = project(normed, w_query, w_key, w_value)
    for index, value in enumerate(queries):
        query[:, tile(index)] = value
    for index, value in enumerate(keyvals):
        keyval[:, tile(index)] = value
    starts = []
    for head in range(LOCAL_HEADS):
        start = ((mp * LOCAL_HEADS + head) & 3) * CLASS_ROWS
        starts.append(pl.ds(pl.multiple_of(start, CLASS_ROWS), CLASS_ROWS))
    low = iota((CLASS_ROWS, LANES), 1) < HEAD_DIM
    for index in range(2):
        mid[:, tile(index)] = jnp.where(
            low, keyval[starts[0], tile(index)], keyval[starts[1], tile(index)]
        )
    mid[:, tile(2)] = keyval[starts[2], tile(2)]


def attend(query, keys, values, head):
    scores = matmul_t(query, keys)
    peak = jnp.max(scores, -1, keepdims=True)
    weights = jnp.exp(scores - peak).astype(jnp.bfloat16)
    sums = matmul(weights, values)
    lane = iota((sums.shape[0], LANES), 1)
    total = sums[:, LANES + SLIDES : LANES + SLIDES + 1]
    return peak, pack(sums[:, :LANES], peak, total, head, lane)


def pack(sums, peak, total, head, lane):
    return jnp.where(
        lane == SPARE[head], peak, jnp.where(lane == SPARE[head] + 1, total, sums)
    )


def join(held, more, peak, head):
    spare = SPARE[head]
    before = held[:, spare : spare + 1]
    largest = jnp.maximum(before, peak)
    both = held * jnp.exp(before - largest) + more * jnp.exp(peak - largest)
    return jnp.where(iota(both.shape, 1) == spare, largest, both)


def marks_near(seq, ends, steps):
    rows = row_at(iota((ROWS, LANES), 0))
    return jnp.concatenate([key_marks(rows + (seq ^ step) * ROWS, ends) for step in steps], 0)


def near_kernel(tiles, query, own, side, state):
    ends = slide_ends(tiles)
    seq = lax.axis_index("seq")
    marks = query_marks(row_at(iota((ROWS, LANES), 0)) + seq * ROWS, ends)
    keys_marks = marks_near(seq, ends, (0, 2))
    for head in range(LOCAL_HEADS):
        key_tile, value_tile = tile(KEY_TILE[head]), tile(VALUE_TILE[head])
        asked = head_lanes(query[:, tile(QUERY_TILE[head])], head)
        keys = jnp.concatenate([own[:, key_tile], side[:, key_tile]], 0)
        values = jnp.concatenate([own[:, value_tile], side[:, value_tile]], 0)
        _, state[head] = attend(
            jnp.concatenate([asked, marks], 1),
            jnp.concatenate([keys, keys_marks], 1),
            jnp.concatenate([values, keys_marks], 1),
            head,
        )


def rest_kernel(tiles, query, own, side, mid_a, mid_b, swapped, held, state):
    ends = slide_ends(tiles)
    seq, mp = lax.axis_index("seq"), lax.axis_index("mp")
    marks = query_marks(row_at(iota((ROWS, LANES), 0)) + seq * ROWS, ends)
    near_marks = marks_near(seq, ends, (1, 3))
    for head in range(LOCAL_HEADS):
        key_tile, value_tile = tile(KEY_TILE[head]), tile(VALUE_TILE[head])
        asked = head_lanes(query[:, tile(QUERY_TILE[head])], head)
        peak, more = attend(
            jnp.concatenate([asked, marks], 1),
            jnp.concatenate([swapped[: 2 * ROWS, key_tile], near_marks], 1),
            jnp.concatenate([swapped[: 2 * ROWS, value_tile], near_marks], 1),
            head,
        )
        state[head] = join(held[head], more, peak, head)

        offset = (mp * LOCAL_HEADS + head) & 3
        start = pl.multiple_of(offset * CLASS_ROWS, CLASS_ROWS)
        picked = pl.ds(start, CLASS_ROWS)
        place = iota((CLASS_ROWS, LANES), 0)
        class_rows = offset + RATE_MID * ((place >> 4) + ((place & 15) << 3))
        class_marks = jnp.concatenate(
            [key_marks(class_rows + (seq ^ step) * ROWS, ends) for step in (0, 2, 1, 3, 4, 6, 5, 7)],
            0,
        )
        asked = head_lanes(query[picked, tile(QUERY_TILE[head])], head)
        asked = jnp.concatenate([asked, query_marks(class_rows + seq * ROWS, ends)], 1)

        def gathered(lanes):
            return jnp.concatenate(
                [
                    own[picked, lanes],
                    side[picked, lanes],
                    swapped[picked, lanes],
                    swapped[pl.ds(start + ROWS, CLASS_ROWS), lanes],
                    mid_a[:, lanes],
                    mid_b[:, lanes],
                    swapped[2 * ROWS :, lanes],
                ],
                0,
            )

        peak, more = attend(
            asked,
            jnp.concatenate([gathered(key_tile), class_marks], 1),
            jnp.concatenate([gathered(value_tile), class_marks], 1),
            head,
        )
        state[head, picked, :] = join(state[head, picked, :], more, peak, head)


def far_kernel(tiles, rows, here, other, parts):
    ends = slide_ends(tiles)
    seq, mp = lax.axis_index("seq"), lax.axis_index("mp")
    column = seq & 15
    beside = column ^ ((seq >> 4) << 1)
    count = FAR_GROUP * FAR_ROWS
    shape = (count, 2 * count)

    def position(place, holder):
        return ((place >> 4) * 16 + holder) * ROWS + (place & 15) * RATE_FAR

    at = iota(shape, 1)
    holder = jnp.where(at < count, beside, beside ^ 1)
    key_at = position(at & (count - 1), holder)
    query_at = position(iota(shape, 0), column)
    lane = iota((count, LANES), 1)
    for head in range(LOCAL_HEADS):
        number = mp * LOCAL_HEADS + head
        key_tile, value_tile = tile(KEY_TILE[head]), tile(VALUE_TILE[head])
        asked = rows[:, :, tile(QUERY_TILE[head])].reshape(count, LANES)
        asked = head_lanes(asked, head)
        scores = matmul_t(asked, jnp.concatenate([here[:, key_tile], other[:, key_tile]], 0))
        same = slide_of(query_at + number, ends) == slide_of(key_at + number, ends)
        scores = jnp.where(same, scores, HIDDEN_SCORE)
        peak = jnp.max(scores, -1, keepdims=True)
        weights = jnp.exp(scores - peak)
        total = jnp.sum(weights, -1, keepdims=True)
        values = jnp.concatenate([here[:, value_tile], other[:, value_tile]], 0)
        part = matmul(weights.astype(jnp.bfloat16), values)
        part = pack(part, peak, total, head, lane)
        parts[:, :, tile(head)] = part.reshape(FAR_GROUP, FAR_ROWS, LANES)


def finish_kernel(parts, held, w_out, terms, far_out, state):
    mp = lax.axis_index("mp")
    state[...] = held[...]
    far_parts = []
    for head in range(LOCAL_HEADS):
        spare = SPARE[head]
        pieces = [parts[index, :, tile(head)] for index in range(FAR_GROUP)]
        tops = [piece[:, spare : spare + 1] for piece in pieces]
        peak = functools.reduce(jnp.maximum, tops)
        total = jnp.zeros((FAR_ROWS, LANES), jnp.float32)
        for piece, top in zip(pieces, tops):
            total = total + piece * jnp.exp(top - peak)
        far_parts.append(total / total[:, spare + 1 : spare + 2])
        number = mp * LOCAL_HEADS + head
        start = (number & 3) * CLASS_ROWS + (number >> 2) * FAR_ROWS
        picked = pl.ds(pl.multiple_of(start, FAR_ROWS), FAR_ROWS)
        state[head, picked, :] = join(state[head, picked, :], total, peak, head)

    def packed(values):
        first = jnp.where(iota(values[0].shape, 1) < HEAD_DIM, values[0], values[1])
        return first.astype(jnp.bfloat16), values[2].astype(jnp.bfloat16)

    first, last = packed(far_parts)
    far_out[:, :128] = first
    far_out[:, 128:] = last[:, HEAD_DIM:]
    back = (place_of(iota((ROWS, ROWS), 0)) == iota((ROWS, ROWS), 1)).astype(jnp.bfloat16)
    first, last = packed(
        [
            state[head] / state[head, :, SPARE[head] + 1 : SPARE[head] + 2]
            for head in range(LOCAL_HEADS)
        ]
    )
    mixed = jnp.concatenate([first, last[:, HEAD_DIM:]], 1)
    mixed = matmul(back, mixed).astype(jnp.bfloat16)
    terms[...] = matmul(mixed, w_out[...]).astype(jnp.bfloat16).reshape(4, BLOCK, WIDTH)


def weights_kernel(w_up, w_down, out):
    start = pl.multiple_of((lax.axis_index("seq") & 1) * HALF, HALF)
    out[:HALF, :HALF] = w_up[:HALF, pl.ds(start, HALF)]
    out[:HALF, HALF:] = w_up[HALF:, pl.ds(start, HALF)]
    out[HALF:, :] = w_down[pl.ds(start, HALF), :]


def hidden_part(normed, weights):
    raised = matmul(normed[:, :HALF], weights[0, :HALF, :HALF])
    raised = raised + matmul(normed[:, HALF:], weights[0, :HALF, HALF:])
    hidden = (0.5 * raised * (1.0 + lax.erf(raised * 0.7071067811865476))).astype(jnp.bfloat16)
    return matmul(hidden, weights[0, HALF:, :])


def norm_kernel(tokens, terms, gain, attended, normed):
    summed = terms[0].astype(jnp.float32)
    for group in range(1, 4):
        summed = summed + terms[group].astype(jnp.float32)
    summed = summed.astype(jnp.bfloat16)
    attended[...] = summed
    start = pl.multiple_of(lax.axis_index("mp") * BLOCK, BLOCK)
    own = tokens[pl.ds(start, BLOCK), :].astype(jnp.float32)
    normed[...] = layer_norm(own + summed.astype(jnp.float32), gain[...])


def ffn_kernel(own, other, weights, kept, sent, rows, total):
    step = pl.program_id(0)

    @pl.when(step == 0)
    def _():
        rows[:BLOCK, :] = own[...]
        rows[BLOCK:, :] = other[...]
        total[...] = jnp.zeros_like(total)

    total[...] += hidden_part(rows[...], weights)

    @pl.when(step == pl.num_programs(0) - 1)
    def _():
        kept[...] = total[:BLOCK, :]
        sent[...] = total[BLOCK:, :].astype(jnp.bfloat16)


def whole(shape):
    return pl.BlockSpec(shape, lambda step: (0,) * len(shape))


def ffn(own, other, weights):
    outs = [((BLOCK, WIDTH), jnp.float32), ((BLOCK, WIDTH), jnp.bfloat16)]
    return pl.pallas_call(
        ffn_kernel,
        grid=(4,),
        out_shape=[jax.ShapeDtypeStruct(*out) for out in outs],
        in_specs=[whole(own.shape), whole(other.shape)]
        + [pl.BlockSpec((1, 2 * HALF, WIDTH), lambda step: (step, 0, 0))],
        out_specs=[whole(out[0]) for out in outs],
        scratch_shapes=[
            pltpu.VMEM((2 * BLOCK, WIDTH), jnp.bfloat16),
            pltpu.VMEM((2 * BLOCK, WIDTH), jnp.float32),
        ],
        cost_estimate=pl.CostEstimate(
            flops=int(4e9), bytes_accessed=int(5e6), transcendentals=0
        ),
        compiler_params=pltpu.CompilerParams(vmem_limit_bytes=VMEM),
    )(own, other, weights)


def call(kernel, micros, outs, ins, scratch=()):
    places = {"smem": pltpu.SMEM, "vmem": pltpu.VMEM}
    return pl.pallas_call(
        kernel,
        out_shape=[jax.ShapeDtypeStruct(*out) for out in outs],
        in_specs=[pl.BlockSpec(memory_space=places[where]) for _, where in ins],
        out_specs=[pl.BlockSpec(memory_space=pltpu.VMEM) for _ in outs],
        scratch_shapes=list(scratch),
        cost_estimate=pl.CostEstimate(
            flops=int(micros * 1.1e9), bytes_accessed=int(micros * 1e6), transcendentals=0
        ),
        compiler_params=pltpu.CompilerParams(vmem_limit_bytes=VMEM),
    )(*[array for array, _ in ins])


def swap(value, step):
    return lax.ppermute(value, "seq", [(i, i ^ step) for i in range(lax.axis_size("seq"))])


def local(tokens, slide_tiles, attn_gain, w_query, w_key, w_value, w_out, ffn_gain, w_up, w_down):
    bf16, f32 = jnp.bfloat16, jnp.float32
    v, s = "vmem", "smem"
    columns = [[16 * z + place for z in range(FAR_GROUP)] for place in range(16)]
    across = [
        (16 * z + (place ^ (2 * z)), 16 * z + place) for z in range(FAR_GROUP) for place in range(16)
    ]
    (packed,) = call(weights_kernel, 2, [((2 * HALF, WIDTH), bf16)], [(w_up, v), (w_down, v)])
    mine = lax.all_gather(packed, "mp", axis=0)
    w_query, w_key, w_value = w_query.T, w_key.T, w_value.T
    (far,) = call(
        far_rows_kernel,
        2,
        [((FAR_GROUP, FAR_ROWS, 640), bf16)],
        [(tokens, v), (attn_gain, v), (w_query, v), (w_key, v), (w_value, v)],
    )
    ordered, _ = lax.optimization_barrier((tokens, far))
    query, own, mid = call(
        project_kernel,
        3,
        [((ROWS, 256), bf16), ((ROWS, 384), bf16), ((CLASS_ROWS, 384), bf16)],
        [(ordered, v), (attn_gain, v), (w_query, v), (w_key, v), (w_value, v)],
    )
    side = swap(own, 2)
    mid_a, mid_b = swap(mid, 4), swap(mid, 6)
    far_rows = lax.all_to_all(
        far, "seq", split_axis=0, concat_axis=0, tiled=True, axis_index_groups=columns
    )
    far_keys = far_rows[:, :, 256:].reshape(128, 384)
    side, mid_a, mid_b, _ = lax.optimization_barrier((side, mid_a, mid_b, far_keys))
    far_here = lax.ppermute(far_keys, "seq", across)
    swapped = swap(jnp.concatenate([own, side, mid_a, mid_b], 0), 1)
    state = ((LOCAL_HEADS, ROWS, LANES), f32)
    asked, _ = lax.optimization_barrier((query, far_rows))
    (near,) = call(
        near_kernel, 3, [state], [(slide_tiles, s), (asked, v), (own, v), (side, v)]
    )
    far_here, _ = lax.optimization_barrier((far_here, near))
    far_other = swap(far_here, 1)
    (parts,) = call(
        far_kernel,
        2,
        [((FAR_GROUP, FAR_ROWS, 384), f32)],
        [(slide_tiles, s), (far_rows, v), (far_here, v), (far_other, v)],
    )
    near, _ = lax.optimization_barrier((near, parts))
    (both,) = call(
        rest_kernel,
        5,
        [state],
        [
            (slide_tiles, s), (query, v), (own, v), (side, v), (mid_a, v), (mid_b, v), (swapped, v),
            (near, v),
        ],
    )
    parts = lax.all_to_all(
        parts, "seq", split_axis=0, concat_axis=0, tiled=True, axis_index_groups=columns
    )
    mine, _ = lax.optimization_barrier((mine, parts))
    terms, far_attended = call(
        finish_kernel,
        3,
        [((4, BLOCK, WIDTH), bf16), ((FAR_ROWS, 192), bf16)],
        [(parts, v), (both, v), (w_out, v)],
        [pltpu.VMEM(*state)],
    )
    terms = lax.all_to_all(terms, "mp", split_axis=0, concat_axis=0, tiled=True)
    attended, normed = call(
        norm_kernel,
        1,
        [((BLOCK, WIDTH), bf16), ((BLOCK, WIDTH), bf16)],
        [(tokens, v), (terms, v), (ffn_gain, v)],
    )
    kept, sent = ffn(normed, swap(normed, 1), mine)
    ffn_out = (kept + swap(sent, 1).astype(f32)).astype(bf16)
    return (attended, far_attended, ffn_out)


def solution(mesh):
    return jax.shard_map(
        local,
        mesh=mesh,
        in_specs=(
            P("seq", None),
            P(),
            P(),
            P(None, "mp"),
            P(None, "mp"),
            P(None, "mp"),
            P("mp", None),
            P(),
            P(None, "mp"),
            P("mp", None),
        ),
        out_specs=(P(("seq", "mp"), None), P("seq", "mp"), P(("seq", "mp"), None)),
        check_vma=False,
    )
```

```python
import functools

import jax
import jax.numpy as jnp
from jax import lax
from jax.experimental import pallas as pl
from jax.experimental.pallas import tpu as pltpu
from jax.sharding import PartitionSpec as P

HEAD_DIM = 64
LOCAL_HEADS = 3
RATE_MID = 4
RATE_FAR = 32
ROWS = 512
CLASS_ROWS = ROWS // RATE_MID
FAR_ROWS = ROWS // RATE_FAR
LANES = 128
SLIDES = 4
WIDTH = 768
HALF = WIDTH // 2
BLOCK = 128
EPS = 1e-05
HIDDEN_SCORE = -1e30
VMEM = 16 * 1024 * 1024

KEY_TILE = (0, 0, 2)
VALUE_TILE = (1, 1, 2)
QUERY_TILE = (0, 0, 1)
SPARE = (64, 0, 0)
FAR_GROUP = 8


def iota(shape, dim):
    return lax.broadcasted_iota(jnp.int32, shape, dim)


def place_of(row):
    return (row & 3) * CLASS_ROWS + ((row >> 2) & 7) * FAR_ROWS + (row >> 5)


def row_at(place):
    return (place & 15) * RATE_FAR + ((place >> 4) & 7) * RATE_MID + (place >> 7)


def layer_norm(as_float, gain):
    mean_val = jnp.mean(as_float, -1, keepdims=True)
    centered = as_float - mean_val
    variance = jnp.mean(centered * centered, -1, keepdims=True)
    return (centered * lax.rsqrt(variance + EPS) * gain.astype(jnp.float32)).astype(jnp.bfloat16)


def matmul(left, right):
    return jnp.dot(left, right, preferred_element_type=jnp.float32)


def matmul_t(left, right):
    return lax.dot_general(
        left, right, (((1,), (1,)), ((), ())), preferred_element_type=jnp.float32
    )


def slide_of(positions, ends):
    index = (positions >= ends[0]).astype(jnp.int32)
    for end in ends[1:]:
        index = index + (positions >= end).astype(jnp.int32)
    return index


def slide_ends(tiles_ref):
    ends = [tiles_ref[0]]
    for slide in range(1, SLIDES - 1):
        ends.append(ends[-1] + tiles_ref[slide])
    return ends


def query_marks(positions, ends):
    rows = positions.shape[0]
    lane = iota((rows, LANES), 1)
    return (lane == slide_of(positions, ends)).astype(jnp.bfloat16)


def key_marks(positions, ends):
    rows = positions.shape[0]
    lane = iota((rows, LANES), 1)
    hide = (lane < SLIDES) & (lane != slide_of(positions, ends))
    marks = jnp.where(hide, HIDDEN_SCORE, jnp.where(lane == SLIDES, 1.0, 0.0))
    return marks.astype(jnp.bfloat16)


def head_lanes(value, head):
    lane = iota(value.shape, 1)
    keep = lane < HEAD_DIM if head != 1 else lane >= HEAD_DIM
    return jnp.where(keep, value, jnp.zeros_like(value))


def tile(index):
    return slice(index * LANES, (index + 1) * LANES)


def project(normed, w_query, w_key, w_value):
    asked = (matmul_t(normed, w_query[...]) * (1.0 / 8.0)).astype(jnp.bfloat16)
    key = matmul_t(normed, w_key[...]).astype(jnp.bfloat16)
    value = matmul_t(normed, w_value[...]).astype(jnp.bfloat16)
    none = jnp.zeros_like(asked[:, 128:])
    queries = [asked[:, :128], jnp.concatenate([asked[:, 128:], none], 1)]
    keyvals = [key[:, :128], value[:, :128]]
    return queries, keyvals + [jnp.concatenate([key[:, 128:], value[:, 128:]], 1)]


def far_rows_kernel(tokens, gain, w_query, w_key, w_value, far):
    first = lax.axis_index("mp") * LOCAL_HEADS
    shape = (LOCAL_HEADS * FAR_ROWS, ROWS)
    place = iota(shape, 0)
    wanted = (place & 15) * RATE_FAR + (place >> 4) + first
    rows = matmul((iota(shape, 1) == wanted).astype(jnp.bfloat16), tokens[...])
    queries, keyvals = project(layer_norm(rows, gain[...]), w_query, w_key, w_value)
    low = iota((FAR_ROWS, LANES), 1) < HEAD_DIM
    for index, value in enumerate(queries + keyvals):
        parts = [value[FAR_ROWS * head : FAR_ROWS * (head + 1)] for head in range(LOCAL_HEADS)]
        chosen = parts[2] if index in (1, 4) else jnp.where(low, parts[0], parts[1])
        for copy in range(FAR_GROUP):
            far[copy, :, tile(index)] = chosen


def project_kernel(tokens, gain, w_query, w_key, w_value, query, keyval, mid):
    mp = lax.axis_index("mp")
    normed = layer_norm(tokens[...].astype(jnp.float32), gain[...])
    order = iota((ROWS, ROWS), 0) == place_of(iota((ROWS, ROWS), 1))
    normed = matmul(order.astype(jnp.bfloat16), normed).astype(jnp.bfloat16)
    queries, keyvals = project(normed, w_query, w_key, w_value)
    for index, value in enumerate(queries):
        query[:, tile(index)] = value
    for index, value in enumerate(keyvals):
        keyval[:, tile(index)] = value
    starts = []
    for head in range(LOCAL_HEADS):
        start = ((mp * LOCAL_HEADS + head) & 3) * CLASS_ROWS
        starts.append(pl.ds(pl.multiple_of(start, CLASS_ROWS), CLASS_ROWS))
    low = iota((CLASS_ROWS, LANES), 1) < HEAD_DIM
    for index in range(2):
        mid[:, tile(index)] = jnp.where(
            low, keyval[starts[0], tile(index)], keyval[starts[1], tile(index)]
        )
    mid[:, tile(2)] = keyval[starts[2], tile(2)]


def attend(query, keys, values, head):
    scores = matmul_t(query, keys)
    peak = jnp.max(scores, -1, keepdims=True)
    weights = jnp.exp(scores - peak).astype(jnp.bfloat16)
    sums = matmul(weights, values)
    lane = iota((sums.shape[0], LANES), 1)
    total = sums[:, LANES + SLIDES : LANES + SLIDES + 1]
    return peak, pack(sums[:, :LANES], peak, total, head, lane)


def pack(sums, peak, total, head, lane):
    return jnp.where(
        lane == SPARE[head], peak, jnp.where(lane == SPARE[head] + 1, total, sums)
    )


def join(held, more, peak, head):
    spare = SPARE[head]
    before = held[:, spare : spare + 1]
    largest = jnp.maximum(before, peak)
    both = held * jnp.exp(before - largest) + more * jnp.exp(peak - largest)
    return jnp.where(iota(both.shape, 1) == spare, largest, both)


def marks_near(seq, ends, steps):
    rows = row_at(iota((ROWS, LANES), 0))
    return jnp.concatenate([key_marks(rows + (seq ^ step) * ROWS, ends) for step in steps], 0)


def near_kernel(tiles, query, own, side, *state):
    ends = slide_ends(tiles)
    seq = lax.axis_index("seq")
    marks = query_marks(row_at(iota((ROWS, LANES), 0)) + seq * ROWS, ends)
    keys_marks = marks_near(seq, ends, (0, 2))
    for head in range(LOCAL_HEADS):
        key_tile, value_tile = tile(KEY_TILE[head]), tile(VALUE_TILE[head])
        asked = head_lanes(query[:, tile(QUERY_TILE[head])], head)
        keys = jnp.concatenate([own[:, key_tile], side[:, key_tile]], 0)
        values = jnp.concatenate([own[:, value_tile], side[:, value_tile]], 0)
        _, state[head][...] = attend(
            jnp.concatenate([asked, marks], 1),
            jnp.concatenate([keys, keys_marks], 1),
            jnp.concatenate([values, keys_marks], 1),
            head,
        )


def rest_kernel(tiles, query, own, side, mid_a, mid_b, swapped, *refs):
    held, state = refs[:LOCAL_HEADS], refs[LOCAL_HEADS:]
    ends = slide_ends(tiles)
    seq, mp = lax.axis_index("seq"), lax.axis_index("mp")
    marks = query_marks(row_at(iota((ROWS, LANES), 0)) + seq * ROWS, ends)
    near_marks = marks_near(seq, ends, (1, 3))
    for head in range(LOCAL_HEADS):
        key_tile, value_tile = tile(KEY_TILE[head]), tile(VALUE_TILE[head])
        asked = head_lanes(query[:, tile(QUERY_TILE[head])], head)
        peak, more = attend(
            jnp.concatenate([asked, marks], 1),
            jnp.concatenate([swapped[: 2 * ROWS, key_tile], near_marks], 1),
            jnp.concatenate([swapped[: 2 * ROWS, value_tile], near_marks], 1),
            head,
        )
        state[head][...] = join(held[head][...], more, peak, head)

        offset = (mp * LOCAL_HEADS + head) & 3
        start = pl.multiple_of(offset * CLASS_ROWS, CLASS_ROWS)
        picked = pl.ds(start, CLASS_ROWS)
        place = iota((CLASS_ROWS, LANES), 0)
        class_rows = offset + RATE_MID * ((place >> 4) + ((place & 15) << 3))
        class_marks = jnp.concatenate(
            [key_marks(class_rows + (seq ^ step) * ROWS, ends) for step in (0, 2, 1, 3, 4, 6, 5, 7)],
            0,
        )
        asked = head_lanes(query[picked, tile(QUERY_TILE[head])], head)
        asked = jnp.concatenate([asked, query_marks(class_rows + seq * ROWS, ends)], 1)

        def gathered(lanes):
            return jnp.concatenate(
                [
                    own[picked, lanes],
                    side[picked, lanes],
                    swapped[picked, lanes],
                    swapped[pl.ds(start + ROWS, CLASS_ROWS), lanes],
                    mid_a[:, lanes],
                    mid_b[:, lanes],
                    swapped[2 * ROWS :, lanes],
                ],
                0,
            )

        peak, more = attend(
            asked,
            jnp.concatenate([gathered(key_tile), class_marks], 1),
            jnp.concatenate([gathered(value_tile), class_marks], 1),
            head,
        )
        state[head][picked, :] = join(state[head][picked, :], more, peak, head)


def far_kernel(tiles, rows, here, other, parts):
    ends = slide_ends(tiles)
    seq, mp = lax.axis_index("seq"), lax.axis_index("mp")
    column = seq & 15
    beside = column ^ ((seq >> 4) << 1)
    count = FAR_GROUP * FAR_ROWS
    shape = (count, 2 * count)

    def position(place, holder):
        return ((place >> 4) * 16 + holder) * ROWS + (place & 15) * RATE_FAR

    at = iota(shape, 1)
    holder = jnp.where(at < count, beside, beside ^ 1)
    key_at = position(at & (count - 1), holder)
    query_at = position(iota(shape, 0), column)
    lane = iota((count, LANES), 1)
    for head in range(LOCAL_HEADS):
        number = mp * LOCAL_HEADS + head
        key_tile, value_tile = tile(KEY_TILE[head]), tile(VALUE_TILE[head])
        asked = rows[:, :, tile(QUERY_TILE[head])].reshape(count, LANES)
        asked = head_lanes(asked, head)
        scores = matmul_t(asked, jnp.concatenate([here[:, key_tile], other[:, key_tile]], 0))
        same = slide_of(query_at + number, ends) == slide_of(key_at + number, ends)
        scores = jnp.where(same, scores, HIDDEN_SCORE)
        peak = jnp.max(scores, -1, keepdims=True)
        weights = jnp.exp(scores - peak)
        total = jnp.sum(weights, -1, keepdims=True)
        values = jnp.concatenate([here[:, value_tile], other[:, value_tile]], 0)
        part = matmul(weights.astype(jnp.bfloat16), values)
        part = pack(part, peak, total, head, lane)
        parts[:, :, tile(head)] = part.reshape(FAR_GROUP, FAR_ROWS, LANES)


def finish_kernel(parts, w_out, *refs):
    held, (terms, far_out), state = refs[:LOCAL_HEADS], refs[LOCAL_HEADS:-LOCAL_HEADS], refs[-LOCAL_HEADS:]
    mp = lax.axis_index("mp")
    far_parts = []
    for head in range(LOCAL_HEADS):
        spare = SPARE[head]
        pieces = [parts[index, :, tile(head)] for index in range(FAR_GROUP)]
        tops = [piece[:, spare : spare + 1] for piece in pieces]
        peak = functools.reduce(jnp.maximum, tops)
        total = jnp.zeros((FAR_ROWS, LANES), jnp.float32)
        for piece, top in zip(pieces, tops):
            total = total + piece * jnp.exp(top - peak)
        far_parts.append(total / total[:, spare + 1 : spare + 2])
        number = mp * LOCAL_HEADS + head
        start = (number & 3) * CLASS_ROWS + (number >> 2) * FAR_ROWS
        picked = pl.ds(pl.multiple_of(start, FAR_ROWS), FAR_ROWS)
        state[head][...] = held[head][...]
        state[head][picked, :] = join(state[head][picked, :], total, peak, head)

    def packed(values):
        first = jnp.where(iota(values[0].shape, 1) < HEAD_DIM, values[0], values[1])
        return first.astype(jnp.bfloat16), values[2].astype(jnp.bfloat16)

    first, last = packed(far_parts)
    far_out[:, :128] = first
    far_out[:, 128:] = last[:, HEAD_DIM:]
    back = (place_of(iota((ROWS, ROWS), 0)) == iota((ROWS, ROWS), 1)).astype(jnp.bfloat16)
    first, last = packed(
        [
            state[head][...] / state[head][:, SPARE[head] + 1 : SPARE[head] + 2]
            for head in range(LOCAL_HEADS)
        ]
    )
    mixed = jnp.concatenate([first, last[:, HEAD_DIM:]], 1)
    mixed = matmul(back, mixed).astype(jnp.bfloat16)
    terms[...] = matmul(mixed, w_out[...]).astype(jnp.bfloat16).reshape(4, BLOCK, WIDTH)


def weights_kernel(w_up, w_down, out):
    start = pl.multiple_of((lax.axis_index("seq") & 1) * HALF, HALF)
    out[:HALF, :HALF] = w_up[:HALF, pl.ds(start, HALF)]
    out[:HALF, HALF:] = w_up[HALF:, pl.ds(start, HALF)]
    out[HALF:, :] = w_down[pl.ds(start, HALF), :]


def hidden_part(normed, weights):
    raised = matmul(normed[:, :HALF], weights[0, :HALF, :HALF])
    raised = raised + matmul(normed[:, HALF:], weights[0, :HALF, HALF:])
    hidden = (0.5 * raised * (1.0 + lax.erf(raised * 0.7071067811865476))).astype(jnp.bfloat16)
    return matmul(hidden, weights[0, HALF:, :])


def norm_kernel(tokens, terms, gain, attended, normed):
    summed = terms[0].astype(jnp.float32)
    for group in range(1, 4):
        summed = summed + terms[group].astype(jnp.float32)
    summed = summed.astype(jnp.bfloat16)
    attended[...] = summed
    start = pl.multiple_of(lax.axis_index("mp") * BLOCK, BLOCK)
    own = tokens[pl.ds(start, BLOCK), :].astype(jnp.float32)
    normed[...] = layer_norm(own + summed.astype(jnp.float32), gain[...])


def ffn_kernel(own, other, weights, kept, sent, rows, total):
    step = pl.program_id(0)

    @pl.when(step == 0)
    def _():
        rows[:BLOCK, :] = own[...]
        rows[BLOCK:, :] = other[...]
        total[...] = jnp.zeros_like(total)

    total[...] += hidden_part(rows[...], weights)

    @pl.when(step == pl.num_programs(0) - 1)
    def _():
        kept[...] = total[:BLOCK, :]
        sent[...] = total[BLOCK:, :].astype(jnp.bfloat16)


def whole(shape):
    return pl.BlockSpec(shape, lambda step: (0,) * len(shape))


def ffn(own, other, weights):
    outs = [((BLOCK, WIDTH), jnp.float32), ((BLOCK, WIDTH), jnp.bfloat16)]
    return pl.pallas_call(
        ffn_kernel,
        grid=(4,),
        out_shape=[jax.ShapeDtypeStruct(*out) for out in outs],
        in_specs=[whole(own.shape), whole(other.shape)]
        + [pl.BlockSpec((1, 2 * HALF, WIDTH), lambda step: (step, 0, 0))],
        out_specs=[whole(out[0]) for out in outs],
        scratch_shapes=[
            pltpu.VMEM((2 * BLOCK, WIDTH), jnp.bfloat16),
            pltpu.VMEM((2 * BLOCK, WIDTH), jnp.float32),
        ],
        cost_estimate=pl.CostEstimate(
            flops=int(4e9), bytes_accessed=int(5e6), transcendentals=0
        ),
        compiler_params=pltpu.CompilerParams(vmem_limit_bytes=56 * 1024 * 1024),
    )(own, other, weights)


def call(kernel, micros, outs, ins, scratch=()):
    places = {"smem": pltpu.SMEM, "vmem": pltpu.VMEM}
    return pl.pallas_call(
        kernel,
        out_shape=[jax.ShapeDtypeStruct(*out) for out in outs],
        in_specs=[pl.BlockSpec(memory_space=places[where]) for _, where in ins],
        out_specs=[pl.BlockSpec(memory_space=pltpu.VMEM) for _ in outs],
        scratch_shapes=list(scratch),
        cost_estimate=pl.CostEstimate(
            flops=int(micros * 1.1e9), bytes_accessed=int(micros * 1e6), transcendentals=0
        ),
        compiler_params=pltpu.CompilerParams(vmem_limit_bytes=VMEM),
    )(*[array for array, _ in ins])


def swap(value, step):
    return lax.ppermute(value, "seq", [(i, i ^ step) for i in range(lax.axis_size("seq"))])


def local(tokens, slide_tiles, attn_gain, w_query, w_key, w_value, w_out, ffn_gain, w_up, w_down):
    bf16, f32 = jnp.bfloat16, jnp.float32
    v, s = "vmem", "smem"
    columns = [[16 * z + place for z in range(FAR_GROUP)] for place in range(16)]
    across = [
        (16 * z + (place ^ (2 * z)), 16 * z + place) for z in range(FAR_GROUP) for place in range(16)
    ]
    w_query, w_key, w_value = w_query.T, w_key.T, w_value.T
    (far,) = call(
        far_rows_kernel,
        2,
        [((FAR_GROUP, FAR_ROWS, 640), bf16)],
        [(tokens, v), (attn_gain, v), (w_query, v), (w_key, v), (w_value, v)],
    )
    far_rows = lax.all_to_all(
        far, "seq", split_axis=0, concat_axis=0, tiled=True, axis_index_groups=columns
    )
    tokens, w_up, w_down, _ = lax.optimization_barrier((tokens, w_up, w_down, far))
    query, own, mid = call(
        project_kernel,
        2,
        [((ROWS, 256), bf16), ((ROWS, 384), bf16), ((CLASS_ROWS, 384), bf16)],
        [(tokens, v), (attn_gain, v), (w_query, v), (w_key, v), (w_value, v)],
    )
    (packed,) = call(weights_kernel, 2, [((2 * HALF, WIDTH), bf16)], [(w_up, v), (w_down, v)])
    mine = lax.all_gather(packed, "mp", axis=0)
    side = swap(own, 2)

    far_keys = far_rows[:, :, 256:].reshape(128, 384)
    far_here = lax.ppermute(far_keys, "seq", across)
    query, _ = lax.optimization_barrier((query, far_keys))
    mid_a, mid_b = swap(mid, 4), swap(mid, 6)
    state = [((ROWS, LANES), f32)] * LOCAL_HEADS
    near = call(near_kernel, 3, state, [(slide_tiles, s), (query, v), (own, v), (side, v)])
    side, mid_a, mid_b, far_here, *near = lax.optimization_barrier(
        (side, mid_a, mid_b, far_here, *near)
    )
    far_other = swap(far_here, 1)
    swapped = swap(jnp.concatenate([own, side, mid_a, mid_b], 0), 1)
    (parts,) = call(
        far_kernel,
        2,
        [((FAR_GROUP, FAR_ROWS, 384), f32)],
        [(slide_tiles, s), (far_rows, v), (far_here, v), (far_other, v)],
    )
    parts, *near = lax.optimization_barrier((parts, *near))
    both = call(
        rest_kernel,
        5,
        state,
        [
            (slide_tiles, s), (query, v), (own, v), (side, v), (mid_a, v), (mid_b, v), (swapped, v),
            *[(held, v) for held in near],
        ],
    )
    parts = lax.all_to_all(
        parts, "seq", split_axis=0, concat_axis=0, tiled=True, axis_index_groups=columns
    )
    mine, _ = lax.optimization_barrier((mine, parts))
    terms, far_attended = call(
        finish_kernel,
        3,
        [((4, BLOCK, WIDTH), bf16), ((FAR_ROWS, 192), bf16)],
        [(parts, v), (w_out, v), *[(held, v) for held in both]],
        [pltpu.VMEM(*shape) for shape in state],
    )
    terms = lax.all_to_all(terms, "mp", split_axis=0, concat_axis=0, tiled=True)
    attended, normed = call(
        norm_kernel,
        1,
        [((BLOCK, WIDTH), bf16), ((BLOCK, WIDTH), bf16)],
        [(tokens, v), (terms, v), (ffn_gain, v)],
    )
    kept, sent = ffn(normed, swap(normed, 1), mine)
    ffn_out = (kept + swap(sent, 1).astype(f32)).astype(bf16)
    return (attended, far_attended, ffn_out)


def solution(mesh):
    return jax.shard_map(
        local,
        mesh=mesh,
        in_specs=(
            P("seq", None),
            P(),
            P(),
            P(None, "mp"),
            P(None, "mp"),
            P(None, "mp"),
            P("mp", None),
            P(),
            P(None, "mp"),
            P("mp", None),
        ),
        out_specs=(P(("seq", "mp"), None), P("seq", "mp"), P(("seq", "mp"), None)),
        check_vma=False,
    )
```

```python
import functools

import jax
import jax.numpy as jnp
from jax import lax
from jax.experimental import pallas as pl
from jax.experimental.pallas import tpu as pltpu
from jax.sharding import PartitionSpec as P

HEAD_DIM = 64
LOCAL_HEADS = 3
RATE_MID = 4
RATE_FAR = 32
ROWS = 512
CLASS_ROWS = ROWS // RATE_MID
FAR_ROWS = ROWS // RATE_FAR
LANES = 128
SLIDES = 4
WIDTH = 768
HALF = WIDTH // 2
BLOCK = 128
EPS = 1e-05
HIDDEN_SCORE = -1e30
VMEM = 16 * 1024 * 1024
WHOLE_VMEM = 58 * 1024 * 1024

KEY_TILE = (0, 0, 2)
VALUE_TILE = (1, 1, 2)
QUERY_TILE = (0, 0, 1)
SPARE = (64, 0, 0)
FAR_GROUP = 8


def iota(shape, dim):
    return lax.broadcasted_iota(jnp.int32, shape, dim)


def place_of(row):
    return (row & 3) * CLASS_ROWS + ((row >> 2) & 7) * FAR_ROWS + (row >> 5)


def row_at(place):
    return (place & 15) * RATE_FAR + ((place >> 4) & 7) * RATE_MID + (place >> 7)


def layer_norm(as_float, gain):
    mean_val = jnp.mean(as_float, -1, keepdims=True)
    centered = as_float - mean_val
    variance = jnp.mean(centered * centered, -1, keepdims=True)
    return (centered * lax.rsqrt(variance + EPS) * gain.astype(jnp.float32)).astype(jnp.bfloat16)


def matmul(left, right):
    return jnp.dot(left, right, preferred_element_type=jnp.float32)


def matmul_t(left, right):
    return lax.dot_general(
        left, right, (((1,), (1,)), ((), ())), preferred_element_type=jnp.float32
    )


def slide_of(positions, ends):
    index = (positions >= ends[0]).astype(jnp.int32)
    for end in ends[1:]:
        index = index + (positions >= end).astype(jnp.int32)
    return index


def slide_ends(tiles_ref):
    ends = [tiles_ref[0]]
    for slide in range(1, SLIDES - 1):
        ends.append(ends[-1] + tiles_ref[slide])
    return ends


def query_marks(positions, ends):
    rows = positions.shape[0]
    lane = iota((rows, LANES), 1)
    return (lane == slide_of(positions, ends)).astype(jnp.bfloat16)


def key_marks(positions, ends):
    rows = positions.shape[0]
    lane = iota((rows, LANES), 1)
    hide = (lane < SLIDES) & (lane != slide_of(positions, ends))
    marks = jnp.where(hide, HIDDEN_SCORE, jnp.where(lane == SLIDES, 1.0, 0.0))
    return marks.astype(jnp.bfloat16)


def head_lanes(value, head):
    lane = iota(value.shape, 1)
    keep = lane < HEAD_DIM if head != 1 else lane >= HEAD_DIM
    return jnp.where(keep, value, jnp.zeros_like(value))


def tile(index):
    return slice(index * LANES, (index + 1) * LANES)


def project(normed, w_query, w_key, w_value):
    asked = (matmul_t(normed, w_query[...]) * (1.0 / 8.0)).astype(jnp.bfloat16)
    key = matmul_t(normed, w_key[...]).astype(jnp.bfloat16)
    value = matmul_t(normed, w_value[...]).astype(jnp.bfloat16)
    none = jnp.zeros_like(asked[:, 128:])
    queries = [asked[:, :128], jnp.concatenate([asked[:, 128:], none], 1)]
    keyvals = [key[:, :128], value[:, :128]]
    return queries, keyvals + [jnp.concatenate([key[:, 128:], value[:, 128:]], 1)]


def project_kernel(
    tokens, gain, w_query, w_key, w_value, query, keyval, mid, far, rows, weights, sems
):
    mp = lax.axis_index("mp")
    copies = []
    for index in range(4):
        part = pl.ds(index * BLOCK, BLOCK)
        copies.append(pltpu.make_async_copy(tokens.at[part], rows.at[part], sems.at[index]))
    for index, weight in enumerate((w_query, w_key, w_value)):
        copies.append(pltpu.make_async_copy(weight, weights.at[index], sems.at[4 + index]))
    for copy in copies:
        copy.start()
    for copy in copies[:4]:
        copy.wait()
    normed = layer_norm(rows[...].astype(jnp.float32), gain[...])
    order = iota((ROWS, ROWS), 0) == place_of(iota((ROWS, ROWS), 1))
    normed = matmul(order.astype(jnp.bfloat16), normed).astype(jnp.bfloat16)
    for copy in copies[4:]:
        copy.wait()
    queries, keyvals = project(normed, *[weights.at[index] for index in range(3)])
    for index, value in enumerate(queries):
        query[:, tile(index)] = value
    for index, value in enumerate(keyvals):
        keyval[:, tile(index)] = value

    def pick(source, index, whose, count):
        starts = []
        for head in range(LOCAL_HEADS):
            number = mp * LOCAL_HEADS + head
            start = (number & 3) * CLASS_ROWS
            if count == FAR_ROWS:
                start = start + (number >> 2) * FAR_ROWS
            starts.append(pl.ds(pl.multiple_of(start, count), count))
        if whose[2] == index:
            return source[starts[2], tile(index)]
        low, high = source[starts[0], tile(index)], source[starts[1], tile(index)]
        return jnp.where(iota(low.shape, 1) < HEAD_DIM, low, high)

    for index in range(3):
        mid[:, tile(index)] = pick(keyval, index, KEY_TILE, CLASS_ROWS)
    picked = [pick(query, index, QUERY_TILE, FAR_ROWS) for index in range(2)]
    picked += [pick(keyval, index, KEY_TILE, FAR_ROWS) for index in range(3)]
    for index, value in enumerate(picked):
        for copy in range(FAR_GROUP):
            far[copy, :, tile(index)] = value


def attend(query, keys, values, head):
    scores = matmul_t(query, keys)
    peak = jnp.max(scores, -1, keepdims=True)
    weights = jnp.exp(scores - peak).astype(jnp.bfloat16)
    sums = matmul(weights, values)
    lane = iota((sums.shape[0], LANES), 1)
    total = sums[:, LANES + SLIDES : LANES + SLIDES + 1]
    return peak, pack(sums[:, :LANES], peak, total, head, lane)


def pack(sums, peak, total, head, lane):
    return jnp.where(
        lane == SPARE[head], peak, jnp.where(lane == SPARE[head] + 1, total, sums)
    )


def join(held, more, peak, head):
    spare = SPARE[head]
    before = held[:, spare : spare + 1]
    largest = jnp.maximum(before, peak)
    both = held * jnp.exp(before - largest) + more * jnp.exp(peak - largest)
    return jnp.where(iota(both.shape, 1) == spare, largest, both)


def marks_near(seq, ends, steps):
    rows = row_at(iota((ROWS, LANES), 0))
    return jnp.concatenate([key_marks(rows + (seq ^ step) * ROWS, ends) for step in steps], 0)


def near_kernel(tiles, query, own, side, *refs):
    out, state, sems = refs[:LOCAL_HEADS], refs[LOCAL_HEADS:-1], refs[-1]
    copies = [
        pltpu.make_async_copy(state[head], out[head], sems.at[head]) for head in range(LOCAL_HEADS)
    ]
    ends = slide_ends(tiles)
    seq = lax.axis_index("seq")
    marks = query_marks(row_at(iota((ROWS, LANES), 0)) + seq * ROWS, ends)
    keys_marks = marks_near(seq, ends, (0, 2))
    for head in range(LOCAL_HEADS):
        key_tile, value_tile = tile(KEY_TILE[head]), tile(VALUE_TILE[head])
        asked = head_lanes(query[:, tile(QUERY_TILE[head])], head)
        keys = jnp.concatenate([own[:, key_tile], side[:, key_tile]], 0)
        values = jnp.concatenate([own[:, value_tile], side[:, value_tile]], 0)
        _, state[head][...] = attend(
            jnp.concatenate([asked, marks], 1),
            jnp.concatenate([keys, keys_marks], 1),
            jnp.concatenate([values, keys_marks], 1),
            head,
        )
        copies[head].start()
    for copy in copies:
        copy.wait()


def rest_kernel(tiles, query, own, side, mid_a, mid_b, swapped, *refs):
    n = LOCAL_HEADS
    held_from, out, held, state, sems = refs[:n], refs[n : 2 * n], refs[2 * n : 3 * n], refs[3 * n : -1], refs[-1]
    fetches = [pltpu.make_async_copy(held_from[i], held[i], sems.at[i]) for i in range(n)]
    copies = [pltpu.make_async_copy(state[i], out[i], sems.at[n + i]) for i in range(n)]
    for fetch in fetches:
        fetch.start()
    ends = slide_ends(tiles)
    seq, mp = lax.axis_index("seq"), lax.axis_index("mp")
    marks = query_marks(row_at(iota((ROWS, LANES), 0)) + seq * ROWS, ends)
    near_marks = marks_near(seq, ends, (1, 3))
    for head in range(LOCAL_HEADS):
        key_tile, value_tile = tile(KEY_TILE[head]), tile(VALUE_TILE[head])
        asked = head_lanes(query[:, tile(QUERY_TILE[head])], head)
        peak, more = attend(
            jnp.concatenate([asked, marks], 1),
            jnp.concatenate([swapped[: 2 * ROWS, key_tile], near_marks], 1),
            jnp.concatenate([swapped[: 2 * ROWS, value_tile], near_marks], 1),
            head,
        )
        fetches[head].wait()
        state[head][...] = join(held[head][...], more, peak, head)

        offset = (mp * LOCAL_HEADS + head) & 3
        start = pl.multiple_of(offset * CLASS_ROWS, CLASS_ROWS)
        picked = pl.ds(start, CLASS_ROWS)
        place = iota((CLASS_ROWS, LANES), 0)
        class_rows = offset + RATE_MID * ((place >> 4) + ((place & 15) << 3))
        class_marks = jnp.concatenate(
            [key_marks(class_rows + (seq ^ step) * ROWS, ends) for step in (0, 2, 1, 3, 4, 6, 5, 7)],
            0,
        )
        asked = head_lanes(query[picked, tile(QUERY_TILE[head])], head)
        asked = jnp.concatenate([asked, query_marks(class_rows + seq * ROWS, ends)], 1)

        def gathered(lanes):
            return jnp.concatenate(
                [
                    own[picked, lanes],
                    side[picked, lanes],
                    swapped[picked, lanes],
                    swapped[pl.ds(start + ROWS, CLASS_ROWS), lanes],
                    mid_a[:, lanes],
                    mid_b[:, lanes],
                    swapped[2 * ROWS :, lanes],
                ],
                0,
            )

        peak, more = attend(
            asked,
            jnp.concatenate([gathered(key_tile), class_marks], 1),
            jnp.concatenate([gathered(value_tile), class_marks], 1),
            head,
        )
        state[head][picked, :] = join(state[head][picked, :], more, peak, head)
        copies[head].start()
    for copy in copies:
        copy.wait()


def far_kernel(tiles, rows, here, other, parts):
    ends = slide_ends(tiles)
    seq, mp = lax.axis_index("seq"), lax.axis_index("mp")
    column = seq & 15
    beside = column ^ ((seq >> 4) << 1)
    count = FAR_GROUP * FAR_ROWS
    shape = (count, 2 * count)

    def position(place, holder):
        return ((place >> 4) * 16 + holder) * ROWS + (place & 15) * RATE_FAR

    at = iota(shape, 1)
    holder = jnp.where(at < count, beside, beside ^ 1)
    key_at = position(at & (count - 1), holder)
    query_at = position(iota(shape, 0), column)
    lane = iota((count, LANES), 1)
    for head in range(LOCAL_HEADS):
        number = mp * LOCAL_HEADS + head
        key_tile, value_tile = tile(KEY_TILE[head]), tile(VALUE_TILE[head])
        asked = rows[:, :, tile(QUERY_TILE[head])].reshape(count, LANES)
        asked = head_lanes(asked, head)
        scores = matmul_t(asked, jnp.concatenate([here[:, key_tile], other[:, key_tile]], 0))
        same = slide_of(query_at + number, ends) == slide_of(key_at + number, ends)
        scores = jnp.where(same, scores, HIDDEN_SCORE)
        peak = jnp.max(scores, -1, keepdims=True)
        weights = jnp.exp(scores - peak)
        total = jnp.sum(weights, -1, keepdims=True)
        values = jnp.concatenate([here[:, value_tile], other[:, value_tile]], 0)
        part = matmul(weights.astype(jnp.bfloat16), values)
        part = pack(part, peak, total, head, lane)
        parts[:, :, tile(head)] = part.reshape(FAR_GROUP, FAR_ROWS, LANES)


def finish_kernel(parts, w_out, *refs):
    n = LOCAL_HEADS
    held, (terms, far_out), state, sems = refs[:n], refs[n : n + 2], refs[n + 2 : -1], refs[-1]
    fetches = [pltpu.make_async_copy(held[i], state[i], sems.at[i]) for i in range(n)]
    for fetch in fetches:
        fetch.start()
    mp = lax.axis_index("mp")
    far_parts = []
    for head in range(LOCAL_HEADS):
        spare = SPARE[head]
        pieces = [parts[index, :, tile(head)] for index in range(FAR_GROUP)]
        tops = [piece[:, spare : spare + 1] for piece in pieces]
        peak = functools.reduce(jnp.maximum, tops)
        total = jnp.zeros((FAR_ROWS, LANES), jnp.float32)
        for piece, top in zip(pieces, tops):
            total = total + piece * jnp.exp(top - peak)
        far_parts.append(total / total[:, spare + 1 : spare + 2])
        number = mp * LOCAL_HEADS + head
        start = (number & 3) * CLASS_ROWS + (number >> 2) * FAR_ROWS
        picked = pl.ds(pl.multiple_of(start, FAR_ROWS), FAR_ROWS)
        fetches[head].wait()
        state[head][picked, :] = join(state[head][picked, :], total, peak, head)

    def packed(values):
        first = jnp.where(iota(values[0].shape, 1) < HEAD_DIM, values[0], values[1])
        return first.astype(jnp.bfloat16), values[2].astype(jnp.bfloat16)

    first, last = packed(far_parts)
    far_out[:, :128] = first
    far_out[:, 128:] = last[:, HEAD_DIM:]
    back = (place_of(iota((ROWS, ROWS), 0)) == iota((ROWS, ROWS), 1)).astype(jnp.bfloat16)
    first, last = packed(
        [
            state[head][...] / state[head][:, SPARE[head] + 1 : SPARE[head] + 2]
            for head in range(LOCAL_HEADS)
        ]
    )
    mixed = jnp.concatenate([first, last[:, HEAD_DIM:]], 1)
    mixed = matmul(back, mixed).astype(jnp.bfloat16)
    terms[...] = matmul(mixed, w_out[...]).astype(jnp.bfloat16).reshape(4, BLOCK, WIDTH)


def weights_kernel(w_up, w_down, out):
    start = pl.multiple_of((lax.axis_index("seq") & 1) * HALF, HALF)
    out[:HALF, :HALF] = w_up[:HALF, pl.ds(start, HALF)]
    out[:HALF, HALF:] = w_up[HALF:, pl.ds(start, HALF)]
    out[HALF:, :] = w_down[pl.ds(start, HALF), :]


def hidden_part(normed, weights):
    raised = matmul(normed[:, :HALF], weights[:HALF, :HALF])
    raised = raised + matmul(normed[:, HALF:], weights[:HALF, HALF:])
    hidden = (0.5 * raised * (1.0 + lax.erf(raised * 0.7071067811865476))).astype(jnp.bfloat16)
    return matmul(hidden, weights[HALF:, :])


def norm_kernel(tokens, terms, gain, attended, normed):
    summed = terms[0].astype(jnp.float32)
    for group in range(1, 4):
        summed = summed + terms[group].astype(jnp.float32)
    summed = summed.astype(jnp.bfloat16)
    attended[...] = summed
    start = pl.multiple_of(lax.axis_index("mp") * BLOCK, BLOCK)
    own = tokens[pl.ds(start, BLOCK), :].astype(jnp.float32)
    normed[...] = layer_norm(own + summed.astype(jnp.float32), gain[...])


def ffn_kernel(own, other, weights, kept, sent, held, sems):
    copies = []
    for group in range(4):
        for index in range(4):
            part = pl.ds(index * 192, 192)
            copies.append(
                pltpu.make_async_copy(
                    weights.at[group, part], held.at[group, part], sems.at[4 * group + index]
                )
            )
    for copy in copies:
        copy.start()
    rows = jnp.concatenate([own[...], other[...]], 0)
    total = jnp.zeros((2 * BLOCK, WIDTH), jnp.float32)
    for group in range(4):
        for copy in copies[4 * group : 4 * group + 4]:
            copy.wait()
        total = total + hidden_part(rows, held.at[group])
    kept[...] = total[:BLOCK, :]
    sent[...] = total[BLOCK:, :].astype(jnp.bfloat16)


def call(kernel, micros, outs, ins, scratch=(), kept=pltpu.VMEM, limit=VMEM):
    places = {"smem": pltpu.SMEM, "vmem": pltpu.VMEM, "hbm": pltpu.HBM}
    return pl.pallas_call(
        kernel,
        out_shape=[jax.ShapeDtypeStruct(*out) for out in outs],
        in_specs=[pl.BlockSpec(memory_space=places[where]) for _, where in ins],
        out_specs=[pl.BlockSpec(memory_space=kept) for _ in outs],
        scratch_shapes=list(scratch),
        cost_estimate=pl.CostEstimate(
            flops=int(micros * 1.1e9), bytes_accessed=int(micros * 1e6), transcendentals=0
        ),
        compiler_params=pltpu.CompilerParams(vmem_limit_bytes=limit),
    )(*[array for array, _ in ins])


def swap(value, step):
    return lax.ppermute(value, "seq", [(i, i ^ step) for i in range(lax.axis_size("seq"))])


def local(tokens, slide_tiles, attn_gain, w_query, w_key, w_value, w_out, ffn_gain, w_up, w_down):
    bf16, f32 = jnp.bfloat16, jnp.float32
    v, s, h = "vmem", "smem", "hbm"
    dma = pltpu.SemaphoreType.DMA
    columns = [[16 * z + place for z in range(FAR_GROUP)] for place in range(16)]
    across = [
        (16 * z + (place ^ (2 * z)), 16 * z + place) for z in range(FAR_GROUP) for place in range(16)
    ]
    w_query, w_key, w_value = w_query.T, w_key.T, w_value.T
    query, own, mid, far = call(
        project_kernel,
        3,
        [
            ((ROWS, 256), bf16), ((ROWS, 384), bf16), ((CLASS_ROWS, 384), bf16),
            ((FAR_GROUP, FAR_ROWS, 640), bf16),
        ],
        [(tokens, h), (attn_gain, v), (w_query, h), (w_key, h), (w_value, h)],
        [pltpu.VMEM((ROWS, WIDTH), bf16), pltpu.VMEM((3, 192, WIDTH), bf16), dma((7,))],
        limit=WHOLE_VMEM,
    )
    far_rows = lax.all_to_all(
        far, "seq", split_axis=0, concat_axis=0, tiled=True, axis_index_groups=columns
    )
    w_up, w_down, _ = lax.optimization_barrier((w_up, w_down, far))
    (packed,) = call(weights_kernel, 2, [((2 * HALF, WIDTH), bf16)], [(w_up, v), (w_down, v)])
    mine = lax.all_gather(packed, "mp", axis=0)
    side = swap(own, 2)

    far_keys = far_rows[:, :, 256:].reshape(128, 384)
    far_here = lax.ppermute(far_keys, "seq", across)
    query, _ = lax.optimization_barrier((query, far_keys))
    mid_a, mid_b = swap(mid, 4), swap(mid, 6)
    state = [((ROWS, LANES), f32)] * LOCAL_HEADS
    scratch = [pltpu.VMEM(*shape) for shape in state]
    near = call(
        near_kernel,
        3,
        state,
        [(slide_tiles, s), (query, v), (own, v), (side, v)],
        [*scratch, dma((3,))],
        pltpu.HBM,
        WHOLE_VMEM,
    )
    side, mid_a, mid_b, far_here, *near = lax.optimization_barrier(
        (side, mid_a, mid_b, far_here, *near)
    )
    far_other = swap(far_here, 1)
    swapped = swap(jnp.concatenate([own, side, mid_a, mid_b], 0), 1)
    (parts,) = call(
        far_kernel,
        2,
        [((FAR_GROUP, FAR_ROWS, 384), f32)],
        [(slide_tiles, s), (far_rows, v), (far_here, v), (far_other, v)],
    )
    parts, *near = lax.optimization_barrier((parts, *near))
    both = call(
        rest_kernel,
        5,
        state,
        [
            (slide_tiles, s), (query, v), (own, v), (side, v), (mid_a, v), (mid_b, v), (swapped, v),
            *[(held, h) for held in near],
        ],
        [*scratch, *scratch, dma((6,))],
        pltpu.HBM,
        WHOLE_VMEM,
    )
    parts = lax.all_to_all(
        parts, "seq", split_axis=0, concat_axis=0, tiled=True, axis_index_groups=columns
    )
    mine, _ = lax.optimization_barrier((mine, parts))
    terms, far_attended = call(
        finish_kernel,
        3,
        [((4, BLOCK, WIDTH), bf16), ((FAR_ROWS, 192), bf16)],
        [(parts, v), (w_out, v), *[(held, h) for held in both]],
        [*scratch, dma((3,))],
        limit=WHOLE_VMEM,
    )
    terms = lax.all_to_all(terms, "mp", split_axis=0, concat_axis=0, tiled=True)
    attended, normed = call(
        norm_kernel,
        1,
        [((BLOCK, WIDTH), bf16), ((BLOCK, WIDTH), bf16)],
        [(tokens, v), (terms, v), (ffn_gain, v)],
    )
    kept, sent = call(
        ffn_kernel,
        4,
        [((BLOCK, WIDTH), f32), ((BLOCK, WIDTH), bf16)],
        [(normed, v), (swap(normed, 1), v), (mine, h)],
        [pltpu.VMEM((4, 2 * HALF, WIDTH), bf16), dma((16,))],
        limit=WHOLE_VMEM,
    )
    ffn_out = (kept + swap(sent, 1).astype(f32)).astype(bf16)
    return (attended, far_attended, ffn_out)


def solution(mesh):
    return jax.shard_map(
        local,
        mesh=mesh,
        in_specs=(
            P("seq", None),
            P(),
            P(),
            P(None, "mp"),
            P(None, "mp"),
            P(None, "mp"),
            P("mp", None),
            P(),
            P(None, "mp"),
            P("mp", None),
        ),
        out_specs=(P(("seq", "mp"), None), P("seq", "mp"), P(("seq", "mp"), None)),
        check_vma=False,
    )
```

```python
import functools

import jax
import jax.numpy as jnp
from jax import lax
from jax.experimental import pallas as pl
from jax.experimental.pallas import tpu as pltpu
from jax.sharding import PartitionSpec as P

HEAD_DIM = 64
LOCAL_HEADS = 3
RATE_MID = 4
RATE_FAR = 32
ROWS = 512
CLASS_ROWS = ROWS // RATE_MID
FAR_ROWS = ROWS // RATE_FAR
LANES = 128
SLIDES = 4
WIDTH = 768
HALF = WIDTH // 2
BLOCK = 128
EPS = 1e-05
HIDDEN_SCORE = -1e30
VMEM = 16 * 1024 * 1024
WHOLE_VMEM = 58 * 1024 * 1024

KEY_TILE = (0, 0, 2)
VALUE_TILE = (1, 1, 2)
QUERY_TILE = (0, 0, 1)
SPARE = (64, 0, 0)
FAR_GROUP = 8


def iota(shape, dim):
    return lax.broadcasted_iota(jnp.int32, shape, dim)


def place_of(row):
    return (row & 3) * CLASS_ROWS + ((row >> 2) & 7) * FAR_ROWS + (row >> 5)


def row_at(place):
    return (place & 15) * RATE_FAR + ((place >> 4) & 7) * RATE_MID + (place >> 7)


def layer_norm(as_float, gain):
    mean_val = jnp.mean(as_float, -1, keepdims=True)
    centered = as_float - mean_val
    variance = jnp.mean(centered * centered, -1, keepdims=True)
    return (centered * lax.rsqrt(variance + EPS) * gain.astype(jnp.float32)).astype(jnp.bfloat16)


def matmul(left, right):
    return jnp.dot(left, right, preferred_element_type=jnp.float32)


def matmul_t(left, right):
    return lax.dot_general(
        left, right, (((1,), (1,)), ((), ())), preferred_element_type=jnp.float32
    )


def slide_of(positions, ends):
    index = (positions >= ends[0]).astype(jnp.int32)
    for end in ends[1:]:
        index = index + (positions >= end).astype(jnp.int32)
    return index


def slide_ends(tiles_ref):
    ends = [tiles_ref[0]]
    for slide in range(1, SLIDES - 1):
        ends.append(ends[-1] + tiles_ref[slide])
    return ends


def query_marks(positions, ends):
    rows = positions.shape[0]
    lane = iota((rows, LANES), 1)
    return (lane == slide_of(positions, ends)).astype(jnp.bfloat16)


def key_marks(positions, ends):
    rows = positions.shape[0]
    lane = iota((rows, LANES), 1)
    hide = (lane < SLIDES) & (lane != slide_of(positions, ends))
    marks = jnp.where(hide, HIDDEN_SCORE, jnp.where(lane == SLIDES, 1.0, 0.0))
    return marks.astype(jnp.bfloat16)


def head_lanes(value, head):
    lane = iota(value.shape, 1)
    keep = lane < HEAD_DIM if head != 1 else lane >= HEAD_DIM
    return jnp.where(keep, value, jnp.zeros_like(value))


def tile(index):
    return slice(index * LANES, (index + 1) * LANES)


def project(normed, w_query, w_key, w_value):
    asked = (matmul_t(normed, w_query[...]) * (1.0 / 8.0)).astype(jnp.bfloat16)
    key = matmul_t(normed, w_key[...]).astype(jnp.bfloat16)
    value = matmul_t(normed, w_value[...]).astype(jnp.bfloat16)
    none = jnp.zeros_like(asked[:, 128:])
    queries = [asked[:, :128], jnp.concatenate([asked[:, 128:], none], 1)]
    keyvals = [key[:, :128], value[:, :128]]
    return queries, keyvals + [jnp.concatenate([key[:, 128:], value[:, 128:]], 1)]


def project_kernel(
    tokens, gain, w_query, w_key, w_value, query, keyval, mid, far, rows, weights, sems
):
    mp = lax.axis_index("mp")
    copies = []
    for index in range(4):
        part = pl.ds(index * BLOCK, BLOCK)
        copies.append(pltpu.make_async_copy(tokens.at[part], rows.at[part], sems.at[index]))
    for index, weight in enumerate((w_query, w_key, w_value)):
        copies.append(pltpu.make_async_copy(weight, weights.at[index], sems.at[4 + index]))
    for copy in copies:
        copy.start()
    for copy in copies[:4]:
        copy.wait()
    normed = layer_norm(rows[...].astype(jnp.float32), gain[...])
    order = iota((ROWS, ROWS), 0) == place_of(iota((ROWS, ROWS), 1))
    normed = matmul(order.astype(jnp.bfloat16), normed).astype(jnp.bfloat16)
    for copy in copies[4:]:
        copy.wait()
    queries, keyvals = project(normed, *[weights.at[index] for index in range(3)])
    for index, value in enumerate(queries):
        query[:, tile(index)] = value
    for index, value in enumerate(keyvals):
        keyval[:, tile(index)] = value

    def pick(source, index, whose, count):
        starts = []
        for head in range(LOCAL_HEADS):
            number = mp * LOCAL_HEADS + head
            start = (number & 3) * CLASS_ROWS
            if count == FAR_ROWS:
                start = start + (number >> 2) * FAR_ROWS
            starts.append(pl.ds(pl.multiple_of(start, count), count))
        if whose[2] == index:
            return source[starts[2], tile(index)]
        low, high = source[starts[0], tile(index)], source[starts[1], tile(index)]
        return jnp.where(iota(low.shape, 1) < HEAD_DIM, low, high)

    for index in range(3):
        mid[:, tile(index)] = pick(keyval, index, KEY_TILE, CLASS_ROWS)
    picked = [pick(query, index, QUERY_TILE, FAR_ROWS) for index in range(2)]
    picked += [pick(keyval, index, KEY_TILE, FAR_ROWS) for index in range(3)]
    for index, value in enumerate(picked):
        for copy in range(FAR_GROUP):
            far[copy, :, tile(index)] = value


def attend(query, keys, values, head):
    scores = matmul_t(query, keys)
    peak = jnp.max(scores, -1, keepdims=True)
    weights = jnp.exp(scores - peak).astype(jnp.bfloat16)
    sums = matmul(weights, values)
    lane = iota((sums.shape[0], LANES), 1)
    total = sums[:, LANES + SLIDES : LANES + SLIDES + 1]
    return peak, pack(sums[:, :LANES], peak, total, head, lane)


def pack(sums, peak, total, head, lane):
    return jnp.where(
        lane == SPARE[head], peak, jnp.where(lane == SPARE[head] + 1, total, sums)
    )


def join(held, more, peak, head):
    spare = SPARE[head]
    before = held[:, spare : spare + 1]
    largest = jnp.maximum(before, peak)
    both = held * jnp.exp(before - largest) + more * jnp.exp(peak - largest)
    return jnp.where(iota(both.shape, 1) == spare, largest, both)


def marks_near(seq, ends, steps):
    rows = row_at(iota((ROWS, LANES), 0))
    return jnp.concatenate([key_marks(rows + (seq ^ step) * ROWS, ends) for step in steps], 0)


def near_kernel(tiles, query, own, side, *state):
    ends = slide_ends(tiles)
    seq = lax.axis_index("seq")
    marks = query_marks(row_at(iota((ROWS, LANES), 0)) + seq * ROWS, ends)
    keys_marks = marks_near(seq, ends, (0, 2))
    for head in range(LOCAL_HEADS):
        key_tile, value_tile = tile(KEY_TILE[head]), tile(VALUE_TILE[head])
        asked = head_lanes(query[:, tile(QUERY_TILE[head])], head)
        keys = jnp.concatenate([own[:, key_tile], side[:, key_tile]], 0)
        values = jnp.concatenate([own[:, value_tile], side[:, value_tile]], 0)
        _, state[head][...] = attend(
            jnp.concatenate([asked, marks], 1),
            jnp.concatenate([keys, keys_marks], 1),
            jnp.concatenate([values, keys_marks], 1),
            head,
        )


def rest_kernel(tiles, query, own, side, mid_a, mid_b, swapped, parts, w_out, *refs):
    n = LOCAL_HEADS
    held, (terms, far_out), state = refs[:n], refs[n : n + 2], refs[n + 2 :]
    ends = slide_ends(tiles)
    seq, mp = lax.axis_index("seq"), lax.axis_index("mp")
    marks = query_marks(row_at(iota((ROWS, LANES), 0)) + seq * ROWS, ends)
    near_marks = marks_near(seq, ends, (1, 3))
    for head in range(LOCAL_HEADS):
        key_tile, value_tile = tile(KEY_TILE[head]), tile(VALUE_TILE[head])
        asked = head_lanes(query[:, tile(QUERY_TILE[head])], head)
        peak, more = attend(
            jnp.concatenate([asked, marks], 1),
            jnp.concatenate([swapped[: 2 * ROWS, key_tile], near_marks], 1),
            jnp.concatenate([swapped[: 2 * ROWS, value_tile], near_marks], 1),
            head,
        )
        state[head][...] = join(held[head][...], more, peak, head)

        offset = (mp * LOCAL_HEADS + head) & 3
        start = pl.multiple_of(offset * CLASS_ROWS, CLASS_ROWS)
        picked = pl.ds(start, CLASS_ROWS)
        place = iota((CLASS_ROWS, LANES), 0)
        class_rows = offset + RATE_MID * ((place >> 4) + ((place & 15) << 3))
        class_marks = jnp.concatenate(
            [key_marks(class_rows + (seq ^ step) * ROWS, ends) for step in (0, 2, 1, 3, 4, 6, 5, 7)],
            0,
        )
        asked = head_lanes(query[picked, tile(QUERY_TILE[head])], head)
        asked = jnp.concatenate([asked, query_marks(class_rows + seq * ROWS, ends)], 1)

        def gathered(lanes):
            return jnp.concatenate(
                [
                    own[picked, lanes],
                    side[picked, lanes],
                    swapped[picked, lanes],
                    swapped[pl.ds(start + ROWS, CLASS_ROWS), lanes],
                    mid_a[:, lanes],
                    mid_b[:, lanes],
                    swapped[2 * ROWS :, lanes],
                ],
                0,
            )

        peak, more = attend(
            asked,
            jnp.concatenate([gathered(key_tile), class_marks], 1),
            jnp.concatenate([gathered(value_tile), class_marks], 1),
            head,
        )
        state[head][picked, :] = join(state[head][picked, :], more, peak, head)
    far_parts = []
    for head in range(LOCAL_HEADS):
        spare = SPARE[head]
        pieces = [parts[index, :, tile(head)] for index in range(FAR_GROUP)]
        tops = [piece[:, spare : spare + 1] for piece in pieces]
        peak = functools.reduce(jnp.maximum, tops)
        total = jnp.zeros((FAR_ROWS, LANES), jnp.float32)
        for piece, top in zip(pieces, tops):
            total = total + piece * jnp.exp(top - peak)
        far_parts.append(total / total[:, spare + 1 : spare + 2])
        number = mp * LOCAL_HEADS + head
        start = (number & 3) * CLASS_ROWS + (number >> 2) * FAR_ROWS
        picked = pl.ds(pl.multiple_of(start, FAR_ROWS), FAR_ROWS)
        state[head][picked, :] = join(state[head][picked, :], total, peak, head)

    def packed(values):
        first = jnp.where(iota(values[0].shape, 1) < HEAD_DIM, values[0], values[1])
        return first.astype(jnp.bfloat16), values[2].astype(jnp.bfloat16)

    first, last = packed(far_parts)
    far_out[:, :128] = first
    far_out[:, 128:] = last[:, HEAD_DIM:]
    back = (place_of(iota((ROWS, ROWS), 0)) == iota((ROWS, ROWS), 1)).astype(jnp.bfloat16)
    first, last = packed(
        [
            state[head][...] / state[head][:, SPARE[head] + 1 : SPARE[head] + 2]
            for head in range(LOCAL_HEADS)
        ]
    )
    mixed = jnp.concatenate([first, last[:, HEAD_DIM:]], 1)
    mixed = matmul(back, mixed).astype(jnp.bfloat16)
    terms[...] = matmul(mixed, w_out[...]).astype(jnp.bfloat16).reshape(4, BLOCK, WIDTH)


def far_kernel(tiles, rows, here, other, parts):
    ends = slide_ends(tiles)
    seq, mp = lax.axis_index("seq"), lax.axis_index("mp")
    column = seq & 15
    beside = column ^ ((seq >> 4) << 1)
    count = FAR_GROUP * FAR_ROWS
    shape = (count, 2 * count)

    def position(place, holder):
        return ((place >> 4) * 16 + holder) * ROWS + (place & 15) * RATE_FAR

    at = iota(shape, 1)
    holder = jnp.where(at < count, beside, beside ^ 1)
    key_at = position(at & (count - 1), holder)
    query_at = position(iota(shape, 0), column)
    lane = iota((count, LANES), 1)
    for head in range(LOCAL_HEADS):
        number = mp * LOCAL_HEADS + head
        key_tile, value_tile = tile(KEY_TILE[head]), tile(VALUE_TILE[head])
        asked = rows[:, :, tile(QUERY_TILE[head])].reshape(count, LANES)
        asked = head_lanes(asked, head)
        scores = matmul_t(asked, jnp.concatenate([here[:, key_tile], other[:, key_tile]], 0))
        same = slide_of(query_at + number, ends) == slide_of(key_at + number, ends)
        scores = jnp.where(same, scores, HIDDEN_SCORE)
        peak = jnp.max(scores, -1, keepdims=True)
        weights = jnp.exp(scores - peak)
        total = jnp.sum(weights, -1, keepdims=True)
        values = jnp.concatenate([here[:, value_tile], other[:, value_tile]], 0)
        part = matmul(weights.astype(jnp.bfloat16), values)
        part = pack(part, peak, total, head, lane)
        parts[:, :, tile(head)] = part.reshape(FAR_GROUP, FAR_ROWS, LANES)


def weights_kernel(w_up, w_down, out):
    start = pl.multiple_of((lax.axis_index("seq") & 1) * HALF, HALF)
    out[:HALF, :HALF] = w_up[:HALF, pl.ds(start, HALF)]
    out[:HALF, HALF:] = w_up[HALF:, pl.ds(start, HALF)]
    out[HALF:, :] = w_down[pl.ds(start, HALF), :]


def hidden_part(normed, weights):
    raised = matmul(normed[:, :HALF], weights[:HALF, :HALF])
    raised = raised + matmul(normed[:, HALF:], weights[:HALF, HALF:])
    hidden = (0.5 * raised * (1.0 + lax.erf(raised * 0.7071067811865476))).astype(jnp.bfloat16)
    return matmul(hidden, weights[HALF:, :])


def norm_kernel(tokens, terms, gain, attended, normed):
    summed = terms[0].astype(jnp.float32)
    for group in range(1, 4):
        summed = summed + terms[group].astype(jnp.float32)
    summed = summed.astype(jnp.bfloat16)
    attended[...] = summed
    start = pl.multiple_of(lax.axis_index("mp") * BLOCK, BLOCK)
    own = tokens[pl.ds(start, BLOCK), :].astype(jnp.float32)
    normed[...] = layer_norm(own + summed.astype(jnp.float32), gain[...])


def ffn_kernel(own, other, weights, kept, sent):
    rows = jnp.concatenate([own[...], other[...]], 0)
    total = jnp.zeros((2 * BLOCK, WIDTH), jnp.float32)
    for group in range(4):
        total = total + hidden_part(rows, weights.at[group])
    kept[...] = total[:BLOCK, :]
    sent[...] = total[BLOCK:, :].astype(jnp.bfloat16)


def call(kernel, micros, outs, ins, scratch=(), limit=VMEM):
    places = {"smem": pltpu.SMEM, "vmem": pltpu.VMEM, "hbm": pltpu.HBM}
    return pl.pallas_call(
        kernel,
        out_shape=[jax.ShapeDtypeStruct(*out) for out in outs],
        in_specs=[pl.BlockSpec(memory_space=places[where]) for _, where in ins],
        out_specs=[pl.BlockSpec(memory_space=pltpu.VMEM) for _ in outs],
        scratch_shapes=list(scratch),
        cost_estimate=pl.CostEstimate(
            flops=int(micros * 1.1e9), bytes_accessed=int(micros * 1e6), transcendentals=0
        ),
        compiler_params=pltpu.CompilerParams(vmem_limit_bytes=limit),
    )(*[array for array, _ in ins])


def swap(value, step):
    return lax.ppermute(value, "seq", [(i, i ^ step) for i in range(lax.axis_size("seq"))])


def local(tokens, slide_tiles, attn_gain, w_query, w_key, w_value, w_out, ffn_gain, w_up, w_down):
    bf16, f32 = jnp.bfloat16, jnp.float32
    v, s, h = "vmem", "smem", "hbm"
    dma = pltpu.SemaphoreType.DMA
    columns = [[16 * z + place for z in range(FAR_GROUP)] for place in range(16)]
    across = [
        (16 * z + (place ^ (2 * z)), 16 * z + place) for z in range(FAR_GROUP) for place in range(16)
    ]
    w_query, w_key, w_value = w_query.T, w_key.T, w_value.T
    query, own, mid, far = call(
        project_kernel,
        3,
        [
            ((ROWS, 256), bf16), ((ROWS, 384), bf16), ((CLASS_ROWS, 384), bf16),
            ((FAR_GROUP, FAR_ROWS, 640), bf16),
        ],
        [(tokens, h), (attn_gain, v), (w_query, h), (w_key, h), (w_value, h)],
        [pltpu.VMEM((ROWS, WIDTH), bf16), pltpu.VMEM((3, 192, WIDTH), bf16), dma((7,))],
        limit=WHOLE_VMEM,
    )
    far_rows = lax.all_to_all(
        far, "seq", split_axis=0, concat_axis=0, tiled=True, axis_index_groups=columns
    )
    w_up, w_down, _ = lax.optimization_barrier((w_up, w_down, far))
    (packed,) = call(weights_kernel, 2, [((2 * HALF, WIDTH), bf16)], [(w_up, v), (w_down, v)])
    mine = lax.all_gather(packed, "mp", axis=0)
    side = swap(own, 2)

    far_keys = far_rows[:, :, 256:].reshape(128, 384)
    far_here = lax.ppermute(far_keys, "seq", across)
    query, _ = lax.optimization_barrier((query, far_keys))
    mid_a, mid_b = swap(mid, 4), swap(mid, 6)
    state = [((ROWS, LANES), f32)] * LOCAL_HEADS
    near = call(near_kernel, 3, state, [(slide_tiles, s), (query, v), (own, v), (side, v)])
    side, mid_a, mid_b, far_here, *near = lax.optimization_barrier(
        (side, mid_a, mid_b, far_here, *near)
    )
    far_other = swap(far_here, 1)
    swapped = swap(jnp.concatenate([own, side, mid_a, mid_b], 0), 1)
    (parts,) = call(
        far_kernel,
        2,
        [((FAR_GROUP, FAR_ROWS, 384), f32)],
        [(slide_tiles, s), (far_rows, v), (far_here, v), (far_other, v)],
    )
    parts = lax.all_to_all(
        parts, "seq", split_axis=0, concat_axis=0, tiled=True, axis_index_groups=columns
    )
    terms, far_attended = call(
        rest_kernel,
        7,
        [((4, BLOCK, WIDTH), bf16), ((FAR_ROWS, 192), bf16)],
        [
            (slide_tiles, s), (query, v), (own, v), (side, v), (mid_a, v), (mid_b, v), (swapped, v),
            (parts, v), (w_out, v), *[(held, v) for held in near],
        ],
        [pltpu.VMEM(*shape) for shape in state],
    )
    terms = lax.all_to_all(terms, "mp", split_axis=0, concat_axis=0, tiled=True)
    terms, mine = lax.optimization_barrier((terms, mine))
    attended, normed = call(
        norm_kernel,
        1,
        [((BLOCK, WIDTH), bf16), ((BLOCK, WIDTH), bf16)],
        [(tokens, v), (terms, v), (ffn_gain, v)],
    )
    kept, sent = call(
        ffn_kernel,
        4,
        [((BLOCK, WIDTH), f32), ((BLOCK, WIDTH), bf16)],
        [(normed, v), (swap(normed, 1), v), (mine, v)],
    )
    ffn_out = (kept + swap(sent, 1).astype(f32)).astype(bf16)
    return (attended, far_attended, ffn_out)


def solution(mesh):
    return jax.shard_map(
        local,
        mesh=mesh,
        in_specs=(
            P("seq", None),
            P(),
            P(),
            P(None, "mp"),
            P(None, "mp"),
            P(None, "mp"),
            P("mp", None),
            P(),
            P(None, "mp"),
            P("mp", None),
        ),
        out_specs=(P(("seq", "mp"), None), P("seq", "mp"), P(("seq", "mp"), None)),
        check_vma=False,
    )
```

```python
import functools

import jax
import jax.numpy as jnp
from jax import lax
from jax.experimental import pallas as pl
from jax.experimental.pallas import tpu as pltpu
from jax.sharding import PartitionSpec as P

HEAD_DIM = 64
LOCAL_HEADS = 3
RATE_MID = 4
RATE_FAR = 32
ROWS = 512
CLASS_ROWS = ROWS // RATE_MID
FAR_ROWS = ROWS // RATE_FAR
LANES = 128
SLIDES = 4
WIDTH = 768
HALF = WIDTH // 2
BLOCK = 128
EPS = 1e-05
HIDDEN_SCORE = -1e30
VMEM = 16 * 1024 * 1024
WHOLE_VMEM = 58 * 1024 * 1024

KEY_TILE = (0, 0, 2)
VALUE_TILE = (1, 1, 2)
QUERY_TILE = (0, 0, 1)
SPARE = (64, 0, 0)
FAR_GROUP = 8


def iota(shape, dim):
    return lax.broadcasted_iota(jnp.int32, shape, dim)


def place_of(row):
    return (row & 3) * CLASS_ROWS + ((row >> 2) & 7) * FAR_ROWS + (row >> 5)


def row_at(place):
    return (place & 15) * RATE_FAR + ((place >> 4) & 7) * RATE_MID + (place >> 7)


def layer_norm(as_float, gain):
    mean_val = jnp.mean(as_float, -1, keepdims=True)
    centered = as_float - mean_val
    variance = jnp.mean(centered * centered, -1, keepdims=True)
    return (centered * lax.rsqrt(variance + EPS) * gain.astype(jnp.float32)).astype(jnp.bfloat16)


def matmul(left, right):
    return jnp.dot(left, right, preferred_element_type=jnp.float32)


def matmul_t(left, right):
    return lax.dot_general(
        left, right, (((1,), (1,)), ((), ())), preferred_element_type=jnp.float32
    )


def slide_of(positions, ends):
    index = (positions >= ends[0]).astype(jnp.int32)
    for end in ends[1:]:
        index = index + (positions >= end).astype(jnp.int32)
    return index


def slide_ends(tiles_ref):
    ends = [tiles_ref[0]]
    for slide in range(1, SLIDES - 1):
        ends.append(ends[-1] + tiles_ref[slide])
    return ends


def query_marks(positions, ends):
    rows = positions.shape[0]
    lane = iota((rows, LANES), 1)
    return (lane == slide_of(positions, ends)).astype(jnp.bfloat16)


def key_marks(positions, ends):
    rows = positions.shape[0]
    lane = iota((rows, LANES), 1)
    hide = (lane < SLIDES) & (lane != slide_of(positions, ends))
    marks = jnp.where(hide, HIDDEN_SCORE, jnp.where(lane == SLIDES, 1.0, 0.0))
    return marks.astype(jnp.bfloat16)


def head_lanes(value, head):
    lane = iota(value.shape, 1)
    keep = lane < HEAD_DIM if head != 1 else lane >= HEAD_DIM
    return jnp.where(keep, value, jnp.zeros_like(value))


def tile(index):
    return slice(index * LANES, (index + 1) * LANES)


def project(normed, w_query, w_key, w_value):
    asked = (matmul_t(normed, w_query[...]) * (1.0 / 8.0)).astype(jnp.bfloat16)
    key = matmul_t(normed, w_key[...]).astype(jnp.bfloat16)
    value = matmul_t(normed, w_value[...]).astype(jnp.bfloat16)
    none = jnp.zeros_like(asked[:, 128:])
    queries = [asked[:, :128], jnp.concatenate([asked[:, 128:], none], 1)]
    keyvals = [key[:, :128], value[:, :128]]
    return queries, keyvals + [jnp.concatenate([key[:, 128:], value[:, 128:]], 1)]


def project_kernel(
    tokens, gain, w_query, w_key, w_value, query, keyval, mid, far_query, far_keyval, rows, weights, sems
):
    mp = lax.axis_index("mp")
    copies = []
    for index in range(4):
        part = pl.ds(index * BLOCK, BLOCK)
        copies.append(pltpu.make_async_copy(tokens.at[part], rows.at[part], sems.at[index]))
    for index, weight in enumerate((w_query, w_key, w_value)):
        copies.append(pltpu.make_async_copy(weight, weights.at[index], sems.at[4 + index]))
    for copy in copies:
        copy.start()
    for copy in copies[:4]:
        copy.wait()
    normed = layer_norm(rows[...].astype(jnp.float32), gain[...])
    order = iota((ROWS, ROWS), 0) == place_of(iota((ROWS, ROWS), 1))
    normed = matmul(order.astype(jnp.bfloat16), normed).astype(jnp.bfloat16)
    for copy in copies[4:]:
        copy.wait()
    queries, keyvals = project(normed, *[weights.at[index] for index in range(3)])
    for index, value in enumerate(queries):
        query[:, tile(index)] = value
    for index, value in enumerate(keyvals):
        keyval[:, tile(index)] = value

    def pick(source, index, whose, count):
        starts = []
        for head in range(LOCAL_HEADS):
            number = mp * LOCAL_HEADS + head
            start = (number & 3) * CLASS_ROWS
            if count == FAR_ROWS:
                start = start + (number >> 2) * FAR_ROWS
            starts.append(pl.ds(pl.multiple_of(start, count), count))
        if whose[2] == index:
            return source[starts[2], tile(index)]
        low, high = source[starts[0], tile(index)], source[starts[1], tile(index)]
        return jnp.where(iota(low.shape, 1) < HEAD_DIM, low, high)

    for index in range(3):
        mid[:, tile(index)] = pick(keyval, index, KEY_TILE, CLASS_ROWS)
    for source, whose, target in ((query, QUERY_TILE, far_query), (keyval, KEY_TILE, far_keyval)):
        for index in range(whose[2] + 1):
            value = pick(source, index, whose, FAR_ROWS)
            for copy in range(FAR_GROUP):
                target[copy, :, tile(index)] = value


def attend(query, keys, values, head):
    scores = matmul_t(query, keys)
    peak = jnp.max(scores, -1, keepdims=True)
    weights = jnp.exp(scores - peak).astype(jnp.bfloat16)
    sums = matmul(weights, values)
    lane = iota((sums.shape[0], LANES), 1)
    total = sums[:, LANES + SLIDES : LANES + SLIDES + 1]
    return peak, pack(sums[:, :LANES], peak, total, head, lane)


def pack(sums, peak, total, head, lane):
    return jnp.where(
        lane == SPARE[head], peak, jnp.where(lane == SPARE[head] + 1, total, sums)
    )


def join(held, more, peak, head):
    spare = SPARE[head]
    before = held[:, spare : spare + 1]
    largest = jnp.maximum(before, peak)
    both = held * jnp.exp(before - largest) + more * jnp.exp(peak - largest)
    return jnp.where(iota(both.shape, 1) == spare, largest, both)


def marks_near(seq, ends, steps):
    rows = row_at(iota((ROWS, LANES), 0))
    return jnp.concatenate([key_marks(rows + (seq ^ step) * ROWS, ends) for step in steps], 0)


def near_kernel(tiles, query, own, side, *state):
    ends = slide_ends(tiles)
    seq = lax.axis_index("seq")
    marks = query_marks(row_at(iota((ROWS, LANES), 0)) + seq * ROWS, ends)
    keys_marks = marks_near(seq, ends, (0, 2))
    for head in range(LOCAL_HEADS):
        key_tile, value_tile = tile(KEY_TILE[head]), tile(VALUE_TILE[head])
        asked = head_lanes(query[:, tile(QUERY_TILE[head])], head)
        keys = jnp.concatenate([own[:, key_tile], side[:, key_tile]], 0)
        values = jnp.concatenate([own[:, value_tile], side[:, value_tile]], 0)
        _, state[head][...] = attend(
            jnp.concatenate([asked, marks], 1),
            jnp.concatenate([keys, keys_marks], 1),
            jnp.concatenate([values, keys_marks], 1),
            head,
        )


def rest_kernel(tiles, query, own, side, mid_a, mid_b, swapped, parts, w_out, *refs):
    n = LOCAL_HEADS
    held, terms, far_out, state = refs[:n], refs[n : n + 4], refs[n + 4], refs[n + 5 :]
    ends = slide_ends(tiles)
    seq, mp = lax.axis_index("seq"), lax.axis_index("mp")
    marks = query_marks(row_at(iota((ROWS, LANES), 0)) + seq * ROWS, ends)
    near_marks = marks_near(seq, ends, (1, 3))
    for head in range(LOCAL_HEADS):
        key_tile, value_tile = tile(KEY_TILE[head]), tile(VALUE_TILE[head])
        asked = head_lanes(query[:, tile(QUERY_TILE[head])], head)
        peak, more = attend(
            jnp.concatenate([asked, marks], 1),
            jnp.concatenate([swapped[: 2 * ROWS, key_tile], near_marks], 1),
            jnp.concatenate([swapped[: 2 * ROWS, value_tile], near_marks], 1),
            head,
        )
        state[head][...] = join(held[head][...], more, peak, head)

        offset = (mp * LOCAL_HEADS + head) & 3
        start = pl.multiple_of(offset * CLASS_ROWS, CLASS_ROWS)
        picked = pl.ds(start, CLASS_ROWS)
        place = iota((CLASS_ROWS, LANES), 0)
        class_rows = offset + RATE_MID * ((place >> 4) + ((place & 15) << 3))
        class_marks = jnp.concatenate(
            [key_marks(class_rows + (seq ^ step) * ROWS, ends) for step in (0, 2, 1, 3, 4, 6, 5, 7)],
            0,
        )
        asked = head_lanes(query[picked, tile(QUERY_TILE[head])], head)
        asked = jnp.concatenate([asked, query_marks(class_rows + seq * ROWS, ends)], 1)

        def gathered(lanes):
            return jnp.concatenate(
                [
                    own[picked, lanes],
                    side[picked, lanes],
                    swapped[picked, lanes],
                    swapped[pl.ds(start + ROWS, CLASS_ROWS), lanes],
                    mid_a[:, lanes],
                    mid_b[:, lanes],
                    swapped[2 * ROWS :, lanes],
                ],
                0,
            )

        peak, more = attend(
            asked,
            jnp.concatenate([gathered(key_tile), class_marks], 1),
            jnp.concatenate([gathered(value_tile), class_marks], 1),
            head,
        )
        state[head][picked, :] = join(state[head][picked, :], more, peak, head)
    far_parts = []
    for head in range(LOCAL_HEADS):
        spare = SPARE[head]
        pieces = [parts[index, :, tile(head)] for index in range(FAR_GROUP)]
        tops = [piece[:, spare : spare + 1] for piece in pieces]
        peak = functools.reduce(jnp.maximum, tops)
        total = jnp.zeros((FAR_ROWS, LANES), jnp.float32)
        for piece, top in zip(pieces, tops):
            total = total + piece * jnp.exp(top - peak)
        far_parts.append(total / total[:, spare + 1 : spare + 2])
        number = mp * LOCAL_HEADS + head
        start = (number & 3) * CLASS_ROWS + (number >> 2) * FAR_ROWS
        picked = pl.ds(pl.multiple_of(start, FAR_ROWS), FAR_ROWS)
        state[head][picked, :] = join(state[head][picked, :], total, peak, head)

    def packed(values):
        first = jnp.where(iota(values[0].shape, 1) < HEAD_DIM, values[0], values[1])
        return first.astype(jnp.bfloat16), values[2].astype(jnp.bfloat16)

    first, last = packed(far_parts)
    far_out[:, :128] = first
    far_out[:, 128:] = last[:, HEAD_DIM:]
    row = (iota((ROWS, ROWS), 0) + mp * BLOCK) & (ROWS - 1)
    back = (place_of(row) == iota((ROWS, ROWS), 1)).astype(jnp.bfloat16)
    first, last = packed(
        [
            state[head][...] / state[head][:, SPARE[head] + 1 : SPARE[head] + 2]
            for head in range(LOCAL_HEADS)
        ]
    )
    mixed = jnp.concatenate([first, last[:, HEAD_DIM:]], 1)
    mixed = matmul(back, mixed).astype(jnp.bfloat16)
    for index, term in enumerate(terms):
        part = mixed[index * BLOCK : (index + 1) * BLOCK]
        term[...] = matmul(part, w_out[...]).astype(jnp.bfloat16)


def far_kernel(tiles, rows, here, other, parts):
    ends = slide_ends(tiles)
    seq, mp = lax.axis_index("seq"), lax.axis_index("mp")
    count = FAR_GROUP * FAR_ROWS
    shape = (count, 2 * count)

    def position(place, holder):
        return holder * ROWS + (place & 15) * RATE_FAR

    at = iota(shape, 1)
    core = (seq & 1) ^ (at >> 7)
    key_at = position(at, (seq & 112) + ((at >> 4) & 7) * 2 + core)
    at = iota(shape, 0)
    query_at = position(at, (at >> 4) * 16 + (seq & 15))
    lane = iota((count, LANES), 1)

    def flat(ref, lanes):
        return ref[:, :, lanes].reshape(count, LANES)

    for head in range(LOCAL_HEADS):
        number = mp * LOCAL_HEADS + head
        key_tile, value_tile = tile(KEY_TILE[head]), tile(VALUE_TILE[head])
        asked = rows[:, :, tile(QUERY_TILE[head])].reshape(count, LANES)
        asked = head_lanes(asked, head)
        scores = matmul_t(asked, jnp.concatenate([flat(here, key_tile), flat(other, key_tile)], 0))
        same = slide_of(query_at + number, ends) == slide_of(key_at + number, ends)
        scores = jnp.where(same, scores, HIDDEN_SCORE)
        peak = jnp.max(scores, -1, keepdims=True)
        weights = jnp.exp(scores - peak)
        total = jnp.sum(weights, -1, keepdims=True)
        values = jnp.concatenate([flat(here, value_tile), flat(other, value_tile)], 0)
        part = matmul(weights.astype(jnp.bfloat16), values)
        part = pack(part, peak, total, head, lane)
        parts[:, :, tile(head)] = part.reshape(FAR_GROUP, FAR_ROWS, LANES)


def weights_kernel(w_up, w_down, out):
    start = pl.multiple_of((lax.axis_index("seq") & 1) * HALF, HALF)
    out[:HALF, :HALF] = w_up[:HALF, pl.ds(start, HALF)]
    out[:HALF, HALF:] = w_up[HALF:, pl.ds(start, HALF)]
    out[HALF:, :] = w_down[pl.ds(start, HALF), :]


def hidden_part(normed, weights):
    raised = matmul(normed[:, :HALF], weights[:HALF, :HALF])
    raised = raised + matmul(normed[:, HALF:], weights[:HALF, HALF:])
    hidden = (0.5 * raised * (1.0 + lax.erf(raised * 0.7071067811865476))).astype(jnp.bfloat16)
    return matmul(hidden, weights[HALF:, :])


def norm_kernel(tokens, gain, *refs):
    terms, attended, normed = refs[:4], refs[4], refs[5]
    summed = terms[0][...].astype(jnp.float32)
    for term in terms[1:]:
        summed = summed + term[...].astype(jnp.float32)
    summed = summed.astype(jnp.bfloat16)
    attended[...] = summed
    start = pl.multiple_of(lax.axis_index("mp") * BLOCK, BLOCK)
    own = tokens[pl.ds(start, BLOCK), :].astype(jnp.float32)
    normed[...] = layer_norm(own + summed.astype(jnp.float32), gain[...])


def ffn_kernel(own, other, weights, kept, sent):
    rows = jnp.concatenate([own[...], other[...]], 0)
    total = jnp.zeros((2 * BLOCK, WIDTH), jnp.float32)
    for group in range(4):
        total = total + hidden_part(rows, weights.at[group])
    kept[...] = total[:BLOCK, :]
    sent[...] = total[BLOCK:, :].astype(jnp.bfloat16)


def call(kernel, micros, outs, ins, scratch=(), limit=VMEM):
    places = {"smem": pltpu.SMEM, "vmem": pltpu.VMEM, "hbm": pltpu.HBM}
    return pl.pallas_call(
        kernel,
        out_shape=[jax.ShapeDtypeStruct(*out) for out in outs],
        in_specs=[pl.BlockSpec(memory_space=places[where]) for _, where in ins],
        out_specs=[pl.BlockSpec(memory_space=pltpu.VMEM) for _ in outs],
        scratch_shapes=list(scratch),
        cost_estimate=pl.CostEstimate(
            flops=int(micros * 1.1e9), bytes_accessed=int(micros * 1e6), transcendentals=0
        ),
        compiler_params=pltpu.CompilerParams(vmem_limit_bytes=limit),
    )(*[array for array, _ in ins])


def swap(value, step):
    return lax.ppermute(value, "seq", [(i, i ^ step) for i in range(lax.axis_size("seq"))])


def local(tokens, slide_tiles, attn_gain, w_query, w_key, w_value, w_out, ffn_gain, w_up, w_down):
    bf16, f32 = jnp.bfloat16, jnp.float32
    v, s, h = "vmem", "smem", "hbm"
    dma = pltpu.SemaphoreType.DMA
    columns = [[16 * z + place for z in range(FAR_GROUP)] for place in range(16)]
    planes = [
        [16 * z + 2 * y + core for y in range(FAR_GROUP)] for z in range(FAR_GROUP) for core in range(2)
    ]

    def to_all(value, groups):
        return lax.all_to_all(
            value, "seq", split_axis=0, concat_axis=0, tiled=True, axis_index_groups=groups
        )

    w_query, w_key, w_value = w_query.T, w_key.T, w_value.T
    query, own, mid, far_query, far_keyval = call(
        project_kernel,
        3,
        [
            ((ROWS, 256), bf16), ((ROWS, 384), bf16), ((CLASS_ROWS, 384), bf16),
            ((FAR_GROUP, FAR_ROWS, 256), bf16), ((FAR_GROUP, FAR_ROWS, 384), bf16),
        ],
        [(tokens, h), (attn_gain, v), (w_query, h), (w_key, h), (w_value, h)],
        [pltpu.VMEM((ROWS, WIDTH), bf16), pltpu.VMEM((3, 192, WIDTH), bf16), dma((7,))],
        limit=WHOLE_VMEM,
    )
    far_here = to_all(far_keyval, planes)
    far_query, _ = lax.optimization_barrier((far_query, far_here))
    far_rows = to_all(far_query, columns)
    w_up, w_down, _ = lax.optimization_barrier((w_up, w_down, far_keyval))
    (packed,) = call(weights_kernel, 2, [((2 * HALF, WIDTH), bf16)], [(w_up, v), (w_down, v)])
    mine = lax.all_gather(packed, "mp", axis=0)
    side = swap(own, 2)

    mid_a, mid_b = swap(mid, 4), swap(mid, 6)
    state = [((ROWS, LANES), f32)] * LOCAL_HEADS
    query, _, _ = lax.optimization_barrier((query, far_here, far_rows))
    near = call(near_kernel, 3, state, [(slide_tiles, s), (query, v), (own, v), (side, v)])
    far_other = swap(far_here, 1)
    far_other, *near = lax.optimization_barrier((far_other, *near))
    swapped = swap(jnp.concatenate([own, side, mid_a, mid_b], 0), 1)
    (parts,) = call(
        far_kernel,
        2,
        [((FAR_GROUP, FAR_ROWS, 384), f32)],
        [(slide_tiles, s), (far_rows, v), (far_here, v), (far_other, v)],
    )
    parts = to_all(parts, columns)
    *terms, far_attended = call(
        rest_kernel,
        7,
        [((BLOCK, WIDTH), bf16)] * 4 + [((FAR_ROWS, 192), bf16)],
        [
            (slide_tiles, s), (query, v), (own, v), (side, v), (mid_a, v), (mid_b, v), (swapped, v),
            (parts, v), (w_out, v), *[(held, v) for held in near],
        ],
        [pltpu.VMEM(*shape) for shape in state],
    )
    for step in (2, 1, 3):
        terms[step] = lax.ppermute(terms[step], "mp", [(i, (i + step) % 4) for i in range(4)])
    terms[2], mine = lax.optimization_barrier((terms[2], mine))
    terms = lax.optimization_barrier(terms)
    attended, normed = call(
        norm_kernel,
        1,
        [((BLOCK, WIDTH), bf16), ((BLOCK, WIDTH), bf16)],
        [(tokens, v), (ffn_gain, v), *[(term, v) for term in terms]],
    )
    kept, sent = call(
        ffn_kernel,
        4,
        [((BLOCK, WIDTH), f32), ((BLOCK, WIDTH), bf16)],
        [(normed, v), (swap(normed, 1), v), (mine, v)],
    )
    ffn_out = (kept + swap(sent, 1).astype(f32)).astype(bf16)
    return (attended, far_attended, ffn_out)


def solution(mesh):
    return jax.shard_map(
        local,
        mesh=mesh,
        in_specs=(
            P("seq", None),
            P(),
            P(),
            P(None, "mp"),
            P(None, "mp"),
            P(None, "mp"),
            P("mp", None),
            P(),
            P(None, "mp"),
            P("mp", None),
        ),
        out_specs=(P(("seq", "mp"), None), P("seq", "mp"), P(("seq", "mp"), None)),
        check_vma=False,
    )
```

```python
import functools

import jax
import jax.numpy as jnp
from jax import lax
from jax.experimental import pallas as pl
from jax.experimental.pallas import tpu as pltpu
from jax.sharding import PartitionSpec as P

HEAD_DIM = 64
LOCAL_HEADS = 3
RATE_MID = 4
RATE_FAR = 32
ROWS = 512
CLASS_ROWS = ROWS // RATE_MID
FAR_ROWS = ROWS // RATE_FAR
LANES = 128
SLIDES = 4
WIDTH = 768
HALF = WIDTH // 2
BLOCK = 128
EPS = 1e-05
HIDDEN_SCORE = -1e30
VMEM = 16 * 1024 * 1024
WHOLE_VMEM = 58 * 1024 * 1024

KEY_TILE = (0, 0, 2)
VALUE_TILE = (1, 1, 2)
QUERY_TILE = (0, 0, 1)
SPARE = (64, 0, 0)
FAR_GROUP = 8


def iota(shape, dim):
    return lax.broadcasted_iota(jnp.int32, shape, dim)


def place_of(row):
    return (row & 3) * CLASS_ROWS + ((row >> 2) & 7) * FAR_ROWS + (row >> 5)


def row_at(place):
    return (place & 15) * RATE_FAR + ((place >> 4) & 7) * RATE_MID + (place >> 7)


def layer_norm(as_float, gain):
    mean_val = jnp.mean(as_float, -1, keepdims=True)
    centered = as_float - mean_val
    variance = jnp.mean(centered * centered, -1, keepdims=True)
    return (centered * lax.rsqrt(variance + EPS) * gain.astype(jnp.float32)).astype(jnp.bfloat16)


def matmul(left, right):
    return jnp.dot(left, right, preferred_element_type=jnp.float32)


def matmul_t(left, right):
    return lax.dot_general(
        left, right, (((1,), (1,)), ((), ())), preferred_element_type=jnp.float32
    )


def slide_of(positions, ends):
    index = (positions >= ends[0]).astype(jnp.int32)
    for end in ends[1:]:
        index = index + (positions >= end).astype(jnp.int32)
    return index


def slide_ends(tiles_ref):
    ends = [tiles_ref[0]]
    for slide in range(1, SLIDES - 1):
        ends.append(ends[-1] + tiles_ref[slide])
    return ends


def query_marks(positions, ends):
    rows = positions.shape[0]
    lane = iota((rows, LANES), 1)
    return (lane == slide_of(positions, ends)).astype(jnp.bfloat16)


def key_marks(positions, ends):
    rows = positions.shape[0]
    lane = iota((rows, LANES), 1)
    hide = (lane < SLIDES) & (lane != slide_of(positions, ends))
    marks = jnp.where(hide, HIDDEN_SCORE, jnp.where(lane == SLIDES, 1.0, 0.0))
    return marks.astype(jnp.bfloat16)


def head_lanes(value, head):
    lane = iota(value.shape, 1)
    keep = lane < HEAD_DIM if head != 1 else lane >= HEAD_DIM
    return jnp.where(keep, value, jnp.zeros_like(value))


def tile(index):
    return slice(index * LANES, (index + 1) * LANES)


def project(normed, w_query, w_key, w_value):
    asked = (matmul_t(normed, w_query[...]) * (1.0 / 8.0)).astype(jnp.bfloat16)
    key = matmul_t(normed, w_key[...]).astype(jnp.bfloat16)
    value = matmul_t(normed, w_value[...]).astype(jnp.bfloat16)
    none = jnp.zeros_like(asked[:, 128:])
    queries = [asked[:, :128], jnp.concatenate([asked[:, 128:], none], 1)]
    keyvals = [key[:, :128], value[:, :128]]
    return queries, keyvals + [jnp.concatenate([key[:, 128:], value[:, 128:]], 1)]


def project_kernel(
    tokens, gain, w_query, w_key, w_value, query, keyval, mid, far_query, far_keyval, rows, weights, sems
):
    mp = lax.axis_index("mp")
    copies = []
    for index in range(4):
        part = pl.ds(index * BLOCK, BLOCK)
        copies.append(pltpu.make_async_copy(tokens.at[part], rows.at[part], sems.at[index]))
    for index, weight in enumerate((w_query, w_key, w_value)):
        copies.append(pltpu.make_async_copy(weight, weights.at[index], sems.at[4 + index]))
    for copy in copies:
        copy.start()
    for copy in copies[:4]:
        copy.wait()
    normed = layer_norm(rows[...].astype(jnp.float32), gain[...])
    order = iota((ROWS, ROWS), 0) == place_of(iota((ROWS, ROWS), 1))
    normed = matmul(order.astype(jnp.bfloat16), normed).astype(jnp.bfloat16)
    for copy in copies[4:]:
        copy.wait()
    queries, keyvals = project(normed, *[weights.at[index] for index in range(3)])
    for index, value in enumerate(queries):
        query[:, tile(index)] = value
    for index, value in enumerate(keyvals):
        keyval[:, tile(index)] = value

    def pick(source, index, whose, count):
        starts = []
        for head in range(LOCAL_HEADS):
            number = mp * LOCAL_HEADS + head
            start = (number & 3) * CLASS_ROWS
            if count == FAR_ROWS:
                start = start + (number >> 2) * FAR_ROWS
            starts.append(pl.ds(pl.multiple_of(start, count), count))
        if whose[2] == index:
            return source[starts[2], tile(index)]
        low, high = source[starts[0], tile(index)], source[starts[1], tile(index)]
        return jnp.where(iota(low.shape, 1) < HEAD_DIM, low, high)

    for index in range(3):
        mid[:, tile(index)] = pick(keyval, index, KEY_TILE, CLASS_ROWS)
    for source, whose, target in ((query, QUERY_TILE, far_query), (keyval, KEY_TILE, far_keyval)):
        for index in range(whose[2] + 1):
            value = pick(source, index, whose, FAR_ROWS)
            for copy in range(FAR_GROUP):
                target[copy, :, tile(index)] = value


def attend(query, keys, values, head):
    scores = matmul_t(query, keys)
    peak = jnp.max(scores, -1, keepdims=True)
    weights = jnp.exp(scores - peak).astype(jnp.bfloat16)
    sums = matmul(weights, values)
    lane = iota((sums.shape[0], LANES), 1)
    total = sums[:, LANES + SLIDES : LANES + SLIDES + 1]
    return peak, pack(sums[:, :LANES], peak, total, head, lane)


def pack(sums, peak, total, head, lane):
    return jnp.where(
        lane == SPARE[head], peak, jnp.where(lane == SPARE[head] + 1, total, sums)
    )


def join(held, more, peak, head):
    spare = SPARE[head]
    before = held[:, spare : spare + 1]
    largest = jnp.maximum(before, peak)
    both = held * jnp.exp(before - largest) + more * jnp.exp(peak - largest)
    return jnp.where(iota(both.shape, 1) == spare, largest, both)


def marks_near(seq, ends, steps):
    rows = row_at(iota((ROWS, LANES), 0))
    return jnp.concatenate([key_marks(rows + (seq ^ step) * ROWS, ends) for step in steps], 0)


def near_kernel(tiles, query, own, side, *state):
    ends = slide_ends(tiles)
    seq = lax.axis_index("seq")
    marks = query_marks(row_at(iota((ROWS, LANES), 0)) + seq * ROWS, ends)
    keys_marks = marks_near(seq, ends, (0, 2))
    for head in range(LOCAL_HEADS):
        key_tile, value_tile = tile(KEY_TILE[head]), tile(VALUE_TILE[head])
        asked = head_lanes(query[:, tile(QUERY_TILE[head])], head)
        keys = jnp.concatenate([own[:, key_tile], side[:, key_tile]], 0)
        values = jnp.concatenate([own[:, value_tile], side[:, value_tile]], 0)
        _, state[head][...] = attend(
            jnp.concatenate([asked, marks], 1),
            jnp.concatenate([keys, keys_marks], 1),
            jnp.concatenate([values, keys_marks], 1),
            head,
        )


def rest_kernel(tiles, query, own, side, mid_a, mid_b, swapped, parts, w_out, *refs):
    n = LOCAL_HEADS
    held, terms, far_out, state = refs[:n], refs[n : n + 4], refs[n + 4], refs[n + 5 :]
    ends = slide_ends(tiles)
    seq, mp = lax.axis_index("seq"), lax.axis_index("mp")
    marks = query_marks(row_at(iota((ROWS, LANES), 0)) + seq * ROWS, ends)
    near_marks = marks_near(seq, ends, (1, 3))
    for head in range(LOCAL_HEADS):
        key_tile, value_tile = tile(KEY_TILE[head]), tile(VALUE_TILE[head])
        asked = head_lanes(query[:, tile(QUERY_TILE[head])], head)
        peak, more = attend(
            jnp.concatenate([asked, marks], 1),
            jnp.concatenate([swapped[: 2 * ROWS, key_tile], near_marks], 1),
            jnp.concatenate([swapped[: 2 * ROWS, value_tile], near_marks], 1),
            head,
        )
        state[head][...] = join(held[head][...], more, peak, head)

        offset = (mp * LOCAL_HEADS + head) & 3
        start = pl.multiple_of(offset * CLASS_ROWS, CLASS_ROWS)
        picked = pl.ds(start, CLASS_ROWS)
        place = iota((CLASS_ROWS, LANES), 0)
        class_rows = offset + RATE_MID * ((place >> 4) + ((place & 15) << 3))
        class_marks = jnp.concatenate(
            [key_marks(class_rows + (seq ^ step) * ROWS, ends) for step in (0, 2, 1, 3, 4, 6, 5, 7)],
            0,
        )
        asked = head_lanes(query[picked, tile(QUERY_TILE[head])], head)
        asked = jnp.concatenate([asked, query_marks(class_rows + seq * ROWS, ends)], 1)

        def gathered(lanes):
            return jnp.concatenate(
                [
                    own[picked, lanes],
                    side[picked, lanes],
                    swapped[picked, lanes],
                    swapped[pl.ds(start + ROWS, CLASS_ROWS), lanes],
                    mid_a[:, lanes],
                    mid_b[:, lanes],
                    swapped[2 * ROWS :, lanes],
                ],
                0,
            )

        peak, more = attend(
            asked,
            jnp.concatenate([gathered(key_tile), class_marks], 1),
            jnp.concatenate([gathered(value_tile), class_marks], 1),
            head,
        )
        state[head][picked, :] = join(state[head][picked, :], more, peak, head)
    far_parts = []
    for head in range(LOCAL_HEADS):
        spare = SPARE[head]
        pieces = [parts[index, :, tile(head)] for index in range(FAR_GROUP)]
        tops = [piece[:, spare : spare + 1] for piece in pieces]
        peak = functools.reduce(jnp.maximum, tops)
        total = jnp.zeros((FAR_ROWS, LANES), jnp.float32)
        for piece, top in zip(pieces, tops):
            total = total + piece * jnp.exp(top - peak)
        far_parts.append(total / total[:, spare + 1 : spare + 2])
        number = mp * LOCAL_HEADS + head
        start = (number & 3) * CLASS_ROWS + (number >> 2) * FAR_ROWS
        picked = pl.ds(pl.multiple_of(start, FAR_ROWS), FAR_ROWS)
        state[head][picked, :] = join(state[head][picked, :], total, peak, head)

    def packed(values):
        first = jnp.where(iota(values[0].shape, 1) < HEAD_DIM, values[0], values[1])
        return first.astype(jnp.bfloat16), values[2].astype(jnp.bfloat16)

    first, last = packed(far_parts)
    far_out[:, :128] = first
    far_out[:, 128:] = last[:, HEAD_DIM:]
    row = (iota((ROWS, ROWS), 0) + mp * BLOCK) & (ROWS - 1)
    back = (place_of(row) == iota((ROWS, ROWS), 1)).astype(jnp.bfloat16)
    first, last = packed(
        [
            state[head][...] / state[head][:, SPARE[head] + 1 : SPARE[head] + 2]
            for head in range(LOCAL_HEADS)
        ]
    )
    mixed = jnp.concatenate([first, last[:, HEAD_DIM:]], 1)
    mixed = matmul(back, mixed).astype(jnp.bfloat16)
    for index, term in enumerate(terms):
        part = mixed[index * BLOCK : (index + 1) * BLOCK]
        term[...] = matmul(part, w_out[...]).astype(jnp.bfloat16)


def far_kernel(tiles, rows, here, other, parts):
    ends = slide_ends(tiles)
    seq, mp = lax.axis_index("seq"), lax.axis_index("mp")
    count = FAR_GROUP * FAR_ROWS
    shape = (count, 2 * count)

    def position(place, holder):
        return holder * ROWS + (place & 15) * RATE_FAR

    at = iota(shape, 1)
    core = (seq & 1) ^ (at >> 7)
    key_at = position(at, (seq & 112) + ((at >> 4) & 7) * 2 + core)
    at = iota(shape, 0)
    query_at = position(at, (at >> 4) * 16 + (seq & 15))
    lane = iota((count, LANES), 1)

    def flat(ref, lanes):
        return ref[:, :, lanes].reshape(count, LANES)

    for head in range(LOCAL_HEADS):
        number = mp * LOCAL_HEADS + head
        key_tile, value_tile = tile(KEY_TILE[head]), tile(VALUE_TILE[head])
        asked = rows[:, :, tile(QUERY_TILE[head])].reshape(count, LANES)
        asked = head_lanes(asked, head)
        scores = matmul_t(asked, jnp.concatenate([flat(here, key_tile), flat(other, key_tile)], 0))
        same = slide_of(query_at + number, ends) == slide_of(key_at + number, ends)
        scores = jnp.where(same, scores, HIDDEN_SCORE)
        peak = jnp.max(scores, -1, keepdims=True)
        weights = jnp.exp(scores - peak)
        total = jnp.sum(weights, -1, keepdims=True)
        values = jnp.concatenate([flat(here, value_tile), flat(other, value_tile)], 0)
        part = matmul(weights.astype(jnp.bfloat16), values)
        part = pack(part, peak, total, head, lane)
        parts[:, :, tile(head)] = part.reshape(FAR_GROUP, FAR_ROWS, LANES)


def weights_kernel(w_up, w_down, out):
    start = pl.multiple_of((lax.axis_index("seq") & 1) * HALF, HALF)
    out[:HALF, :HALF] = w_up[:HALF, pl.ds(start, HALF)]
    out[:HALF, HALF:] = w_up[HALF:, pl.ds(start, HALF)]
    out[HALF:, :] = w_down[pl.ds(start, HALF), :]


def hidden_part(normed, weights):
    raised = matmul(normed[:, :HALF], weights[:HALF, :HALF])
    raised = raised + matmul(normed[:, HALF:], weights[:HALF, HALF:])
    hidden = (0.5 * raised * (1.0 + lax.erf(raised * 0.7071067811865476))).astype(jnp.bfloat16)
    return matmul(hidden, weights[HALF:, :])


def norm_kernel(tokens, gain, *refs):
    terms, attended, normed = refs[:4], refs[4], refs[5]
    summed = terms[0][...].astype(jnp.float32)
    for term in terms[1:]:
        summed = summed + term[...].astype(jnp.float32)
    summed = summed.astype(jnp.bfloat16)
    attended[...] = summed
    start = pl.multiple_of(lax.axis_index("mp") * BLOCK, BLOCK)
    own = tokens[pl.ds(start, BLOCK), :].astype(jnp.float32)
    normed[...] = layer_norm(own + summed.astype(jnp.float32), gain[...])


def ffn_kernel(own, other, weights, kept, sent):
    rows = jnp.concatenate([own[...], other[...]], 0)
    total = jnp.zeros((2 * BLOCK, WIDTH), jnp.float32)
    for group in range(4):
        total = total + hidden_part(rows, weights.at[group])
    kept[...] = total[:BLOCK, :]
    sent[...] = total[BLOCK:, :].astype(jnp.bfloat16)


def call(kernel, micros, outs, ins, scratch=(), limit=VMEM):
    places = {"smem": pltpu.SMEM, "vmem": pltpu.VMEM, "hbm": pltpu.HBM}
    return pl.pallas_call(
        kernel,
        out_shape=[jax.ShapeDtypeStruct(*out) for out in outs],
        in_specs=[pl.BlockSpec(memory_space=places[where]) for _, where in ins],
        out_specs=[pl.BlockSpec(memory_space=pltpu.VMEM) for _ in outs],
        scratch_shapes=list(scratch),
        cost_estimate=pl.CostEstimate(
            flops=int(micros * 1.1e9), bytes_accessed=int(micros * 1e6), transcendentals=0
        ),
        compiler_params=pltpu.CompilerParams(vmem_limit_bytes=limit),
    )(*[array for array, _ in ins])


def swap(value, step):
    return lax.ppermute(value, "seq", [(i, i ^ step) for i in range(lax.axis_size("seq"))])


def local(tokens, slide_tiles, attn_gain, w_query, w_key, w_value, w_out, ffn_gain, w_up, w_down):
    bf16, f32 = jnp.bfloat16, jnp.float32
    v, s, h = "vmem", "smem", "hbm"
    dma = pltpu.SemaphoreType.DMA
    columns = [[16 * z + place for z in range(FAR_GROUP)] for place in range(16)]
    planes = [
        [16 * z + 2 * y + core for y in range(FAR_GROUP)] for z in range(FAR_GROUP) for core in range(2)
    ]

    def to_all(value, groups):
        return lax.all_to_all(
            value, "seq", split_axis=0, concat_axis=0, tiled=True, axis_index_groups=groups
        )

    w_query, w_key, w_value = w_query.T, w_key.T, w_value.T
    query, own, mid, far_query, far_keyval = call(
        project_kernel,
        3,
        [
            ((ROWS, 256), bf16), ((ROWS, 384), bf16), ((CLASS_ROWS, 384), bf16),
            ((FAR_GROUP, FAR_ROWS, 256), bf16), ((FAR_GROUP, FAR_ROWS, 384), bf16),
        ],
        [(tokens, h), (attn_gain, v), (w_query, h), (w_key, h), (w_value, h)],
        [pltpu.VMEM((ROWS, WIDTH), bf16), pltpu.VMEM((3, 192, WIDTH), bf16), dma((7,))],
        limit=WHOLE_VMEM,
    )
    far_here = to_all(far_keyval, planes)
    far_query, _ = lax.optimization_barrier((far_query, far_here))
    far_rows = to_all(far_query, columns)
    w_up, w_down, _ = lax.optimization_barrier((w_up, w_down, far_keyval))
    (packed,) = call(weights_kernel, 2, [((2 * HALF, WIDTH), bf16)], [(w_up, v), (w_down, v)])
    mine = lax.all_gather(packed, "mp", axis=0)
    side = swap(own, 2)

    mid_a, mid_b = swap(mid, 4), swap(mid, 6)
    state = [((ROWS, LANES), f32)] * LOCAL_HEADS
    query, side, mid_a, mid_b, _, _ = lax.optimization_barrier(
        (query, side, mid_a, mid_b, far_here, far_rows)
    )
    near = call(near_kernel, 3, state, [(slide_tiles, s), (query, v), (own, v), (side, v)])
    far_other = swap(far_here, 1)
    far_other, *near = lax.optimization_barrier((far_other, *near))
    swapped = swap(jnp.concatenate([own, side, mid_a, mid_b], 0), 1)
    (parts,) = call(
        far_kernel,
        2,
        [((FAR_GROUP, FAR_ROWS, 384), f32)],
        [(slide_tiles, s), (far_rows, v), (far_here, v), (far_other, v)],
    )
    parts = to_all(parts, columns)
    *terms, far_attended = call(
        rest_kernel,
        7,
        [((BLOCK, WIDTH), bf16)] * 4 + [((FAR_ROWS, 192), bf16)],
        [
            (slide_tiles, s), (query, v), (own, v), (side, v), (mid_a, v), (mid_b, v), (swapped, v),
            (parts, v), (w_out, v), *[(held, v) for held in near],
        ],
        [pltpu.VMEM(*shape) for shape in state],
    )
    for step in (2, 1, 3):
        terms[step] = lax.ppermute(terms[step], "mp", [(i, (i + step) % 4) for i in range(4)])
    terms[2], mine = lax.optimization_barrier((terms[2], mine))
    terms = lax.optimization_barrier(terms)
    attended, normed = call(
        norm_kernel,
        1,
        [((BLOCK, WIDTH), bf16), ((BLOCK, WIDTH), bf16)],
        [(tokens, v), (ffn_gain, v), *[(term, v) for term in terms]],
    )
    kept, sent = call(
        ffn_kernel,
        4,
        [((BLOCK, WIDTH), f32), ((BLOCK, WIDTH), bf16)],
        [(normed, v), (swap(normed, 1), v), (mine, v)],
    )
    ffn_out = (kept + swap(sent, 1).astype(f32)).astype(bf16)
    return (attended, far_attended, ffn_out)


def solution(mesh):
    return jax.shard_map(
        local,
        mesh=mesh,
        in_specs=(
            P("seq", None),
            P(),
            P(),
            P(None, "mp"),
            P(None, "mp"),
            P(None, "mp"),
            P("mp", None),
            P(),
            P(None, "mp"),
            P("mp", None),
        ),
        out_specs=(P(("seq", "mp"), None), P("seq", "mp"), P(("seq", "mp"), None)),
        check_vma=False,
    )
```

```python
import functools

import jax
import jax.numpy as jnp
from jax import lax
from jax.experimental import pallas as pl
from jax.experimental.pallas import tpu as pltpu
from jax.sharding import PartitionSpec as P

HEAD_DIM = 64
LOCAL_HEADS = 3
RATE_MID = 4
RATE_FAR = 32
ROWS = 512
CLASS_ROWS = ROWS // RATE_MID
FAR_ROWS = ROWS // RATE_FAR
LANES = 128
SLIDES = 4
WIDTH = 768
HALF = WIDTH // 2
BLOCK = 128
EPS = 1e-05
HIDDEN_SCORE = -1e30
VMEM = 16 * 1024 * 1024
WHOLE_VMEM = 58 * 1024 * 1024

KEY_TILE = (0, 0, 2)
VALUE_TILE = (1, 1, 2)
QUERY_TILE = (0, 0, 1)
SPARE = (64, 0, 0)
FAR_GROUP = 8


def iota(shape, dim):
    return lax.broadcasted_iota(jnp.int32, shape, dim)


def place_of(row):
    return (row & 3) * CLASS_ROWS + ((row >> 2) & 7) * FAR_ROWS + (row >> 5)


def row_at(place):
    return (place & 15) * RATE_FAR + ((place >> 4) & 7) * RATE_MID + (place >> 7)


def layer_norm(as_float, gain):
    mean_val = jnp.mean(as_float, -1, keepdims=True)
    centered = as_float - mean_val
    variance = jnp.mean(centered * centered, -1, keepdims=True)
    return (centered * lax.rsqrt(variance + EPS) * gain.astype(jnp.float32)).astype(jnp.bfloat16)


def matmul(left, right):
    return jnp.dot(left, right, preferred_element_type=jnp.float32)


def matmul_t(left, right):
    return lax.dot_general(
        left, right, (((1,), (1,)), ((), ())), preferred_element_type=jnp.float32
    )


def slide_of(positions, ends):
    index = (positions >= ends[0]).astype(jnp.int32)
    for end in ends[1:]:
        index = index + (positions >= end).astype(jnp.int32)
    return index


def slide_ends(tiles_ref):
    ends = [tiles_ref[0]]
    for slide in range(1, SLIDES - 1):
        ends.append(ends[-1] + tiles_ref[slide])
    return ends


def query_marks(positions, ends):
    rows = positions.shape[0]
    lane = iota((rows, LANES), 1)
    return (lane == slide_of(positions, ends)).astype(jnp.bfloat16)


def key_marks(positions, ends):
    rows = positions.shape[0]
    lane = iota((rows, LANES), 1)
    hide = (lane < SLIDES) & (lane != slide_of(positions, ends))
    marks = jnp.where(hide, HIDDEN_SCORE, jnp.where(lane == SLIDES, 1.0, 0.0))
    return marks.astype(jnp.bfloat16)


def head_lanes(value, head):
    lane = iota(value.shape, 1)
    keep = lane < HEAD_DIM if head != 1 else lane >= HEAD_DIM
    return jnp.where(keep, value, jnp.zeros_like(value))


def tile(index):
    return slice(index * LANES, (index + 1) * LANES)


def project(normed, w_query, w_key, w_value):
    asked = (matmul_t(normed, w_query[...]) * (1.0 / 8.0)).astype(jnp.bfloat16)
    key = matmul_t(normed, w_key[...]).astype(jnp.bfloat16)
    value = matmul_t(normed, w_value[...]).astype(jnp.bfloat16)
    none = jnp.zeros_like(asked[:, 128:])
    queries = [asked[:, :128], jnp.concatenate([asked[:, 128:], none], 1)]
    keyvals = [key[:, :128], value[:, :128]]
    return queries, keyvals + [jnp.concatenate([key[:, 128:], value[:, 128:]], 1)]


def project_kernel(
    tokens, gain, w_query, w_key, w_value, query, keyval, mid, far, rows, weights, sems
):
    mp = lax.axis_index("mp")
    copies = []
    for index in range(4):
        part = pl.ds(index * BLOCK, BLOCK)
        copies.append(pltpu.make_async_copy(tokens.at[part], rows.at[part], sems.at[index]))
    for index, weight in enumerate((w_query, w_key, w_value)):
        copies.append(pltpu.make_async_copy(weight, weights.at[index], sems.at[4 + index]))
    for copy in copies:
        copy.start()
    for copy in copies[:4]:
        copy.wait()
    normed = layer_norm(rows[...].astype(jnp.float32), gain[...])
    order = iota((ROWS, ROWS), 0) == place_of(iota((ROWS, ROWS), 1))
    normed = matmul(order.astype(jnp.bfloat16), normed).astype(jnp.bfloat16)
    for copy in copies[4:]:
        copy.wait()
    queries, keyvals = project(normed, *[weights.at[index] for index in range(3)])
    for index, value in enumerate(queries):
        query[:, tile(index)] = value
    for index, value in enumerate(keyvals):
        keyval[:, tile(index)] = value

    def pick(source, index, whose, count):
        starts = []
        for head in range(LOCAL_HEADS):
            number = mp * LOCAL_HEADS + head
            start = (number & 3) * CLASS_ROWS
            if count == FAR_ROWS:
                start = start + (number >> 2) * FAR_ROWS
            starts.append(pl.ds(pl.multiple_of(start, count), count))
        if whose[2] == index:
            return source[starts[2], tile(index)]
        low, high = source[starts[0], tile(index)], source[starts[1], tile(index)]
        return jnp.where(iota(low.shape, 1) < HEAD_DIM, low, high)

    for index in range(3):
        mid[:, tile(index)] = pick(keyval, index, KEY_TILE, CLASS_ROWS)
    picked = [pick(query, index, QUERY_TILE, FAR_ROWS) for index in range(2)]
    picked += [pick(keyval, index, KEY_TILE, FAR_ROWS) for index in range(3)]
    for index, value in enumerate(picked):
        for copy in range(FAR_GROUP):
            far[copy, :, tile(index)] = value


def attend(query, keys, values, head):
    scores = matmul_t(query, keys)
    peak = jnp.max(scores, -1, keepdims=True)
    weights = jnp.exp(scores - peak).astype(jnp.bfloat16)
    sums = matmul(weights, values)
    lane = iota((sums.shape[0], LANES), 1)
    total = sums[:, LANES + SLIDES : LANES + SLIDES + 1]
    return peak, pack(sums[:, :LANES], peak, total, head, lane)


def pack(sums, peak, total, head, lane):
    return jnp.where(
        lane == SPARE[head], peak, jnp.where(lane == SPARE[head] + 1, total, sums)
    )


def join(held, more, peak, head):
    spare = SPARE[head]
    before = held[:, spare : spare + 1]
    largest = jnp.maximum(before, peak)
    both = held * jnp.exp(before - largest) + more * jnp.exp(peak - largest)
    return jnp.where(iota(both.shape, 1) == spare, largest, both)


def marks_near(seq, ends, steps):
    rows = row_at(iota((ROWS, LANES), 0))
    return jnp.concatenate([key_marks(rows + (seq ^ step) * ROWS, ends) for step in steps], 0)


def near_kernel(tiles, query, own, side, *state):
    ends = slide_ends(tiles)
    seq = lax.axis_index("seq")
    marks = query_marks(row_at(iota((ROWS, LANES), 0)) + seq * ROWS, ends)
    keys_marks = marks_near(seq, ends, (0, 2))
    for head in range(LOCAL_HEADS):
        key_tile, value_tile = tile(KEY_TILE[head]), tile(VALUE_TILE[head])
        asked = head_lanes(query[:, tile(QUERY_TILE[head])], head)
        keys = jnp.concatenate([own[:, key_tile], side[:, key_tile]], 0)
        values = jnp.concatenate([own[:, value_tile], side[:, value_tile]], 0)
        _, state[head][...] = attend(
            jnp.concatenate([asked, marks], 1),
            jnp.concatenate([keys, keys_marks], 1),
            jnp.concatenate([values, keys_marks], 1),
            head,
        )


def rest_kernel(tiles, query, own, side, mid_a, mid_b, swapped, parts, w_out, *refs):
    n = LOCAL_HEADS
    held, (terms, far_out), state = refs[:n], refs[n : n + 2], refs[n + 2 :]
    ends = slide_ends(tiles)
    seq, mp = lax.axis_index("seq"), lax.axis_index("mp")
    marks = query_marks(row_at(iota((ROWS, LANES), 0)) + seq * ROWS, ends)
    near_marks = marks_near(seq, ends, (1, 3))
    for head in range(LOCAL_HEADS):
        key_tile, value_tile = tile(KEY_TILE[head]), tile(VALUE_TILE[head])
        asked = head_lanes(query[:, tile(QUERY_TILE[head])], head)
        peak, more = attend(
            jnp.concatenate([asked, marks], 1),
            jnp.concatenate([swapped[: 2 * ROWS, key_tile], near_marks], 1),
            jnp.concatenate([swapped[: 2 * ROWS, value_tile], near_marks], 1),
            head,
        )
        state[head][...] = join(held[head][...], more, peak, head)

        offset = (mp * LOCAL_HEADS + head) & 3
        start = pl.multiple_of(offset * CLASS_ROWS, CLASS_ROWS)
        picked = pl.ds(start, CLASS_ROWS)
        place = iota((CLASS_ROWS, LANES), 0)
        class_rows = offset + RATE_MID * ((place >> 4) + ((place & 15) << 3))
        class_marks = jnp.concatenate(
            [key_marks(class_rows + (seq ^ step) * ROWS, ends) for step in (0, 2, 1, 3, 4, 6, 5, 7)],
            0,
        )
        asked = head_lanes(query[picked, tile(QUERY_TILE[head])], head)
        asked = jnp.concatenate([asked, query_marks(class_rows + seq * ROWS, ends)], 1)

        def gathered(lanes):
            return jnp.concatenate(
                [
                    own[picked, lanes],
                    side[picked, lanes],
                    swapped[picked, lanes],
                    swapped[pl.ds(start + ROWS, CLASS_ROWS), lanes],
                    mid_a[:, lanes],
                    mid_b[:, lanes],
                    swapped[2 * ROWS :, lanes],
                ],
                0,
            )

        peak, more = attend(
            asked,
            jnp.concatenate([gathered(key_tile), class_marks], 1),
            jnp.concatenate([gathered(value_tile), class_marks], 1),
            head,
        )
        state[head][picked, :] = join(state[head][picked, :], more, peak, head)
    far_parts = []
    for head in range(LOCAL_HEADS):
        spare = SPARE[head]
        pieces = [parts[index, :, tile(head)] for index in range(FAR_GROUP)]
        tops = [piece[:, spare : spare + 1] for piece in pieces]
        peak = functools.reduce(jnp.maximum, tops)
        total = jnp.zeros((FAR_ROWS, LANES), jnp.float32)
        for piece, top in zip(pieces, tops):
            total = total + piece * jnp.exp(top - peak)
        far_parts.append(total / total[:, spare + 1 : spare + 2])
        number = mp * LOCAL_HEADS + head
        start = (number & 3) * CLASS_ROWS + (number >> 2) * FAR_ROWS
        picked = pl.ds(pl.multiple_of(start, FAR_ROWS), FAR_ROWS)
        state[head][picked, :] = join(state[head][picked, :], total, peak, head)

    def packed(values):
        first = jnp.where(iota(values[0].shape, 1) < HEAD_DIM, values[0], values[1])
        return first.astype(jnp.bfloat16), values[2].astype(jnp.bfloat16)

    first, last = packed(far_parts)
    far_out[:, :128] = first
    far_out[:, 128:] = last[:, HEAD_DIM:]
    back = (place_of(iota((ROWS, ROWS), 0)) == iota((ROWS, ROWS), 1)).astype(jnp.bfloat16)
    first, last = packed(
        [
            state[head][...] / state[head][:, SPARE[head] + 1 : SPARE[head] + 2]
            for head in range(LOCAL_HEADS)
        ]
    )
    mixed = jnp.concatenate([first, last[:, HEAD_DIM:]], 1)
    mixed = matmul(back, mixed).astype(jnp.bfloat16)
    terms[...] = matmul(mixed, w_out[...]).astype(jnp.bfloat16).reshape(4, BLOCK, WIDTH)


def far_kernel(tiles, rows, here, other, parts):
    ends = slide_ends(tiles)
    seq, mp = lax.axis_index("seq"), lax.axis_index("mp")
    column = seq & 15
    beside = ((((seq >> 4) - (column >> 1)) & 7) << 1) + (column & 1)
    count = FAR_GROUP * FAR_ROWS
    shape = (count, 2 * count)

    def position(place, holder):
        return ((place >> 4) * 16 + holder) * ROWS + (place & 15) * RATE_FAR

    at = iota(shape, 1)
    holder = jnp.where(at < count, beside, beside ^ 1)
    key_at = position(at & (count - 1), holder)
    query_at = position(iota(shape, 0), column)
    lane = iota((count, LANES), 1)
    for head in range(LOCAL_HEADS):
        number = mp * LOCAL_HEADS + head
        key_tile, value_tile = tile(KEY_TILE[head]), tile(VALUE_TILE[head])
        asked = rows[:, :, tile(QUERY_TILE[head])].reshape(count, LANES)
        asked = head_lanes(asked, head)
        scores = matmul_t(asked, jnp.concatenate([here[:, key_tile], other[:, key_tile]], 0))
        same = slide_of(query_at + number, ends) == slide_of(key_at + number, ends)
        scores = jnp.where(same, scores, HIDDEN_SCORE)
        peak = jnp.max(scores, -1, keepdims=True)
        weights = jnp.exp(scores - peak)
        total = jnp.sum(weights, -1, keepdims=True)
        values = jnp.concatenate([here[:, value_tile], other[:, value_tile]], 0)
        part = matmul(weights.astype(jnp.bfloat16), values)
        part = pack(part, peak, total, head, lane)
        parts[:, :, tile(head)] = part.reshape(FAR_GROUP, FAR_ROWS, LANES)


def weights_kernel(w_up, w_down, out):
    start = pl.multiple_of((lax.axis_index("seq") & 1) * HALF, HALF)
    out[:HALF, :HALF] = w_up[:HALF, pl.ds(start, HALF)]
    out[:HALF, HALF:] = w_up[HALF:, pl.ds(start, HALF)]
    out[HALF:, :] = w_down[pl.ds(start, HALF), :]


def hidden_part(normed, weights):
    raised = matmul(normed[:, :HALF], weights[:HALF, :HALF])
    raised = raised + matmul(normed[:, HALF:], weights[:HALF, HALF:])
    hidden = (0.5 * raised * (1.0 + lax.erf(raised * 0.7071067811865476))).astype(jnp.bfloat16)
    return matmul(hidden, weights[HALF:, :])


def norm_kernel(tokens, terms, gain, attended, normed):
    summed = terms[0].astype(jnp.float32)
    for group in range(1, 4):
        summed = summed + terms[group].astype(jnp.float32)
    summed = summed.astype(jnp.bfloat16)
    attended[...] = summed
    start = pl.multiple_of(lax.axis_index("mp") * BLOCK, BLOCK)
    own = tokens[pl.ds(start, BLOCK), :].astype(jnp.float32)
    normed[...] = layer_norm(own + summed.astype(jnp.float32), gain[...])


def ffn_kernel(own, other, weights, kept, sent):
    rows = jnp.concatenate([own[...], other[...]], 0)
    total = jnp.zeros((2 * BLOCK, WIDTH), jnp.float32)
    for group in range(4):
        total = total + hidden_part(rows, weights.at[group])
    kept[...] = total[:BLOCK, :]
    sent[...] = total[BLOCK:, :].astype(jnp.bfloat16)


def call(kernel, micros, outs, ins, scratch=(), limit=VMEM):
    places = {"smem": pltpu.SMEM, "vmem": pltpu.VMEM, "hbm": pltpu.HBM}
    return pl.pallas_call(
        kernel,
        out_shape=[jax.ShapeDtypeStruct(*out) for out in outs],
        in_specs=[pl.BlockSpec(memory_space=places[where]) for _, where in ins],
        out_specs=[pl.BlockSpec(memory_space=pltpu.VMEM) for _ in outs],
        scratch_shapes=list(scratch),
        cost_estimate=pl.CostEstimate(
            flops=int(micros * 1.1e9), bytes_accessed=int(micros * 1e6), transcendentals=0
        ),
        compiler_params=pltpu.CompilerParams(vmem_limit_bytes=limit),
    )(*[array for array, _ in ins])


def swap(value, step):
    return lax.ppermute(value, "seq", [(i, i ^ step) for i in range(lax.axis_size("seq"))])


def local(tokens, slide_tiles, attn_gain, w_query, w_key, w_value, w_out, ffn_gain, w_up, w_down):
    bf16, f32 = jnp.bfloat16, jnp.float32
    v, s, h = "vmem", "smem", "hbm"
    dma = pltpu.SemaphoreType.DMA
    columns = [[16 * z + place for z in range(FAR_GROUP)] for place in range(16)]
    across = [
        (16 * z + 2 * ((z - y) % 8) + core, 16 * z + 2 * y + core)
        for z in range(FAR_GROUP)
        for y in range(8)
        for core in range(2)
    ]
    w_query, w_key, w_value = w_query.T, w_key.T, w_value.T
    query, own, mid, far = call(
        project_kernel,
        3,
        [
            ((ROWS, 256), bf16), ((ROWS, 384), bf16), ((CLASS_ROWS, 384), bf16),
            ((FAR_GROUP, FAR_ROWS, 640), bf16),
        ],
        [(tokens, h), (attn_gain, v), (w_query, h), (w_key, h), (w_value, h)],
        [pltpu.VMEM((ROWS, WIDTH), bf16), pltpu.VMEM((3, 192, WIDTH), bf16), dma((7,))],
        limit=WHOLE_VMEM,
    )
    far_rows = lax.all_to_all(
        far, "seq", split_axis=0, concat_axis=0, tiled=True, axis_index_groups=columns
    )
    w_up, w_down, _ = lax.optimization_barrier((w_up, w_down, far))
    (packed,) = call(weights_kernel, 2, [((2 * HALF, WIDTH), bf16)], [(w_up, v), (w_down, v)])
    mine = lax.all_gather(packed, "mp", axis=0)
    side = swap(own, 2)

    far_keys = far_rows[:, :, 256:].reshape(128, 384)
    far_here = lax.ppermute(far_keys, "seq", across)
    query, _ = lax.optimization_barrier((query, far_keys))
    mid_a, mid_b = swap(mid, 4), swap(mid, 6)
    state = [((ROWS, LANES), f32)] * LOCAL_HEADS
    near = call(near_kernel, 3, state, [(slide_tiles, s), (query, v), (own, v), (side, v)])
    far_here, *near = lax.optimization_barrier((far_here, *near))
    far_other = swap(far_here, 1)
    side, mid_a, mid_b, far_other = lax.optimization_barrier((side, mid_a, mid_b, far_other))
    swapped = swap(jnp.concatenate([own, side, mid_a, mid_b], 0), 1)
    (parts,) = call(
        far_kernel,
        2,
        [((FAR_GROUP, FAR_ROWS, 384), f32)],
        [(slide_tiles, s), (far_rows, v), (far_here, v), (far_other, v)],
    )
    parts = lax.all_to_all(
        parts, "seq", split_axis=0, concat_axis=0, tiled=True, axis_index_groups=columns
    )
    terms, far_attended = call(
        rest_kernel,
        7,
        [((4, BLOCK, WIDTH), bf16), ((FAR_ROWS, 192), bf16)],
        [
            (slide_tiles, s), (query, v), (own, v), (side, v), (mid_a, v), (mid_b, v), (swapped, v),
            (parts, v), (w_out, v), *[(held, v) for held in near],
        ],
        [pltpu.VMEM(*shape) for shape in state],
    )
    terms = lax.all_to_all(terms, "mp", split_axis=0, concat_axis=0, tiled=True)
    terms, mine = lax.optimization_barrier((terms, mine))
    attended, normed = call(
        norm_kernel,
        1,
        [((BLOCK, WIDTH), bf16), ((BLOCK, WIDTH), bf16)],
        [(tokens, v), (terms, v), (ffn_gain, v)],
    )
    kept, sent = call(
        ffn_kernel,
        4,
        [((BLOCK, WIDTH), f32), ((BLOCK, WIDTH), bf16)],
        [(normed, v), (swap(normed, 1), v), (mine, v)],
    )
    ffn_out = (kept + swap(sent, 1).astype(f32)).astype(bf16)
    return (attended, far_attended, ffn_out)


def solution(mesh):
    return jax.shard_map(
        local,
        mesh=mesh,
        in_specs=(
            P("seq", None),
            P(),
            P(),
            P(None, "mp"),
            P(None, "mp"),
            P(None, "mp"),
            P("mp", None),
            P(),
            P(None, "mp"),
            P("mp", None),
        ),
        out_specs=(P(("seq", "mp"), None), P("seq", "mp"), P(("seq", "mp"), None)),
        check_vma=False,
    )
```

```python
import functools

import jax
import jax.numpy as jnp
from jax import lax
from jax.experimental import pallas as pl
from jax.experimental.pallas import tpu as pltpu
from jax.sharding import PartitionSpec as P

HEAD_DIM = 64
LOCAL_HEADS = 3
RATE_MID = 4
RATE_FAR = 32
ROWS = 512
CLASS_ROWS = ROWS // RATE_MID
FAR_ROWS = ROWS // RATE_FAR
LANES = 128
SLIDES = 4
WIDTH = 768
HALF = WIDTH // 2
BLOCK = 128
EPS = 1e-05
HIDDEN_SCORE = -1e30
VMEM = 16 * 1024 * 1024
WHOLE_VMEM = 58 * 1024 * 1024

KEY_TILE = (0, 0, 2)
VALUE_TILE = (1, 1, 2)
QUERY_TILE = (0, 0, 1)
SPARE = (64, 0, 0)
FAR_GROUP = 8


def iota(shape, dim):
    return lax.broadcasted_iota(jnp.int32, shape, dim)


def place_of(row):
    return (row & 3) * CLASS_ROWS + ((row >> 2) & 7) * FAR_ROWS + (row >> 5)


def row_at(place):
    return (place & 15) * RATE_FAR + ((place >> 4) & 7) * RATE_MID + (place >> 7)


def layer_norm(as_float, gain):
    mean_val = jnp.mean(as_float, -1, keepdims=True)
    centered = as_float - mean_val
    variance = jnp.mean(centered * centered, -1, keepdims=True)
    return (centered * lax.rsqrt(variance + EPS) * gain.astype(jnp.float32)).astype(jnp.bfloat16)


def matmul(left, right):
    return jnp.dot(left, right, preferred_element_type=jnp.float32)


def matmul_t(left, right):
    return lax.dot_general(
        left, right, (((1,), (1,)), ((), ())), preferred_element_type=jnp.float32
    )


def slide_of(positions, ends):
    index = (positions >= ends[0]).astype(jnp.int32)
    for end in ends[1:]:
        index = index + (positions >= end).astype(jnp.int32)
    return index


def slide_ends(tiles_ref):
    ends = [tiles_ref[0]]
    for slide in range(1, SLIDES - 1):
        ends.append(ends[-1] + tiles_ref[slide])
    return ends


def query_marks(positions, ends):
    rows = positions.shape[0]
    lane = iota((rows, LANES), 1)
    return (lane == slide_of(positions, ends)).astype(jnp.bfloat16)


def key_marks(positions, ends):
    rows = positions.shape[0]
    lane = iota((rows, LANES), 1)
    hide = (lane < SLIDES) & (lane != slide_of(positions, ends))
    marks = jnp.where(hide, HIDDEN_SCORE, jnp.where(lane == SLIDES, 1.0, 0.0))
    return marks.astype(jnp.bfloat16)


def head_lanes(value, head):
    lane = iota(value.shape, 1)
    keep = lane < HEAD_DIM if head != 1 else lane >= HEAD_DIM
    return jnp.where(keep, value, jnp.zeros_like(value))


def tile(index):
    return slice(index * LANES, (index + 1) * LANES)


def project(normed, w_query, w_key, w_value):
    asked = (matmul_t(normed, w_query[...]) * (1.0 / 8.0)).astype(jnp.bfloat16)
    key = matmul_t(normed, w_key[...]).astype(jnp.bfloat16)
    value = matmul_t(normed, w_value[...]).astype(jnp.bfloat16)
    none = jnp.zeros_like(asked[:, 128:])
    queries = [asked[:, :128], jnp.concatenate([asked[:, 128:], none], 1)]
    keyvals = [key[:, :128], value[:, :128]]
    return queries, keyvals + [jnp.concatenate([key[:, 128:], value[:, 128:]], 1)]


def project_kernel(
    tokens, gain, w_query, w_key, w_value, query, keyval, mid, far, rows, weights, sems
):
    mp = lax.axis_index("mp")
    copies = [pltpu.make_async_copy(tokens, rows, sems.at[0])]
    for index, weight in enumerate((w_key, w_value, w_query)):
        copies.append(pltpu.make_async_copy(weight, weights.at[index], sems.at[1 + index]))
    for copy in copies:
        copy.start()
    copies[0].wait()
    normed = layer_norm(rows[...].astype(jnp.float32), gain[...])
    order = iota((ROWS, ROWS), 0) == place_of(iota((ROWS, ROWS), 1))
    normed = matmul(order.astype(jnp.bfloat16), normed).astype(jnp.bfloat16)
    for copy in copies[1:]:
        copy.wait()
    queries, keyvals = project(normed, *[weights.at[index] for index in (2, 0, 1)])
    for index, value in enumerate(queries):
        query[:, tile(index)] = value
    for index, value in enumerate(keyvals):
        keyval[:, tile(index)] = value

    def pick(source, index, whose, count):
        starts = []
        for head in range(LOCAL_HEADS):
            number = mp * LOCAL_HEADS + head
            start = (number & 3) * CLASS_ROWS
            if count == FAR_ROWS:
                start = start + (number >> 2) * FAR_ROWS
            starts.append(pl.ds(pl.multiple_of(start, count), count))
        if whose[2] == index:
            return source[starts[2], tile(index)]
        low, high = source[starts[0], tile(index)], source[starts[1], tile(index)]
        return jnp.where(iota(low.shape, 1) < HEAD_DIM, low, high)

    for index in range(3):
        mid[:, tile(index)] = pick(keyval, index, KEY_TILE, CLASS_ROWS)
    picked = [pick(query, index, QUERY_TILE, FAR_ROWS) for index in range(2)]
    picked += [pick(keyval, index, KEY_TILE, FAR_ROWS) for index in range(3)]
    for index, value in enumerate(picked):
        for copy in range(FAR_GROUP):
            far[copy, :, tile(index)] = value


def attend(query, keys, values, head):
    scores = matmul_t(query, keys)
    peak = jnp.max(scores, -1, keepdims=True)
    weights = jnp.exp(scores - peak).astype(jnp.bfloat16)
    sums = matmul(weights, values)
    lane = iota((sums.shape[0], LANES), 1)
    total = sums[:, LANES + SLIDES : LANES + SLIDES + 1]
    return peak, pack(sums[:, :LANES], peak, total, head, lane)


def pack(sums, peak, total, head, lane):
    return jnp.where(
        lane == SPARE[head], peak, jnp.where(lane == SPARE[head] + 1, total, sums)
    )


def join(held, more, peak, head):
    spare = SPARE[head]
    before = held[:, spare : spare + 1]
    largest = jnp.maximum(before, peak)
    both = held * jnp.exp(before - largest) + more * jnp.exp(peak - largest)
    return jnp.where(iota(both.shape, 1) == spare, largest, both)


def marks_near(seq, ends, steps):
    rows = row_at(iota((ROWS, LANES), 0))
    return jnp.concatenate([key_marks(rows + (seq ^ step) * ROWS, ends) for step in steps], 0)


def near_kernel(tiles, query, own, side, *state):
    ends = slide_ends(tiles)
    seq = lax.axis_index("seq")
    marks = query_marks(row_at(iota((ROWS, LANES), 0)) + seq * ROWS, ends)
    keys_marks = marks_near(seq, ends, (0, 2))
    for head in range(LOCAL_HEADS):
        key_tile, value_tile = tile(KEY_TILE[head]), tile(VALUE_TILE[head])
        asked = head_lanes(query[:, tile(QUERY_TILE[head])], head)
        keys = jnp.concatenate([own[:, key_tile], side[:, key_tile]], 0)
        values = jnp.concatenate([own[:, value_tile], side[:, value_tile]], 0)
        _, state[head][...] = attend(
            jnp.concatenate([asked, marks], 1),
            jnp.concatenate([keys, keys_marks], 1),
            jnp.concatenate([values, keys_marks], 1),
            head,
        )


def rest_kernel(tiles, query, own, side, mid_a, mid_b, swapped, parts, w_out, *refs):
    n = LOCAL_HEADS
    held, (terms, far_out), state = refs[:n], refs[n : n + 2], refs[n + 2 :]
    ends = slide_ends(tiles)
    seq, mp = lax.axis_index("seq"), lax.axis_index("mp")
    marks = query_marks(row_at(iota((ROWS, LANES), 0)) + seq * ROWS, ends)
    near_marks = marks_near(seq, ends, (1, 3))
    for head in range(LOCAL_HEADS):
        key_tile, value_tile = tile(KEY_TILE[head]), tile(VALUE_TILE[head])
        asked = head_lanes(query[:, tile(QUERY_TILE[head])], head)
        peak, more = attend(
            jnp.concatenate([asked, marks], 1),
            jnp.concatenate([swapped[: 2 * ROWS, key_tile], near_marks], 1),
            jnp.concatenate([swapped[: 2 * ROWS, value_tile], near_marks], 1),
            head,
        )
        state[head][...] = join(held[head][...], more, peak, head)

        offset = (mp * LOCAL_HEADS + head) & 3
        start = pl.multiple_of(offset * CLASS_ROWS, CLASS_ROWS)
        picked = pl.ds(start, CLASS_ROWS)
        place = iota((CLASS_ROWS, LANES), 0)
        class_rows = offset + RATE_MID * ((place >> 4) + ((place & 15) << 3))
        class_marks = jnp.concatenate(
            [key_marks(class_rows + (seq ^ step) * ROWS, ends) for step in (0, 2, 1, 3, 4, 6, 5, 7)],
            0,
        )
        asked = head_lanes(query[picked, tile(QUERY_TILE[head])], head)
        asked = jnp.concatenate([asked, query_marks(class_rows + seq * ROWS, ends)], 1)

        def gathered(lanes):
            return jnp.concatenate(
                [
                    own[picked, lanes],
                    side[picked, lanes],
                    swapped[picked, lanes],
                    swapped[pl.ds(start + ROWS, CLASS_ROWS), lanes],
                    mid_a[:, lanes],
                    mid_b[:, lanes],
                    swapped[2 * ROWS :, lanes],
                ],
                0,
            )

        peak, more = attend(
            asked,
            jnp.concatenate([gathered(key_tile), class_marks], 1),
            jnp.concatenate([gathered(value_tile), class_marks], 1),
            head,
        )
        state[head][picked, :] = join(state[head][picked, :], more, peak, head)
    far_parts = []
    for head in range(LOCAL_HEADS):
        spare = SPARE[head]
        pieces = [parts[index, :, tile(head)] for index in range(FAR_GROUP)]
        tops = [piece[:, spare : spare + 1] for piece in pieces]
        peak = functools.reduce(jnp.maximum, tops)
        total = jnp.zeros((FAR_ROWS, LANES), jnp.float32)
        for piece, top in zip(pieces, tops):
            total = total + piece * jnp.exp(top - peak)
        far_parts.append(total / total[:, spare + 1 : spare + 2])
        number = mp * LOCAL_HEADS + head
        start = (number & 3) * CLASS_ROWS + (number >> 2) * FAR_ROWS
        picked = pl.ds(pl.multiple_of(start, FAR_ROWS), FAR_ROWS)
        state[head][picked, :] = join(state[head][picked, :], total, peak, head)

    def packed(values):
        first = jnp.where(iota(values[0].shape, 1) < HEAD_DIM, values[0], values[1])
        return first.astype(jnp.bfloat16), values[2].astype(jnp.bfloat16)

    first, last = packed(far_parts)
    far_out[:, :128] = first
    far_out[:, 128:] = last[:, HEAD_DIM:]
    back = (place_of(iota((ROWS, ROWS), 0)) == iota((ROWS, ROWS), 1)).astype(jnp.bfloat16)
    first, last = packed(
        [
            state[head][...] / state[head][:, SPARE[head] + 1 : SPARE[head] + 2]
            for head in range(LOCAL_HEADS)
        ]
    )
    mixed = jnp.concatenate([first, last[:, HEAD_DIM:]], 1)
    mixed = matmul(back, mixed).astype(jnp.bfloat16)
    terms[...] = matmul(mixed, w_out[...]).astype(jnp.bfloat16).reshape(4, BLOCK, WIDTH)


def far_kernel(tiles, rows, here, other, parts):
    ends = slide_ends(tiles)
    seq, mp = lax.axis_index("seq"), lax.axis_index("mp")
    column = seq & 15
    beside = ((((seq >> 4) - (column >> 1)) & 7) << 1) + (column & 1)
    count = FAR_GROUP * FAR_ROWS
    shape = (count, 2 * count)

    def position(place, holder):
        return ((place >> 4) * 16 + holder) * ROWS + (place & 15) * RATE_FAR

    at = iota(shape, 1)
    holder = jnp.where(at < count, beside, beside ^ 1)
    key_at = position(at & (count - 1), holder)
    query_at = position(iota(shape, 0), column)
    lane = iota((count, LANES), 1)
    for head in range(LOCAL_HEADS):
        number = mp * LOCAL_HEADS + head
        key_tile, value_tile = tile(KEY_TILE[head]), tile(VALUE_TILE[head])
        asked = rows[:, :, tile(QUERY_TILE[head])].reshape(count, LANES)
        asked = head_lanes(asked, head)
        scores = matmul_t(asked, jnp.concatenate([here[:, key_tile], other[:, key_tile]], 0))
        same = slide_of(query_at + number, ends) == slide_of(key_at + number, ends)
        scores = jnp.where(same, scores, HIDDEN_SCORE)
        peak = jnp.max(scores, -1, keepdims=True)
        weights = jnp.exp(scores - peak)
        total = jnp.sum(weights, -1, keepdims=True)
        values = jnp.concatenate([here[:, value_tile], other[:, value_tile]], 0)
        part = matmul(weights.astype(jnp.bfloat16), values)
        part = pack(part, peak, total, head, lane)
        parts[:, :, tile(head)] = part.reshape(FAR_GROUP, FAR_ROWS, LANES)


def weights_kernel(w_up, w_down, out):
    start = pl.multiple_of((lax.axis_index("seq") & 1) * HALF, HALF)
    out[:HALF, :HALF] = w_up[:HALF, pl.ds(start, HALF)]
    out[:HALF, HALF:] = w_up[HALF:, pl.ds(start, HALF)]
    out[HALF:, :] = w_down[pl.ds(start, HALF), :]


def hidden_part(normed, weights):
    raised = matmul(normed[:, :HALF], weights[:HALF, :HALF])
    raised = raised + matmul(normed[:, HALF:], weights[:HALF, HALF:])
    hidden = (0.5 * raised * (1.0 + lax.erf(raised * 0.7071067811865476))).astype(jnp.bfloat16)
    return matmul(hidden, weights[HALF:, :])


def norm_kernel(tokens, terms, gain, attended, normed):
    summed = terms[0].astype(jnp.float32)
    for group in range(1, 4):
        summed = summed + terms[group].astype(jnp.float32)
    summed = summed.astype(jnp.bfloat16)
    attended[...] = summed
    start = pl.multiple_of(lax.axis_index("mp") * BLOCK, BLOCK)
    own = tokens[pl.ds(start, BLOCK), :].astype(jnp.float32)
    normed[...] = layer_norm(own + summed.astype(jnp.float32), gain[...])


def ffn_kernel(own, other, weights, kept, sent):
    rows = jnp.concatenate([own[...], other[...]], 0)
    total = jnp.zeros((2 * BLOCK, WIDTH), jnp.float32)
    for group in range(4):
        total = total + hidden_part(rows, weights.at[group])
    kept[...] = total[:BLOCK, :]
    sent[...] = total[BLOCK:, :].astype(jnp.bfloat16)


def call(kernel, micros, outs, ins, scratch=(), limit=VMEM):
    places = {"smem": pltpu.SMEM, "vmem": pltpu.VMEM, "hbm": pltpu.HBM}
    return pl.pallas_call(
        kernel,
        out_shape=[jax.ShapeDtypeStruct(*out) for out in outs],
        in_specs=[pl.BlockSpec(memory_space=places[where]) for _, where in ins],
        out_specs=[pl.BlockSpec(memory_space=pltpu.VMEM) for _ in outs],
        scratch_shapes=list(scratch),
        cost_estimate=pl.CostEstimate(
            flops=int(micros * 1.1e9), bytes_accessed=int(micros * 1e6), transcendentals=0
        ),
        compiler_params=pltpu.CompilerParams(vmem_limit_bytes=limit),
    )(*[array for array, _ in ins])


def swap(value, step):
    return lax.ppermute(value, "seq", [(i, i ^ step) for i in range(lax.axis_size("seq"))])


def local(tokens, slide_tiles, attn_gain, w_query, w_key, w_value, w_out, ffn_gain, w_up, w_down):
    bf16, f32 = jnp.bfloat16, jnp.float32
    v, s, h = "vmem", "smem", "hbm"
    dma = pltpu.SemaphoreType.DMA
    columns = [[16 * z + place for z in range(FAR_GROUP)] for place in range(16)]
    across = [
        (16 * z + 2 * ((z - y) % 8) + core, 16 * z + 2 * y + core)
        for z in range(FAR_GROUP)
        for y in range(8)
        for core in range(2)
    ]
    w_query, w_key, w_value = w_query.T, w_key.T, w_value.T
    query, own, mid, far = call(
        project_kernel,
        3,
        [
            ((ROWS, 256), bf16), ((ROWS, 384), bf16), ((CLASS_ROWS, 384), bf16),
            ((FAR_GROUP, FAR_ROWS, 640), bf16),
        ],
        [(tokens, h), (attn_gain, v), (w_query, h), (w_key, h), (w_value, h)],
        [pltpu.VMEM((ROWS, WIDTH), bf16), pltpu.VMEM((3, 192, WIDTH), bf16), dma((4,))],
        limit=WHOLE_VMEM,
    )
    far_rows = lax.all_to_all(
        far, "seq", split_axis=0, concat_axis=0, tiled=True, axis_index_groups=columns
    )
    w_up, w_down, _ = lax.optimization_barrier((w_up, w_down, far))
    (packed,) = call(weights_kernel, 2, [((2 * HALF, WIDTH), bf16)], [(w_up, v), (w_down, v)])
    mine = lax.all_gather(packed, "mp", axis=0)
    side = swap(own, 2)

    far_keys = far_rows[:, :, 256:].reshape(128, 384)
    far_here = lax.ppermute(far_keys, "seq", across)
    query, _ = lax.optimization_barrier((query, far_keys))
    mid_a, mid_b = swap(mid, 4), swap(mid, 6)
    state = [((ROWS, LANES), f32)] * LOCAL_HEADS
    near = call(near_kernel, 3, state, [(slide_tiles, s), (query, v), (own, v), (side, v)])
    far_here, *near = lax.optimization_barrier((far_here, *near))
    far_other = swap(far_here, 1)
    side, mid_a, mid_b, _ = lax.optimization_barrier((side, mid_a, mid_b, far_here))
    swapped = swap(jnp.concatenate([own, side, mid_a, mid_b], 0), 1)
    (parts,) = call(
        far_kernel,
        2,
        [((FAR_GROUP, FAR_ROWS, 384), f32)],
        [(slide_tiles, s), (far_rows, v), (far_here, v), (far_other, v)],
    )
    parts = lax.all_to_all(
        parts, "seq", split_axis=0, concat_axis=0, tiled=True, axis_index_groups=columns
    )
    terms, far_attended = call(
        rest_kernel,
        7,
        [((4, BLOCK, WIDTH), bf16), ((FAR_ROWS, 192), bf16)],
        [
            (slide_tiles, s), (query, v), (own, v), (side, v), (mid_a, v), (mid_b, v), (swapped, v),
            (parts, v), (w_out, v), *[(held, v) for held in near],
        ],
        [pltpu.VMEM(*shape) for shape in state],
    )
    terms = lax.all_to_all(terms, "mp", split_axis=0, concat_axis=0, tiled=True)
    terms, mine = lax.optimization_barrier((terms, mine))
    attended, normed = call(
        norm_kernel,
        9,
        [((BLOCK, WIDTH), bf16), ((BLOCK, WIDTH), bf16)],
        [(tokens, v), (terms, v), (ffn_gain, v)],
    )
    kept, sent = call(
        ffn_kernel,
        4,
        [((BLOCK, WIDTH), f32), ((BLOCK, WIDTH), bf16)],
        [(normed, v), (swap(normed, 1), v), (mine, v)],
    )
    ffn_out = (kept + swap(sent, 1).astype(f32)).astype(bf16)
    return (attended, far_attended, ffn_out)


def solution(mesh):
    return jax.shard_map(
        local,
        mesh=mesh,
        in_specs=(
            P("seq", None),
            P(),
            P(),
            P(None, "mp"),
            P(None, "mp"),
            P(None, "mp"),
            P("mp", None),
            P(),
            P(None, "mp"),
            P("mp", None),
        ),
        out_specs=(P(("seq", "mp"), None), P("seq", "mp"), P(("seq", "mp"), None)),
        check_vma=False,
    )
```

```python
import functools

import jax
import jax.numpy as jnp
from jax import lax
from jax.experimental import pallas as pl
from jax.experimental.pallas import tpu as pltpu
from jax.sharding import PartitionSpec as P

HEAD_DIM = 64
LOCAL_HEADS = 3
RATE_MID = 4
RATE_FAR = 32
ROWS = 512
CLASS_ROWS = ROWS // RATE_MID
FAR_ROWS = ROWS // RATE_FAR
LANES = 128
SLIDES = 4
WIDTH = 768
HALF = WIDTH // 2
BLOCK = 128
EPS = 1e-05
HIDDEN_SCORE = -1e30
VMEM = 16 * 1024 * 1024
WHOLE_VMEM = 58 * 1024 * 1024

KEY_TILE = (0, 0, 2)
VALUE_TILE = (1, 1, 2)
QUERY_TILE = (0, 0, 1)
SPARE = (64, 0, 0)
FAR_GROUP = 8


def iota(shape, dim):
    return lax.broadcasted_iota(jnp.int32, shape, dim)


def place_of(row):
    return (row & 3) * CLASS_ROWS + ((row >> 2) & 7) * FAR_ROWS + (row >> 5)


def row_at(place):
    return (place & 15) * RATE_FAR + ((place >> 4) & 7) * RATE_MID + (place >> 7)


def layer_norm(as_float, gain):
    mean_val = jnp.mean(as_float, -1, keepdims=True)
    centered = as_float - mean_val
    variance = jnp.mean(centered * centered, -1, keepdims=True)
    return (centered * lax.rsqrt(variance + EPS) * gain.astype(jnp.float32)).astype(jnp.bfloat16)


def matmul(left, right):
    return jnp.dot(left, right, preferred_element_type=jnp.float32)


def matmul_t(left, right):
    return lax.dot_general(
        left, right, (((1,), (1,)), ((), ())), preferred_element_type=jnp.float32
    )


def slide_of(positions, ends):
    index = (positions >= ends[0]).astype(jnp.int32)
    for end in ends[1:]:
        index = index + (positions >= end).astype(jnp.int32)
    return index


def slide_ends(tiles_ref):
    ends = [tiles_ref[0]]
    for slide in range(1, SLIDES - 1):
        ends.append(ends[-1] + tiles_ref[slide])
    return ends


def query_marks(positions, ends):
    rows = positions.shape[0]
    lane = iota((rows, LANES), 1)
    return (lane == slide_of(positions, ends)).astype(jnp.bfloat16)


def key_marks(positions, ends):
    rows = positions.shape[0]
    lane = iota((rows, LANES), 1)
    hide = (lane < SLIDES) & (lane != slide_of(positions, ends))
    marks = jnp.where(hide, HIDDEN_SCORE, jnp.where(lane == SLIDES, 1.0, 0.0))
    return marks.astype(jnp.bfloat16)


def head_lanes(value, head):
    lane = iota(value.shape, 1)
    keep = lane < HEAD_DIM if head != 1 else lane >= HEAD_DIM
    return jnp.where(keep, value, jnp.zeros_like(value))


def tile(index):
    return slice(index * LANES, (index + 1) * LANES)


def project(normed, w_query, w_key, w_value):
    asked = (matmul_t(normed, w_query[...]) * (1.0 / 8.0)).astype(jnp.bfloat16)
    key = matmul_t(normed, w_key[...]).astype(jnp.bfloat16)
    value = matmul_t(normed, w_value[...]).astype(jnp.bfloat16)
    none = jnp.zeros_like(asked[:, 128:])
    queries = [asked[:, :128], jnp.concatenate([asked[:, 128:], none], 1)]
    keyvals = [key[:, :128], value[:, :128]]
    return queries, keyvals + [jnp.concatenate([key[:, 128:], value[:, 128:]], 1)]


def project_kernel(
    tokens, gain, w_query, w_key, w_value, query, keyval, mid, far, rows, weights, sems
):
    mp = lax.axis_index("mp")
    copies = [pltpu.make_async_copy(tokens, rows, sems.at[0])]
    for index, weight in enumerate((w_key, w_value, w_query)):
        copies.append(pltpu.make_async_copy(weight, weights.at[index], sems.at[1 + index]))
    for copy in copies:
        copy.start()
    copies[0].wait()
    normed = layer_norm(rows[...].astype(jnp.float32), gain[...])
    order = iota((ROWS, ROWS), 0) == place_of(iota((ROWS, ROWS), 1))
    normed = matmul(order.astype(jnp.bfloat16), normed).astype(jnp.bfloat16)
    for copy in copies[1:]:
        copy.wait()
    queries, keyvals = project(normed, *[weights.at[index] for index in (2, 0, 1)])
    for index, value in enumerate(queries):
        query[:, tile(index)] = value
    for index, value in enumerate(keyvals):
        keyval[:, tile(index)] = value

    def pick(source, index, whose, count):
        starts = []
        for head in range(LOCAL_HEADS):
            number = mp * LOCAL_HEADS + head
            start = (number & 3) * CLASS_ROWS
            if count == FAR_ROWS:
                start = start + (number >> 2) * FAR_ROWS
            starts.append(pl.ds(pl.multiple_of(start, count), count))
        if whose[2] == index:
            return source[starts[2], tile(index)]
        low, high = source[starts[0], tile(index)], source[starts[1], tile(index)]
        return jnp.where(iota(low.shape, 1) < HEAD_DIM, low, high)

    for index in range(3):
        mid[:, tile(index)] = pick(keyval, index, KEY_TILE, CLASS_ROWS)
    picked = [pick(query, index, QUERY_TILE, FAR_ROWS) for index in range(2)]
    picked += [pick(keyval, index, KEY_TILE, FAR_ROWS) for index in range(3)]
    for index, value in enumerate(picked):
        for copy in range(FAR_GROUP):
            far[copy, :, tile(index)] = value


def attend(query, keys, values, head):
    scores = matmul_t(query, keys)
    peak = jnp.max(scores, -1, keepdims=True)
    weights = jnp.exp(scores - peak).astype(jnp.bfloat16)
    sums = matmul(weights, values)
    lane = iota((sums.shape[0], LANES), 1)
    total = sums[:, LANES + SLIDES : LANES + SLIDES + 1]
    return peak, pack(sums[:, :LANES], peak, total, head, lane)


def pack(sums, peak, total, head, lane):
    return jnp.where(
        lane == SPARE[head], peak, jnp.where(lane == SPARE[head] + 1, total, sums)
    )


def join(held, more, peak, head):
    spare = SPARE[head]
    before = held[:, spare : spare + 1]
    largest = jnp.maximum(before, peak)
    both = held * jnp.exp(before - largest) + more * jnp.exp(peak - largest)
    return jnp.where(iota(both.shape, 1) == spare, largest, both)


def marks_near(seq, ends, steps):
    rows = row_at(iota((ROWS, LANES), 0))
    return jnp.concatenate([key_marks(rows + (seq ^ step) * ROWS, ends) for step in steps], 0)


def near_kernel(tiles, query, own, side, *state):
    ends = slide_ends(tiles)
    seq = lax.axis_index("seq")
    marks = query_marks(row_at(iota((ROWS, LANES), 0)) + seq * ROWS, ends)
    keys_marks = marks_near(seq, ends, (0, 2))
    for head in range(LOCAL_HEADS):
        key_tile, value_tile = tile(KEY_TILE[head]), tile(VALUE_TILE[head])
        asked = head_lanes(query[:, tile(QUERY_TILE[head])], head)
        keys = jnp.concatenate([own[:, key_tile], side[:, key_tile]], 0)
        values = jnp.concatenate([own[:, value_tile], side[:, value_tile]], 0)
        _, state[head][...] = attend(
            jnp.concatenate([asked, marks], 1),
            jnp.concatenate([keys, keys_marks], 1),
            jnp.concatenate([values, keys_marks], 1),
            head,
        )


def rest_kernel(tiles, query, own, side, mid_a, mid_b, swapped, parts, w_out, *refs):
    n = LOCAL_HEADS
    held, (terms, far_out), state = refs[:n], refs[n : n + 2], refs[n + 2 :]
    ends = slide_ends(tiles)
    seq, mp = lax.axis_index("seq"), lax.axis_index("mp")
    marks = query_marks(row_at(iota((ROWS, LANES), 0)) + seq * ROWS, ends)
    near_marks = marks_near(seq, ends, (1, 3))
    for head in range(LOCAL_HEADS):
        key_tile, value_tile = tile(KEY_TILE[head]), tile(VALUE_TILE[head])
        asked = head_lanes(query[:, tile(QUERY_TILE[head])], head)
        peak, more = attend(
            jnp.concatenate([asked, marks], 1),
            jnp.concatenate([swapped[: 2 * ROWS, key_tile], near_marks], 1),
            jnp.concatenate([swapped[: 2 * ROWS, value_tile], near_marks], 1),
            head,
        )
        state[head][...] = join(held[head][...], more, peak, head)

        offset = (mp * LOCAL_HEADS + head) & 3
        start = pl.multiple_of(offset * CLASS_ROWS, CLASS_ROWS)
        picked = pl.ds(start, CLASS_ROWS)
        place = iota((CLASS_ROWS, LANES), 0)
        class_rows = offset + RATE_MID * ((place >> 4) + ((place & 15) << 3))
        class_marks = jnp.concatenate(
            [key_marks(class_rows + (seq ^ step) * ROWS, ends) for step in (0, 2, 1, 3, 4, 6, 5, 7)],
            0,
        )
        asked = head_lanes(query[picked, tile(QUERY_TILE[head])], head)
        asked = jnp.concatenate([asked, query_marks(class_rows + seq * ROWS, ends)], 1)

        def gathered(lanes):
            return jnp.concatenate(
                [
                    own[picked, lanes],
                    side[picked, lanes],
                    swapped[picked, lanes],
                    swapped[pl.ds(start + ROWS, CLASS_ROWS), lanes],
                    mid_a[:, lanes],
                    mid_b[:, lanes],
                    swapped[2 * ROWS :, lanes],
                ],
                0,
            )

        peak, more = attend(
            asked,
            jnp.concatenate([gathered(key_tile), class_marks], 1),
            jnp.concatenate([gathered(value_tile), class_marks], 1),
            head,
        )
        state[head][picked, :] = join(state[head][picked, :], more, peak, head)
    far_parts = []
    for head in range(LOCAL_HEADS):
        pieces = [parts[index, :, tile(QUERY_TILE[head])] for index in range(FAR_GROUP)]
        stats = [parts[index, :, LANES + 2 * head : LANES + 2 * head + 2] for index in range(FAR_GROUP)]
        peak = functools.reduce(jnp.maximum, [stat[:, :1] for stat in stats])
        total = jnp.zeros((FAR_ROWS, LANES), jnp.float32)
        weight = jnp.zeros((FAR_ROWS, 1), jnp.float32)
        for piece, stat in zip(pieces, stats):
            factor = jnp.exp(stat[:, :1] - peak)
            total = total + piece * factor
            weight = weight + stat[:, 1:] * factor
        far_parts.append(total / weight)
        total = pack(total, peak, weight, head, iota((FAR_ROWS, LANES), 1))
        number = mp * LOCAL_HEADS + head
        start = (number & 3) * CLASS_ROWS + (number >> 2) * FAR_ROWS
        picked = pl.ds(pl.multiple_of(start, FAR_ROWS), FAR_ROWS)
        state[head][picked, :] = join(state[head][picked, :], total, peak, head)

    def packed(values):
        first = jnp.where(iota(values[0].shape, 1) < HEAD_DIM, values[0], values[1])
        return first.astype(jnp.bfloat16), values[2].astype(jnp.bfloat16)

    first, last = packed(far_parts)
    far_out[:, :128] = first
    far_out[:, 128:] = last[:, HEAD_DIM:]
    back = (place_of(iota((ROWS, ROWS), 0)) == iota((ROWS, ROWS), 1)).astype(jnp.bfloat16)
    first, last = packed(
        [
            state[head][...] / state[head][:, SPARE[head] + 1 : SPARE[head] + 2]
            for head in range(LOCAL_HEADS)
        ]
    )
    mixed = jnp.concatenate([first, last[:, HEAD_DIM:]], 1)
    mixed = matmul(back, mixed).astype(jnp.bfloat16)
    terms[...] = matmul(mixed, w_out[...]).astype(jnp.bfloat16).reshape(4, BLOCK, WIDTH)


def far_kernel(tiles, rows, here, other, parts):
    ends = slide_ends(tiles)
    seq, mp = lax.axis_index("seq"), lax.axis_index("mp")
    column = seq & 15
    beside = ((((seq >> 4) - (column >> 1)) & 7) << 1) + (column & 1)
    count = FAR_GROUP * FAR_ROWS
    shape = (count, 2 * count)

    def position(place, holder):
        return ((place >> 4) * 16 + holder) * ROWS + (place & 15) * RATE_FAR

    at = iota(shape, 1)
    holder = jnp.where(at < count, beside, beside ^ 1)
    key_at = position(at & (count - 1), holder)
    query_at = position(iota(shape, 0), column)
    lane = iota((count, LANES), 1)
    results, stats = [], jnp.zeros((count, LANES), jnp.float32)
    for head in range(LOCAL_HEADS):
        number = mp * LOCAL_HEADS + head
        key_tile, value_tile = tile(KEY_TILE[head]), tile(VALUE_TILE[head])
        asked = rows[:, :, tile(QUERY_TILE[head])].reshape(count, LANES)
        asked = head_lanes(asked, head)
        scores = matmul_t(asked, jnp.concatenate([here[:, key_tile], other[:, key_tile]], 0))
        same = slide_of(query_at + number, ends) == slide_of(key_at + number, ends)
        scores = jnp.where(same, scores, HIDDEN_SCORE)
        peak = jnp.max(scores, -1, keepdims=True)
        weights = jnp.exp(scores - peak)
        total = jnp.sum(weights, -1, keepdims=True)
        values = jnp.concatenate([here[:, value_tile], other[:, value_tile]], 0)
        part = matmul(weights.astype(jnp.bfloat16), values)
        results.append(part)
        for step, value in enumerate((peak, total)):
            stats = jnp.where(lane == 2 * head + step, value, stats)
    low = lane < HEAD_DIM
    whole = (FAR_GROUP, FAR_ROWS, LANES)
    parts[:, :, tile(0)] = jnp.where(low, results[0], results[1]).reshape(whole)
    parts[:, :, tile(1)] = jnp.where(low, stats, results[2]).reshape(whole)


def weights_kernel(w_up, w_down, out):
    start = pl.multiple_of((lax.axis_index("seq") & 1) * HALF, HALF)
    out[:HALF, :HALF] = w_up[:HALF, pl.ds(start, HALF)]
    out[:HALF, HALF:] = w_up[HALF:, pl.ds(start, HALF)]
    out[HALF:, :] = w_down[pl.ds(start, HALF), :]


def hidden_part(normed, weights):
    raised = matmul(normed[:, :HALF], weights[:HALF, :HALF])
    raised = raised + matmul(normed[:, HALF:], weights[:HALF, HALF:])
    hidden = (0.5 * raised * (1.0 + lax.erf(raised * 0.7071067811865476))).astype(jnp.bfloat16)
    return matmul(hidden, weights[HALF:, :])


def norm_kernel(tokens, terms, gain, attended, normed):
    summed = terms[0].astype(jnp.float32)
    for group in range(1, 4):
        summed = summed + terms[group].astype(jnp.float32)
    summed = summed.astype(jnp.bfloat16)
    attended[...] = summed
    start = pl.multiple_of(lax.axis_index("mp") * BLOCK, BLOCK)
    own = tokens[pl.ds(start, BLOCK), :].astype(jnp.float32)
    normed[...] = layer_norm(own + summed.astype(jnp.float32), gain[...])


def ffn_kernel(own, other, weights, kept, sent):
    rows = jnp.concatenate([own[...], other[...]], 0)
    total = jnp.zeros((2 * BLOCK, WIDTH), jnp.float32)
    for group in range(4):
        total = total + hidden_part(rows, weights.at[group])
    kept[...] = total[:BLOCK, :]
    sent[...] = total[BLOCK:, :].astype(jnp.bfloat16)


def call(kernel, micros, outs, ins, scratch=(), limit=VMEM):
    places = {"smem": pltpu.SMEM, "vmem": pltpu.VMEM, "hbm": pltpu.HBM}
    return pl.pallas_call(
        kernel,
        out_shape=[jax.ShapeDtypeStruct(*out) for out in outs],
        in_specs=[pl.BlockSpec(memory_space=places[where]) for _, where in ins],
        out_specs=[pl.BlockSpec(memory_space=pltpu.VMEM) for _ in outs],
        scratch_shapes=list(scratch),
        cost_estimate=pl.CostEstimate(
            flops=int(micros * 1.1e9), bytes_accessed=int(micros * 1e6), transcendentals=0
        ),
        compiler_params=pltpu.CompilerParams(vmem_limit_bytes=limit),
    )(*[array for array, _ in ins])


def swap(value, step):
    return lax.ppermute(value, "seq", [(i, i ^ step) for i in range(lax.axis_size("seq"))])


def local(tokens, slide_tiles, attn_gain, w_query, w_key, w_value, w_out, ffn_gain, w_up, w_down):
    bf16, f32 = jnp.bfloat16, jnp.float32
    v, s, h = "vmem", "smem", "hbm"
    dma = pltpu.SemaphoreType.DMA
    columns = [[16 * z + place for z in range(FAR_GROUP)] for place in range(16)]
    across = [
        (16 * z + 2 * ((z - y) % 8) + core, 16 * z + 2 * y + core)
        for z in range(FAR_GROUP)
        for y in range(8)
        for core in range(2)
    ]
    w_query, w_key, w_value = w_query.T, w_key.T, w_value.T
    query, own, mid, far = call(
        project_kernel,
        3,
        [
            ((ROWS, 256), bf16), ((ROWS, 384), bf16), ((CLASS_ROWS, 384), bf16),
            ((FAR_GROUP, FAR_ROWS, 640), bf16),
        ],
        [(tokens, h), (attn_gain, v), (w_query, h), (w_key, h), (w_value, h)],
        [pltpu.VMEM((ROWS, WIDTH), bf16), pltpu.VMEM((3, 192, WIDTH), bf16), dma((4,))],
        limit=WHOLE_VMEM,
    )
    far_rows = lax.all_to_all(
        far, "seq", split_axis=0, concat_axis=0, tiled=True, axis_index_groups=columns
    )
    w_up, w_down, _ = lax.optimization_barrier((w_up, w_down, far))
    (packed,) = call(weights_kernel, 2, [((2 * HALF, WIDTH), bf16)], [(w_up, v), (w_down, v)])
    mine = lax.all_gather(packed, "mp", axis=0)
    side = swap(own, 2)

    far_keys = far_rows[:, :, 256:].reshape(128, 384)
    far_here = lax.ppermute(far_keys, "seq", across)
    query, _ = lax.optimization_barrier((query, far_keys))
    mid_a, mid_b = swap(mid, 4), swap(mid, 6)
    state = [((ROWS, LANES), f32)] * LOCAL_HEADS
    near = call(near_kernel, 3, state, [(slide_tiles, s), (query, v), (own, v), (side, v)])
    far_here, *near = lax.optimization_barrier((far_here, *near))
    far_other = swap(far_here, 1)
    side, mid_a, mid_b, _ = lax.optimization_barrier((side, mid_a, mid_b, far_here))
    swapped = swap(jnp.concatenate([own, side, mid_a, mid_b], 0), 1)
    (parts,) = call(
        far_kernel,
        2,
        [((FAR_GROUP, FAR_ROWS, 256), f32)],
        [(slide_tiles, s), (far_rows, v), (far_here, v), (far_other, v)],
    )
    parts = lax.all_to_all(
        parts, "seq", split_axis=0, concat_axis=0, tiled=True, axis_index_groups=columns
    )
    terms, far_attended = call(
        rest_kernel,
        7,
        [((4, BLOCK, WIDTH), bf16), ((FAR_ROWS, 192), bf16)],
        [
            (slide_tiles, s), (query, v), (own, v), (side, v), (mid_a, v), (mid_b, v), (swapped, v),
            (parts, v), (w_out, v), *[(held, v) for held in near],
        ],
        [pltpu.VMEM(*shape) for shape in state],
    )
    terms = lax.all_to_all(terms, "mp", split_axis=0, concat_axis=0, tiled=True)
    terms, mine = lax.optimization_barrier((terms, mine))
    attended, normed = call(
        norm_kernel,
        9,
        [((BLOCK, WIDTH), bf16), ((BLOCK, WIDTH), bf16)],
        [(tokens, v), (terms, v), (ffn_gain, v)],
    )
    kept, sent = call(
        ffn_kernel,
        4,
        [((BLOCK, WIDTH), f32), ((BLOCK, WIDTH), bf16)],
        [(normed, v), (swap(normed, 1), v), (mine, v)],
    )
    ffn_out = (kept + swap(sent, 1).astype(f32)).astype(bf16)
    return (attended, far_attended, ffn_out)


def solution(mesh):
    return jax.shard_map(
        local,
        mesh=mesh,
        in_specs=(
            P("seq", None),
            P(),
            P(),
            P(None, "mp"),
            P(None, "mp"),
            P(None, "mp"),
            P("mp", None),
            P(),
            P(None, "mp"),
            P("mp", None),
        ),
        out_specs=(P(("seq", "mp"), None), P("seq", "mp"), P(("seq", "mp"), None)),
        check_vma=False,
    )
```

```python
import functools

import jax
import jax.numpy as jnp
from jax import lax
from jax.experimental import pallas as pl
from jax.experimental.pallas import tpu as pltpu
from jax.sharding import PartitionSpec as P

HEAD_DIM = 64
LOCAL_HEADS = 3
RATE_MID = 4
RATE_FAR = 32
ROWS = 512
CLASS_ROWS = ROWS // RATE_MID
FAR_ROWS = ROWS // RATE_FAR
LANES = 128
SLIDES = 4
WIDTH = 768
HALF = WIDTH // 2
BLOCK = 128
EPS = 1e-05
HIDDEN_SCORE = -1e30
VMEM = 16 * 1024 * 1024
WHOLE_VMEM = 58 * 1024 * 1024

KEY_TILE = (0, 0, 2)
VALUE_TILE = (1, 1, 2)
QUERY_TILE = (0, 0, 1)
SPARE = (64, 0, 0)
FAR_GROUP = 8


def iota(shape, dim):
    return lax.broadcasted_iota(jnp.int32, shape, dim)


def place_of(row):
    return (row & 3) * CLASS_ROWS + ((row >> 2) & 7) * FAR_ROWS + (row >> 5)


def row_at(place):
    return (place & 15) * RATE_FAR + ((place >> 4) & 7) * RATE_MID + (place >> 7)


def layer_norm(as_float, gain):
    mean_val = jnp.mean(as_float, -1, keepdims=True)
    centered = as_float - mean_val
    variance = jnp.mean(centered * centered, -1, keepdims=True)
    return (centered * lax.rsqrt(variance + EPS) * gain.astype(jnp.float32)).astype(jnp.bfloat16)


def matmul(left, right):
    return jnp.dot(left, right, preferred_element_type=jnp.float32)


def matmul_t(left, right):
    return lax.dot_general(
        left, right, (((1,), (1,)), ((), ())), preferred_element_type=jnp.float32
    )


def slide_of(positions, ends):
    index = (positions >= ends[0]).astype(jnp.int32)
    for end in ends[1:]:
        index = index + (positions >= end).astype(jnp.int32)
    return index


def slide_ends(tiles_ref):
    ends = [tiles_ref[0]]
    for slide in range(1, SLIDES - 1):
        ends.append(ends[-1] + tiles_ref[slide])
    return ends


def query_marks(positions, ends):
    rows = positions.shape[0]
    lane = iota((rows, LANES), 1)
    return (lane == slide_of(positions, ends)).astype(jnp.bfloat16)


def key_marks(positions, ends):
    rows = positions.shape[0]
    lane = iota((rows, LANES), 1)
    hide = (lane < SLIDES) & (lane != slide_of(positions, ends))
    marks = jnp.where(hide, HIDDEN_SCORE, jnp.where(lane == SLIDES, 1.0, 0.0))
    return marks.astype(jnp.bfloat16)


def head_lanes(value, head):
    lane = iota(value.shape, 1)
    keep = lane < HEAD_DIM if head != 1 else lane >= HEAD_DIM
    return jnp.where(keep, value, jnp.zeros_like(value))


def tile(index):
    return slice(index * LANES, (index + 1) * LANES)


def project(normed, w_query, w_key, w_value):
    asked = (matmul_t(normed, w_query[...]) * (1.0 / 8.0)).astype(jnp.bfloat16)
    key = matmul_t(normed, w_key[...]).astype(jnp.bfloat16)
    value = matmul_t(normed, w_value[...]).astype(jnp.bfloat16)
    none = jnp.zeros_like(asked[:, 128:])
    queries = [asked[:, :128], jnp.concatenate([asked[:, 128:], none], 1)]
    keyvals = [key[:, :128], value[:, :128]]
    return queries, keyvals + [jnp.concatenate([key[:, 128:], value[:, 128:]], 1)]


def project_kernel(
    tokens, gain, w_query, w_key, w_value, query, keyval, mid, far, rows, weights, sems
):
    mp = lax.axis_index("mp")
    copies = [pltpu.make_async_copy(tokens, rows, sems.at[0])]
    for index, weight in enumerate((w_key, w_value, w_query)):
        copies.append(pltpu.make_async_copy(weight, weights.at[index], sems.at[1 + index]))
    for copy in copies:
        copy.start()
    copies[0].wait()
    normed = layer_norm(rows[...].astype(jnp.float32), gain[...])
    order = iota((ROWS, ROWS), 0) == place_of(iota((ROWS, ROWS), 1))
    normed = matmul(order.astype(jnp.bfloat16), normed).astype(jnp.bfloat16)
    for copy in copies[1:]:
        copy.wait()
    queries, keyvals = project(normed, *[weights.at[index] for index in (2, 0, 1)])
    for index, value in enumerate(queries):
        query[:, tile(index)] = value
    for index, value in enumerate(keyvals):
        keyval[:, tile(index)] = value

    def pick(source, index, whose, count):
        starts = []
        for head in range(LOCAL_HEADS):
            number = mp * LOCAL_HEADS + head
            start = (number & 3) * CLASS_ROWS
            if count == FAR_ROWS:
                start = start + (number >> 2) * FAR_ROWS
            starts.append(pl.ds(pl.multiple_of(start, count), count))
        if whose[2] == index:
            return source[starts[2], tile(index)]
        low, high = source[starts[0], tile(index)], source[starts[1], tile(index)]
        return jnp.where(iota(low.shape, 1) < HEAD_DIM, low, high)

    for index in range(3):
        mid[:, tile(index)] = pick(keyval, index, KEY_TILE, CLASS_ROWS)
    picked = [pick(query, index, QUERY_TILE, FAR_ROWS) for index in range(2)]
    picked += [pick(keyval, index, KEY_TILE, FAR_ROWS) for index in range(3)]
    for index, value in enumerate(picked):
        for copy in range(FAR_GROUP):
            far[copy, :, tile(index)] = value


def attend(query, keys, values, head):
    scores = matmul_t(query, keys)
    peak = jnp.max(scores, -1, keepdims=True)
    weights = jnp.exp(scores - peak).astype(jnp.bfloat16)
    sums = matmul(weights, values)
    lane = iota((sums.shape[0], LANES), 1)
    total = sums[:, LANES + SLIDES : LANES + SLIDES + 1]
    return peak, pack(sums[:, :LANES], peak, total, head, lane)


def pack(sums, peak, total, head, lane):
    return jnp.where(
        lane == SPARE[head], peak, jnp.where(lane == SPARE[head] + 1, total, sums)
    )


def join(held, more, peak, head):
    spare = SPARE[head]
    before = held[:, spare : spare + 1]
    largest = jnp.maximum(before, peak)
    both = held * jnp.exp(before - largest) + more * jnp.exp(peak - largest)
    return jnp.where(iota(both.shape, 1) == spare, largest, both)


def marks_near(seq, ends, steps):
    rows = row_at(iota((ROWS, LANES), 0))
    return jnp.concatenate([key_marks(rows + (seq ^ step) * ROWS, ends) for step in steps], 0)


def near_kernel(tiles, query, own, side, *state):
    ends = slide_ends(tiles)
    seq = lax.axis_index("seq")
    marks = query_marks(row_at(iota((ROWS, LANES), 0)) + seq * ROWS, ends)
    keys_marks = marks_near(seq, ends, (0, 2))
    for head in range(LOCAL_HEADS):
        key_tile, value_tile = tile(KEY_TILE[head]), tile(VALUE_TILE[head])
        asked = head_lanes(query[:, tile(QUERY_TILE[head])], head)
        keys = jnp.concatenate([own[:, key_tile], side[:, key_tile]], 0)
        values = jnp.concatenate([own[:, value_tile], side[:, value_tile]], 0)
        _, state[head][...] = attend(
            jnp.concatenate([asked, marks], 1),
            jnp.concatenate([keys, keys_marks], 1),
            jnp.concatenate([values, keys_marks], 1),
            head,
        )


def rest_kernel(tiles, query, own, side, mid_a, mid_b, swapped, parts, w_out, *refs):
    n = LOCAL_HEADS
    held, (terms, far_out), state = refs[:n], refs[n : n + 2], refs[n + 2 :]
    ends = slide_ends(tiles)
    seq, mp = lax.axis_index("seq"), lax.axis_index("mp")
    marks = query_marks(row_at(iota((ROWS, LANES), 0)) + seq * ROWS, ends)
    near_marks = marks_near(seq, ends, (1, 3))
    for head in range(LOCAL_HEADS):
        key_tile, value_tile = tile(KEY_TILE[head]), tile(VALUE_TILE[head])
        asked = head_lanes(query[:, tile(QUERY_TILE[head])], head)
        peak, more = attend(
            jnp.concatenate([asked, marks], 1),
            jnp.concatenate([swapped[: 2 * ROWS, key_tile], near_marks], 1),
            jnp.concatenate([swapped[: 2 * ROWS, value_tile], near_marks], 1),
            head,
        )
        state[head][...] = join(held[head][...], more, peak, head)

        offset = (mp * LOCAL_HEADS + head) & 3
        start = pl.multiple_of(offset * CLASS_ROWS, CLASS_ROWS)
        picked = pl.ds(start, CLASS_ROWS)
        place = iota((CLASS_ROWS, LANES), 0)
        class_rows = offset + RATE_MID * ((place >> 4) + ((place & 15) << 3))
        class_marks = jnp.concatenate(
            [key_marks(class_rows + (seq ^ step) * ROWS, ends) for step in (0, 2, 1, 3, 4, 6, 5, 7)],
            0,
        )
        asked = head_lanes(query[picked, tile(QUERY_TILE[head])], head)
        asked = jnp.concatenate([asked, query_marks(class_rows + seq * ROWS, ends)], 1)

        def gathered(lanes):
            return jnp.concatenate(
                [
                    own[picked, lanes],
                    side[picked, lanes],
                    swapped[picked, lanes],
                    swapped[pl.ds(start + ROWS, CLASS_ROWS), lanes],
                    mid_a[:, lanes],
                    mid_b[:, lanes],
                    swapped[2 * ROWS :, lanes],
                ],
                0,
            )

        peak, more = attend(
            asked,
            jnp.concatenate([gathered(key_tile), class_marks], 1),
            jnp.concatenate([gathered(value_tile), class_marks], 1),
            head,
        )
        state[head][picked, :] = join(state[head][picked, :], more, peak, head)
    far_parts = []
    for head in range(LOCAL_HEADS):
        pieces, tops, weights = [], [], []
        for index in range(FAR_GROUP):
            pieces.append(parts[index, :, tile(QUERY_TILE[head])].astype(jnp.float32))
            stats = parts[index, :, tile(1)].astype(jnp.float32)
            thirds_of = [stats[:, 6 * head + step : 6 * head + step + 1] for step in range(6)]
            tops.append(thirds_of[0] + thirds_of[1] + thirds_of[2])
            weights.append(thirds_of[3] + thirds_of[4] + thirds_of[5])
        peak = functools.reduce(jnp.maximum, tops)
        total = jnp.zeros((FAR_ROWS, LANES), jnp.float32)
        weight = jnp.zeros((FAR_ROWS, 1), jnp.float32)
        for piece, top, held_weight in zip(pieces, tops, weights):
            factor = held_weight * jnp.exp(top - peak)
            total = total + piece * factor
            weight = weight + factor
        far_parts.append(total / weight)
        total = pack(total, peak, weight, head, iota((FAR_ROWS, LANES), 1))
        number = mp * LOCAL_HEADS + head
        start = (number & 3) * CLASS_ROWS + (number >> 2) * FAR_ROWS
        picked = pl.ds(pl.multiple_of(start, FAR_ROWS), FAR_ROWS)
        state[head][picked, :] = join(state[head][picked, :], total, peak, head)

    def packed(values):
        first = jnp.where(iota(values[0].shape, 1) < HEAD_DIM, values[0], values[1])
        return first.astype(jnp.bfloat16), values[2].astype(jnp.bfloat16)

    first, last = packed(far_parts)
    far_out[:, :128] = first
    far_out[:, 128:] = last[:, HEAD_DIM:]
    back = (place_of(iota((ROWS, ROWS), 0)) == iota((ROWS, ROWS), 1)).astype(jnp.bfloat16)
    first, last = packed(
        [
            state[head][...] / state[head][:, SPARE[head] + 1 : SPARE[head] + 2]
            for head in range(LOCAL_HEADS)
        ]
    )
    mixed = jnp.concatenate([first, last[:, HEAD_DIM:]], 1)
    mixed = matmul(back, mixed).astype(jnp.bfloat16)
    terms[...] = matmul(mixed, w_out[...]).astype(jnp.bfloat16).reshape(4, BLOCK, WIDTH)


def thirds(value):
    parts = []
    for _ in range(3):
        parts.append(value.astype(jnp.bfloat16).astype(jnp.float32))
        value = value - parts[-1]
    return parts


def far_kernel(tiles, rows, here, other, parts):
    ends = slide_ends(tiles)
    seq, mp = lax.axis_index("seq"), lax.axis_index("mp")
    column = seq & 15
    beside = ((((seq >> 4) - (column >> 1)) & 7) << 1) + (column & 1)
    count = FAR_GROUP * FAR_ROWS
    shape = (count, 2 * count)

    def position(place, holder):
        return ((place >> 4) * 16 + holder) * ROWS + (place & 15) * RATE_FAR

    at = iota(shape, 1)
    holder = jnp.where(at < count, beside, beside ^ 1)
    key_at = position(at & (count - 1), holder)
    query_at = position(iota(shape, 0), column)
    lane = iota((count, LANES), 1)
    results, stats = [], jnp.zeros((count, LANES), jnp.float32)
    for head in range(LOCAL_HEADS):
        number = mp * LOCAL_HEADS + head
        key_tile, value_tile = tile(KEY_TILE[head]), tile(VALUE_TILE[head])
        asked = rows[:, :, tile(QUERY_TILE[head])].reshape(count, LANES)
        asked = head_lanes(asked, head)
        scores = matmul_t(asked, jnp.concatenate([here[:, key_tile], other[:, key_tile]], 0))
        same = slide_of(query_at + number, ends) == slide_of(key_at + number, ends)
        scores = jnp.where(same, scores, HIDDEN_SCORE)
        peak = jnp.max(scores, -1, keepdims=True)
        weights = jnp.exp(scores - peak)
        total = jnp.sum(weights, -1, keepdims=True)
        values = jnp.concatenate([here[:, value_tile], other[:, value_tile]], 0)
        part = matmul(weights.astype(jnp.bfloat16), values)
        results.append(part / total)
        for step, value in enumerate(thirds(peak) + thirds(total)):
            stats = jnp.where(lane == 6 * head + step, value, stats)
    low = lane < HEAD_DIM
    for index, value in enumerate(
        (jnp.where(low, results[0], results[1]), jnp.where(low, stats, results[2]))
    ):
        shaped = value.reshape(FAR_GROUP, FAR_ROWS, LANES)
        parts[:, :, tile(index)] = shaped.astype(jnp.bfloat16)


def weights_kernel(w_up, w_down, out):
    start = pl.multiple_of((lax.axis_index("seq") & 1) * HALF, HALF)
    out[:HALF, :HALF] = w_up[:HALF, pl.ds(start, HALF)]
    out[:HALF, HALF:] = w_up[HALF:, pl.ds(start, HALF)]
    out[HALF:, :] = w_down[pl.ds(start, HALF), :]


def hidden_part(normed, weights):
    raised = matmul(normed[:, :HALF], weights[:HALF, :HALF])
    raised = raised + matmul(normed[:, HALF:], weights[:HALF, HALF:])
    hidden = (0.5 * raised * (1.0 + lax.erf(raised * 0.7071067811865476))).astype(jnp.bfloat16)
    return matmul(hidden, weights[HALF:, :])


def norm_kernel(tokens, terms, gain, attended, normed):
    summed = terms[0].astype(jnp.float32)
    for group in range(1, 4):
        summed = summed + terms[group].astype(jnp.float32)
    summed = summed.astype(jnp.bfloat16)
    attended[...] = summed
    start = pl.multiple_of(lax.axis_index("mp") * BLOCK, BLOCK)
    own = tokens[pl.ds(start, BLOCK), :].astype(jnp.float32)
    normed[...] = layer_norm(own + summed.astype(jnp.float32), gain[...])


def ffn_kernel(own, other, weights, kept, sent):
    rows = jnp.concatenate([own[...], other[...]], 0)
    total = jnp.zeros((2 * BLOCK, WIDTH), jnp.float32)
    for group in range(4):
        total = total + hidden_part(rows, weights.at[group])
    kept[...] = total[:BLOCK, :]
    sent[...] = total[BLOCK:, :].astype(jnp.bfloat16)


def call(kernel, micros, outs, ins, scratch=(), limit=VMEM):
    places = {"smem": pltpu.SMEM, "vmem": pltpu.VMEM, "hbm": pltpu.HBM}
    return pl.pallas_call(
        kernel,
        out_shape=[jax.ShapeDtypeStruct(*out) for out in outs],
        in_specs=[pl.BlockSpec(memory_space=places[where]) for _, where in ins],
        out_specs=[pl.BlockSpec(memory_space=pltpu.VMEM) for _ in outs],
        scratch_shapes=list(scratch),
        cost_estimate=pl.CostEstimate(
            flops=int(micros * 1.1e9), bytes_accessed=int(micros * 1e6), transcendentals=0
        ),
        compiler_params=pltpu.CompilerParams(vmem_limit_bytes=limit),
    )(*[array for array, _ in ins])


def swap(value, step):
    return lax.ppermute(value, "seq", [(i, i ^ step) for i in range(lax.axis_size("seq"))])


def local(tokens, slide_tiles, attn_gain, w_query, w_key, w_value, w_out, ffn_gain, w_up, w_down):
    bf16, f32 = jnp.bfloat16, jnp.float32
    v, s, h = "vmem", "smem", "hbm"
    dma = pltpu.SemaphoreType.DMA
    columns = [[16 * z + place for z in range(FAR_GROUP)] for place in range(16)]
    across = [
        (16 * z + 2 * ((z - y) % 8) + core, 16 * z + 2 * y + core)
        for z in range(FAR_GROUP)
        for y in range(8)
        for core in range(2)
    ]
    w_query, w_key, w_value = w_query.T, w_key.T, w_value.T
    query, own, mid, far = call(
        project_kernel,
        3,
        [
            ((ROWS, 256), bf16), ((ROWS, 384), bf16), ((CLASS_ROWS, 384), bf16),
            ((FAR_GROUP, FAR_ROWS, 640), bf16),
        ],
        [(tokens, h), (attn_gain, v), (w_query, h), (w_key, h), (w_value, h)],
        [pltpu.VMEM((ROWS, WIDTH), bf16), pltpu.VMEM((3, 192, WIDTH), bf16), dma((4,))],
        limit=WHOLE_VMEM,
    )
    far_rows = lax.all_to_all(
        far, "seq", split_axis=0, concat_axis=0, tiled=True, axis_index_groups=columns
    )
    w_up, w_down, _ = lax.optimization_barrier((w_up, w_down, far))
    (packed,) = call(weights_kernel, 2, [((2 * HALF, WIDTH), bf16)], [(w_up, v), (w_down, v)])
    mine = lax.all_gather(packed, "mp", axis=0)
    side = swap(own, 2)

    far_keys = far_rows[:, :, 256:].reshape(128, 384)
    far_here = lax.ppermute(far_keys, "seq", across)
    query, _ = lax.optimization_barrier((query, far_keys))
    mid_a, mid_b = swap(mid, 4), swap(mid, 6)
    state = [((ROWS, LANES), f32)] * LOCAL_HEADS
    near = call(near_kernel, 3, state, [(slide_tiles, s), (query, v), (own, v), (side, v)])
    far_here, *near = lax.optimization_barrier((far_here, *near))
    far_other = swap(far_here, 1)
    side, mid_a, mid_b, _ = lax.optimization_barrier((side, mid_a, mid_b, far_here))
    swapped = swap(jnp.concatenate([own, side, mid_a, mid_b], 0), 1)
    (parts,) = call(
        far_kernel,
        2,
        [((FAR_GROUP, FAR_ROWS, 256), bf16)],
        [(slide_tiles, s), (far_rows, v), (far_here, v), (far_other, v)],
    )
    parts = lax.all_to_all(
        parts, "seq", split_axis=0, concat_axis=0, tiled=True, axis_index_groups=columns
    )
    terms, far_attended = call(
        rest_kernel,
        7,
        [((4, BLOCK, WIDTH), bf16), ((FAR_ROWS, 192), bf16)],
        [
            (slide_tiles, s), (query, v), (own, v), (side, v), (mid_a, v), (mid_b, v), (swapped, v),
            (parts, v), (w_out, v), *[(held, v) for held in near],
        ],
        [pltpu.VMEM(*shape) for shape in state],
    )
    terms = lax.all_to_all(terms, "mp", split_axis=0, concat_axis=0, tiled=True)
    terms, mine = lax.optimization_barrier((terms, mine))
    attended, normed = call(
        norm_kernel,
        9,
        [((BLOCK, WIDTH), bf16), ((BLOCK, WIDTH), bf16)],
        [(tokens, v), (terms, v), (ffn_gain, v)],
    )
    kept, sent = call(
        ffn_kernel,
        4,
        [((BLOCK, WIDTH), f32), ((BLOCK, WIDTH), bf16)],
        [(normed, v), (swap(normed, 1), v), (mine, v)],
    )
    ffn_out = (kept + swap(sent, 1).astype(f32)).astype(bf16)
    return (attended, far_attended, ffn_out)


def solution(mesh):
    return jax.shard_map(
        local,
        mesh=mesh,
        in_specs=(
            P("seq", None),
            P(),
            P(),
            P(None, "mp"),
            P(None, "mp"),
            P(None, "mp"),
            P("mp", None),
            P(),
            P(None, "mp"),
            P("mp", None),
        ),
        out_specs=(P(("seq", "mp"), None), P("seq", "mp"), P(("seq", "mp"), None)),
        check_vma=False,
    )
```

```python
import functools

import jax
import jax.numpy as jnp
from jax import lax
from jax.experimental import pallas as pl
from jax.experimental.pallas import tpu as pltpu
from jax.sharding import PartitionSpec as P

HEAD_DIM = 64
LOCAL_HEADS = 3
RATE_MID = 4
RATE_FAR = 32
ROWS = 512
CLASS_ROWS = ROWS // RATE_MID
FAR_ROWS = ROWS // RATE_FAR
LANES = 128
SLIDES = 4
WIDTH = 768
HALF = WIDTH // 2
BLOCK = 128
EPS = 1e-05
HIDDEN_SCORE = -1e30
VMEM = 16 * 1024 * 1024
WHOLE_VMEM = 58 * 1024 * 1024

KEY_TILE = (0, 0, 2)
VALUE_TILE = (1, 1, 2)
QUERY_TILE = (0, 0, 1)
SPARE = (64, 0, 0)
FAR_GROUP = 8


def iota(shape, dim):
    return lax.broadcasted_iota(jnp.int32, shape, dim)


def place_of(row):
    return (row & 3) * CLASS_ROWS + ((row >> 2) & 7) * FAR_ROWS + (row >> 5)


def row_at(place):
    return (place & 15) * RATE_FAR + ((place >> 4) & 7) * RATE_MID + (place >> 7)


def layer_norm(as_float, gain):
    mean_val = jnp.mean(as_float, -1, keepdims=True)
    centered = as_float - mean_val
    variance = jnp.mean(centered * centered, -1, keepdims=True)
    return (centered * lax.rsqrt(variance + EPS) * gain.astype(jnp.float32)).astype(jnp.bfloat16)


def matmul(left, right):
    return jnp.dot(left, right, preferred_element_type=jnp.float32)


def matmul_t(left, right):
    return lax.dot_general(
        left, right, (((1,), (1,)), ((), ())), preferred_element_type=jnp.float32
    )


def slide_of(positions, ends):
    index = (positions >= ends[0]).astype(jnp.int32)
    for end in ends[1:]:
        index = index + (positions >= end).astype(jnp.int32)
    return index


def slide_ends(tiles_ref):
    ends = [tiles_ref[0]]
    for slide in range(1, SLIDES - 1):
        ends.append(ends[-1] + tiles_ref[slide])
    return ends


def query_marks(positions, ends):
    rows = positions.shape[0]
    lane = iota((rows, LANES), 1)
    return (lane == slide_of(positions, ends)).astype(jnp.bfloat16)


def key_marks(positions, ends):
    rows = positions.shape[0]
    lane = iota((rows, LANES), 1)
    hide = (lane < SLIDES) & (lane != slide_of(positions, ends))
    marks = jnp.where(hide, HIDDEN_SCORE, jnp.where(lane == SLIDES, 1.0, 0.0))
    return marks.astype(jnp.bfloat16)


def head_lanes(value, head):
    lane = iota(value.shape, 1)
    keep = lane < HEAD_DIM if head != 1 else lane >= HEAD_DIM
    return jnp.where(keep, value, jnp.zeros_like(value))


def tile(index):
    return slice(index * LANES, (index + 1) * LANES)


def project(normed, w_query, w_key, w_value):
    asked = (matmul_t(normed, w_query[...]) * (1.0 / 8.0)).astype(jnp.bfloat16)
    key = matmul_t(normed, w_key[...]).astype(jnp.bfloat16)
    value = matmul_t(normed, w_value[...]).astype(jnp.bfloat16)
    none = jnp.zeros_like(asked[:, 128:])
    queries = [asked[:, :128], jnp.concatenate([asked[:, 128:], none], 1)]
    keyvals = [key[:, :128], value[:, :128]]
    return queries, keyvals + [jnp.concatenate([key[:, 128:], value[:, 128:]], 1)]


def project_kernel(
    tokens, gain, w_query, w_key, w_value, query, keyval, mid, far, rows, weights, sems
):
    mp = lax.axis_index("mp")
    copies = [pltpu.make_async_copy(tokens, rows, sems.at[0])]
    for index, weight in enumerate((w_key, w_value, w_query)):
        copies.append(pltpu.make_async_copy(weight, weights.at[index], sems.at[1 + index]))
    for copy in copies:
        copy.start()
    copies[0].wait()
    normed = layer_norm(rows[...].astype(jnp.float32), gain[...])
    order = iota((ROWS, ROWS), 0) == place_of(iota((ROWS, ROWS), 1))
    normed = matmul(order.astype(jnp.bfloat16), normed).astype(jnp.bfloat16)
    for copy in copies[1:]:
        copy.wait()
    queries, keyvals = project(normed, *[weights.at[index] for index in (2, 0, 1)])
    for index, value in enumerate(queries):
        query[:, tile(index)] = value
    for index, value in enumerate(keyvals):
        keyval[:, tile(index)] = value

    def pick(source, index, whose, count):
        starts = []
        for head in range(LOCAL_HEADS):
            number = mp * LOCAL_HEADS + head
            start = (number & 3) * CLASS_ROWS
            if count == FAR_ROWS:
                start = start + (number >> 2) * FAR_ROWS
            starts.append(pl.ds(pl.multiple_of(start, count), count))
        if whose[2] == index:
            return source[starts[2], tile(index)]
        low, high = source[starts[0], tile(index)], source[starts[1], tile(index)]
        return jnp.where(iota(low.shape, 1) < HEAD_DIM, low, high)

    for index in range(3):
        mid[:, tile(index)] = pick(keyval, index, KEY_TILE, CLASS_ROWS)
    picked = [pick(query, index, QUERY_TILE, FAR_ROWS) for index in range(2)]
    picked += [pick(keyval, index, KEY_TILE, FAR_ROWS) for index in range(3)]
    for index, value in enumerate(picked):
        for copy in range(FAR_GROUP):
            far[copy, :, tile(index)] = value


def attend(query, keys, values, head):
    scores = matmul_t(query, keys)
    peak = jnp.max(scores, -1, keepdims=True)
    weights = jnp.exp(scores - peak).astype(jnp.bfloat16)
    sums = matmul(weights, values)
    lane = iota((sums.shape[0], LANES), 1)
    total = sums[:, LANES + SLIDES : LANES + SLIDES + 1]
    return peak, pack(sums[:, :LANES], peak, total, head, lane)


def pack(sums, peak, total, head, lane):
    return jnp.where(
        lane == SPARE[head], peak, jnp.where(lane == SPARE[head] + 1, total, sums)
    )


def join(held, more, peak, head):
    spare = SPARE[head]
    before = held[:, spare : spare + 1]
    largest = jnp.maximum(before, peak)
    both = held * jnp.exp(before - largest) + more * jnp.exp(peak - largest)
    return jnp.where(iota(both.shape, 1) == spare, largest, both)


def marks_near(seq, ends, steps):
    rows = row_at(iota((ROWS, LANES), 0))
    return jnp.concatenate([key_marks(rows + (seq ^ step) * ROWS, ends) for step in steps], 0)


def near_kernel(tiles, query, own, side, *state):
    ends = slide_ends(tiles)
    seq = lax.axis_index("seq")
    marks = query_marks(row_at(iota((ROWS, LANES), 0)) + seq * ROWS, ends)
    keys_marks = marks_near(seq, ends, (0, 2))
    for head in range(LOCAL_HEADS):
        key_tile, value_tile = tile(KEY_TILE[head]), tile(VALUE_TILE[head])
        asked = head_lanes(query[:, tile(QUERY_TILE[head])], head)
        keys = jnp.concatenate([own[:, key_tile], side[:, key_tile]], 0)
        values = jnp.concatenate([own[:, value_tile], side[:, value_tile]], 0)
        _, state[head][...] = attend(
            jnp.concatenate([asked, marks], 1),
            jnp.concatenate([keys, keys_marks], 1),
            jnp.concatenate([values, keys_marks], 1),
            head,
        )


def rest_kernel(tiles, query, own, side, mid_a, mid_b, swapped, parts, w_out, *refs):
    n = LOCAL_HEADS
    held, (terms, far_out), state = refs[:n], refs[n : n + 2], refs[n + 2 :]
    ends = slide_ends(tiles)
    seq, mp = lax.axis_index("seq"), lax.axis_index("mp")
    marks = query_marks(row_at(iota((ROWS, LANES), 0)) + seq * ROWS, ends)
    near_marks = marks_near(seq, ends, (1, 3))
    for head in range(LOCAL_HEADS):
        key_tile, value_tile = tile(KEY_TILE[head]), tile(VALUE_TILE[head])
        asked = head_lanes(query[:, tile(QUERY_TILE[head])], head)
        peak, more = attend(
            jnp.concatenate([asked, marks], 1),
            jnp.concatenate([swapped[: 2 * ROWS, key_tile], near_marks], 1),
            jnp.concatenate([swapped[: 2 * ROWS, value_tile], near_marks], 1),
            head,
        )
        state[head][...] = join(held[head][...], more, peak, head)

        offset = (mp * LOCAL_HEADS + head) & 3
        start = pl.multiple_of(offset * CLASS_ROWS, CLASS_ROWS)
        picked = pl.ds(start, CLASS_ROWS)
        place = iota((CLASS_ROWS, LANES), 0)
        class_rows = offset + RATE_MID * ((place >> 4) + ((place & 15) << 3))
        class_marks = jnp.concatenate(
            [key_marks(class_rows + (seq ^ step) * ROWS, ends) for step in (0, 2, 1, 3, 4, 6, 5, 7)],
            0,
        )
        asked = head_lanes(query[picked, tile(QUERY_TILE[head])], head)
        asked = jnp.concatenate([asked, query_marks(class_rows + seq * ROWS, ends)], 1)

        def gathered(lanes):
            return jnp.concatenate(
                [
                    own[picked, lanes],
                    side[picked, lanes],
                    swapped[picked, lanes],
                    swapped[pl.ds(start + ROWS, CLASS_ROWS), lanes],
                    mid_a[:, lanes],
                    mid_b[:, lanes],
                    swapped[2 * ROWS :, lanes],
                ],
                0,
            )

        peak, more = attend(
            asked,
            jnp.concatenate([gathered(key_tile), class_marks], 1),
            jnp.concatenate([gathered(value_tile), class_marks], 1),
            head,
        )
        state[head][picked, :] = join(state[head][picked, :], more, peak, head)
    far_parts = []
    for head in range(LOCAL_HEADS):
        pieces, tops, weights = [], [], []
        for index in range(FAR_GROUP):
            pieces.append(parts[index, :, tile(QUERY_TILE[head])].astype(jnp.float32))
            stats = parts[index, :, tile(1)].astype(jnp.float32)
            thirds_of = [stats[:, 6 * head + step : 6 * head + step + 1] for step in range(6)]
            tops.append(thirds_of[0] + thirds_of[1] + thirds_of[2])
            weights.append(thirds_of[3] + thirds_of[4] + thirds_of[5])
        peak = functools.reduce(jnp.maximum, tops)
        total = jnp.zeros((FAR_ROWS, LANES), jnp.float32)
        weight = jnp.zeros((FAR_ROWS, 1), jnp.float32)
        for piece, top, held_weight in zip(pieces, tops, weights):
            factor = held_weight * jnp.exp(top - peak)
            total = total + piece * factor
            weight = weight + factor
        far_parts.append(total / weight)
        total = pack(total, peak, weight, head, iota((FAR_ROWS, LANES), 1))
        number = mp * LOCAL_HEADS + head
        start = (number & 3) * CLASS_ROWS + (number >> 2) * FAR_ROWS
        picked = pl.ds(pl.multiple_of(start, FAR_ROWS), FAR_ROWS)
        state[head][picked, :] = join(state[head][picked, :], total, peak, head)

    def packed(values):
        first = jnp.where(iota(values[0].shape, 1) < HEAD_DIM, values[0], values[1])
        return first.astype(jnp.bfloat16), values[2].astype(jnp.bfloat16)

    first, last = packed(far_parts)
    far_out[:, :128] = first
    far_out[:, 128:] = last[:, HEAD_DIM:]
    back = (place_of(iota((ROWS, ROWS), 0)) == iota((ROWS, ROWS), 1)).astype(jnp.bfloat16)
    first, last = packed(
        [
            state[head][...] / state[head][:, SPARE[head] + 1 : SPARE[head] + 2]
            for head in range(LOCAL_HEADS)
        ]
    )
    mixed = jnp.concatenate([first, last[:, HEAD_DIM:]], 1)
    mixed = matmul(back, mixed).astype(jnp.bfloat16)
    terms[...] = matmul(mixed, w_out[...]).astype(jnp.bfloat16).reshape(4, BLOCK, WIDTH)


def thirds(value):
    parts = []
    for _ in range(3):
        parts.append(value.astype(jnp.bfloat16).astype(jnp.float32))
        value = value - parts[-1]
    return parts


def far_kernel(tiles, rows, here, other, parts):
    ends = slide_ends(tiles)
    seq, mp = lax.axis_index("seq"), lax.axis_index("mp")
    column = seq & 15
    beside = ((((seq >> 4) - (column >> 1)) & 7) << 1) + (column & 1)
    count = FAR_GROUP * FAR_ROWS
    shape = (count, 2 * count)

    def position(place, holder):
        return ((place >> 4) * 16 + holder) * ROWS + (place & 15) * RATE_FAR

    at = iota(shape, 1)
    holder = jnp.where(at < count, beside, beside ^ 1)
    key_at = position(at & (count - 1), holder)
    query_at = position(iota(shape, 0), column)
    lane = iota((count, LANES), 1)
    results, stats = [], jnp.zeros((count, LANES), jnp.float32)
    for head in range(LOCAL_HEADS):
        number = mp * LOCAL_HEADS + head
        key_tile, value_tile = tile(KEY_TILE[head]), tile(VALUE_TILE[head])
        asked = rows[:, :, tile(QUERY_TILE[head])].reshape(count, LANES)
        asked = head_lanes(asked, head)
        scores = matmul_t(asked, jnp.concatenate([here[:, key_tile], other[:, key_tile]], 0))
        same = slide_of(query_at + number, ends) == slide_of(key_at + number, ends)
        scores = jnp.where(same, scores, HIDDEN_SCORE)
        peak = jnp.max(scores, -1, keepdims=True)
        weights = jnp.exp(scores - peak)
        total = jnp.sum(weights, -1, keepdims=True)
        values = jnp.concatenate([here[:, value_tile], other[:, value_tile]], 0)
        part = matmul(weights.astype(jnp.bfloat16), values)
        results.append(part / total)
        for step, value in enumerate(thirds(peak) + thirds(total)):
            stats = jnp.where(lane == 6 * head + step, value, stats)
    low = lane < HEAD_DIM
    for index, value in enumerate(
        (jnp.where(low, results[0], results[1]), jnp.where(low, stats, results[2]))
    ):
        shaped = value.reshape(FAR_GROUP, FAR_ROWS, LANES)
        parts[:, :, tile(index)] = shaped.astype(jnp.bfloat16)


def weights_kernel(w_up, w_down, out, sems):
    start = pl.multiple_of((lax.axis_index("seq") & 1) * HALF, HALF)
    upper, lower = pl.ds(0, HALF), pl.ds(HALF, HALF)
    parts = [
        (w_up.at[upper, pl.ds(start, HALF)], out.at[upper, upper]),
        (w_up.at[lower, pl.ds(start, HALF)], out.at[upper, lower]),
        (w_down.at[pl.ds(start, HALF), :], out.at[lower, :]),
    ]
    copies = [
        pltpu.make_async_copy(source, target, sems.at[index])
        for index, (source, target) in enumerate(parts)
    ]
    for copy in copies:
        copy.start()
    for copy in copies:
        copy.wait()


def hidden_part(normed, weights):
    raised = matmul(normed[:, :HALF], weights[:HALF, :HALF])
    raised = raised + matmul(normed[:, HALF:], weights[:HALF, HALF:])
    hidden = (0.5 * raised * (1.0 + lax.erf(raised * 0.7071067811865476))).astype(jnp.bfloat16)
    return matmul(hidden, weights[HALF:, :])


def norm_kernel(tokens, terms, gain, attended, normed):
    summed = terms[0].astype(jnp.float32)
    for group in range(1, 4):
        summed = summed + terms[group].astype(jnp.float32)
    summed = summed.astype(jnp.bfloat16)
    attended[...] = summed
    start = pl.multiple_of(lax.axis_index("mp") * BLOCK, BLOCK)
    own = tokens[pl.ds(start, BLOCK), :].astype(jnp.float32)
    normed[...] = layer_norm(own + summed.astype(jnp.float32), gain[...])


def ffn_kernel(own, other, weights, kept, sent):
    rows = jnp.concatenate([own[...], other[...]], 0)
    total = jnp.zeros((2 * BLOCK, WIDTH), jnp.float32)
    for group in range(4):
        total = total + hidden_part(rows, weights.at[group])
    kept[...] = total[:BLOCK, :]
    sent[...] = total[BLOCK:, :].astype(jnp.bfloat16)


def call(kernel, micros, outs, ins, scratch=(), limit=VMEM):
    places = {"smem": pltpu.SMEM, "vmem": pltpu.VMEM, "hbm": pltpu.HBM}
    return pl.pallas_call(
        kernel,
        out_shape=[jax.ShapeDtypeStruct(*out) for out in outs],
        in_specs=[pl.BlockSpec(memory_space=places[where]) for _, where in ins],
        out_specs=[pl.BlockSpec(memory_space=pltpu.VMEM) for _ in outs],
        scratch_shapes=list(scratch),
        cost_estimate=pl.CostEstimate(
            flops=int(micros * 1.1e9), bytes_accessed=int(micros * 1e6), transcendentals=0
        ),
        compiler_params=pltpu.CompilerParams(vmem_limit_bytes=limit),
    )(*[array for array, _ in ins])


def swap(value, step):
    return lax.ppermute(value, "seq", [(i, i ^ step) for i in range(lax.axis_size("seq"))])


def local(tokens, slide_tiles, attn_gain, w_query, w_key, w_value, w_out, ffn_gain, w_up, w_down):
    bf16, f32 = jnp.bfloat16, jnp.float32
    v, s, h = "vmem", "smem", "hbm"
    dma = pltpu.SemaphoreType.DMA
    columns = [[16 * z + place for z in range(FAR_GROUP)] for place in range(16)]
    across = [
        (16 * z + 2 * ((z - y) % 8) + core, 16 * z + 2 * y + core)
        for z in range(FAR_GROUP)
        for y in range(8)
        for core in range(2)
    ]
    w_query, w_key, w_value = w_query.T, w_key.T, w_value.T
    (packed,) = call(
        weights_kernel,
        2,
        [((2 * HALF, WIDTH), bf16)],
        [(w_up, h), (w_down, h)],
        [dma((3,))],
        WHOLE_VMEM,
    )
    mine = lax.all_gather(packed, "mp", axis=0)
    tokens, _ = lax.optimization_barrier((tokens, packed))
    query, own, mid, far = call(
        project_kernel,
        3,
        [
            ((ROWS, 256), bf16), ((ROWS, 384), bf16), ((CLASS_ROWS, 384), bf16),
            ((FAR_GROUP, FAR_ROWS, 640), bf16),
        ],
        [(tokens, h), (attn_gain, v), (w_query, h), (w_key, h), (w_value, h)],
        [pltpu.VMEM((ROWS, WIDTH), bf16), pltpu.VMEM((3, 192, WIDTH), bf16), dma((4,))],
        limit=WHOLE_VMEM,
    )
    far_rows = lax.all_to_all(
        far, "seq", split_axis=0, concat_axis=0, tiled=True, axis_index_groups=columns
    )
    side = swap(own, 2)

    far_keys = far_rows[:, :, 256:].reshape(128, 384)
    far_here = lax.ppermute(far_keys, "seq", across)
    query, _ = lax.optimization_barrier((query, far_keys))
    mid_a, mid_b = swap(mid, 4), swap(mid, 6)
    state = [((ROWS, LANES), f32)] * LOCAL_HEADS
    near = call(near_kernel, 3, state, [(slide_tiles, s), (query, v), (own, v), (side, v)])
    far_here, *near = lax.optimization_barrier((far_here, *near))
    far_other = swap(far_here, 1)
    side, mid_a, mid_b, _ = lax.optimization_barrier((side, mid_a, mid_b, far_here))
    swapped = swap(jnp.concatenate([own, side, mid_a, mid_b], 0), 1)
    (parts,) = call(
        far_kernel,
        2,
        [((FAR_GROUP, FAR_ROWS, 256), bf16)],
        [(slide_tiles, s), (far_rows, v), (far_here, v), (far_other, v)],
    )
    parts = lax.all_to_all(
        parts, "seq", split_axis=0, concat_axis=0, tiled=True, axis_index_groups=columns
    )
    terms, far_attended = call(
        rest_kernel,
        7,
        [((4, BLOCK, WIDTH), bf16), ((FAR_ROWS, 192), bf16)],
        [
            (slide_tiles, s), (query, v), (own, v), (side, v), (mid_a, v), (mid_b, v), (swapped, v),
            (parts, v), (w_out, v), *[(held, v) for held in near],
        ],
        [pltpu.VMEM(*shape) for shape in state],
    )
    terms = lax.all_to_all(terms, "mp", split_axis=0, concat_axis=0, tiled=True)
    terms, mine = lax.optimization_barrier((terms, mine))
    attended, normed = call(
        norm_kernel,
        9,
        [((BLOCK, WIDTH), bf16), ((BLOCK, WIDTH), bf16)],
        [(tokens, v), (terms, v), (ffn_gain, v)],
    )
    kept, sent = call(
        ffn_kernel,
        4,
        [((BLOCK, WIDTH), f32), ((BLOCK, WIDTH), bf16)],
        [(normed, v), (swap(normed, 1), v), (mine, v)],
    )
    ffn_out = (kept + swap(sent, 1).astype(f32)).astype(bf16)
    return (attended, far_attended, ffn_out)


def solution(mesh):
    return jax.shard_map(
        local,
        mesh=mesh,
        in_specs=(
            P("seq", None),
            P(),
            P(),
            P(None, "mp"),
            P(None, "mp"),
            P(None, "mp"),
            P("mp", None),
            P(),
            P(None, "mp"),
            P("mp", None),
        ),
        out_specs=(P(("seq", "mp"), None), P("seq", "mp"), P(("seq", "mp"), None)),
        check_vma=False,
    )
```
